512 devices in a mesh: dp: 32 (over z_hi, y, core), ctx: 16 (over x, z_lo).
Axes of the slice: x: 4, y: 8, z: 8 (z_hi: 2, z_lo: 4; z = z_hi * 4 + z_lo), core: 2. Of those that a mesh axis runs over, the one named last changes fastest.
Arguments:
- input_proj: bfloat16 [64, 1024, 1024], P('dp', 'ctx'), may hold values from -6 to 6
- value_proj: bfloat16 [64, 1024, 1024], P('dp', 'ctx'), may hold values from -6 to 6
- output_proj: bfloat16 [64, 1024, 1024], P('dp', 'ctx'), may hold values from -6 to 6
- grad_out: bfloat16 [64, 1024, 1024], P('dp', 'ctx'), may hold values from -6 to 6
- filter_spectrum: float32 [32, 2, 1024, 1024], P('dp', None, 'ctx'), may hold values from -4 to 4
Outputs:
- grad_input: bfloat16 [64, 1024, 1024], P('dp', 'ctx')
- grad_value: bfloat16 [64, 1024, 1024], P('dp', 'ctx')
- grad_output_proj: bfloat16 [64, 1024, 1024], P('dp', 'ctx')
- grad_filter: float32 [32, 2, 1024, 1024], P('dp', None, 'ctx')
The draws below stay inside these ranges and needn't reach their ends.
All inputs are finite; a program needn't handle non-finite values.
Results may differ from the reference program's by a relative error of at most 0.014.
Values may be sent and summed in bfloat16 or wider, within the bound.
No kernel may reach another device: no remote copies, remote signals or barrier semaphores. Data moves between devices by JAX's collectives and lax.ppermute only.
A program may use at most 64 MiB of HBM per device.

```python
import math
import jax
import jax.numpy as jnp
from jax import lax

N1 = 1024
N2 = 1024
CH = 32
SEQS = 2
CH_DEV = 2


def levels(own_key, dims, split, low, largest):
    gain, own = 1.0, jax.random.fold_in(own_key, 6)
    for dim, shards_of in split:
        heights = jnp.exp(jax.random.uniform(jax.random.fold_in(own, dim), (shards_of,), jnp.float32, low / len(split), largest / len(split)))
        gain = gain * jnp.repeat(heights, dims[dim] // shards_of).reshape([-1 if axis == dim else 1 for axis in range(len(dims))])
    return gain


def bell_draw(rng, shape, scale, limit, shards=(), kind=jnp.bfloat16):
    values = jax.random.normal(rng, shape, jnp.float32) * scale
    if len(shards) > 0:
        values = levels(rng, shape, shards, -0.22, 0.18) * values
    return jnp.clip(values, min=-limit, max=limit).astype(kind)


def setup_inputs(seed: int = 0) -> dict:
    arg_keys = jax.random.split(jax.random.key(seed), 6)
    input_proj = bell_draw(arg_keys[0], (SEQS * CH, N2, N1), 1.0, 6.0, ((0, 32), (1, 16)))
    value_proj = bell_draw(arg_keys[1], (SEQS * CH, N2, N1), 1.0, 6.0, ((0, 32), (1, 16)))
    output_proj = bell_draw(arg_keys[2], (SEQS * CH, N2, N1), 1.0, 6.0, ((0, 32), (1, 16)))
    grad_out = bell_draw(arg_keys[3], (SEQS * CH, N2, N1), 1.0, 6.0, ((0, 32), (1, 16)))
    filter_spectrum = bell_draw(arg_keys[4], (CH, 2, N1, N2), 0.7, 4.0, ((0, 32), (2, 16)), jnp.float32)
    return {"input_proj": input_proj, "value_proj": value_proj, "output_proj": output_proj, "grad_out": grad_out, "filter_spectrum": filter_spectrum}


def dft_tables(count):
    index = jnp.arange(count, dtype=jnp.int32)
    folded = (index[:, None] * index[None, :]) % count
    phase = folded.astype(jnp.float32) * (2.0 * math.pi / count)
    return jnp.cos(phase).astype(jnp.bfloat16), jnp.sin(phase).astype(jnp.bfloat16)


def turn_tables(first_index, second_index, total):
    folded = (first_index[:, None] * second_index[None, :]) % total
    phase = folded.astype(jnp.float32) * (2.0 * math.pi / total)
    return jnp.cos(phase), jnp.sin(phase)


def flat_dot(left, table):
    shape = left.shape
    result = jnp.dot(left.reshape(-1, shape[-1]), table, preferred_element_type=jnp.float32)
    return result.reshape(shape[:-1] + (table.shape[1],))


def forward_mix(left, table):
    return jnp.einsum("pbk,bd->pkd", left.astype(jnp.float32), table.astype(jnp.float32))


def inverse_mix(left, table):
    return jnp.einsum("pkb,ka->pba", left.astype(jnp.float32), table.astype(jnp.float32))


def reference(input_proj, value_proj, output_proj, grad_out, filter_spectrum):
    length = N1 * N2
    scale = 1.0 / length
    groups = CH // CH_DEV
    cos_one, sin_one = dft_tables(N1)
    cos_two, sin_two = dft_tables(N2)
    tw_cos, tw_sin = turn_tables(jnp.arange(N2, dtype=jnp.int32), jnp.arange(N1, dtype=jnp.int32), length)
    un_cos = tw_cos.T
    un_sin = tw_sin.T

    def natural(array):
        return array.reshape(groups, SEQS, CH_DEV, N2, N1).transpose(1, 0, 2, 3, 4).reshape(SEQS, CH, N2, N1)

    def stored(array):
        return array.reshape(SEQS, groups, CH_DEV, N2, N1).transpose(1, 0, 2, 3, 4).reshape(SEQS * CH, N2, N1)

    def one_channel(items):
        inp, val, outp, grad, h_re, h_im = items
        gated = (inp.astype(jnp.float32) * val.astype(jnp.float32)).astype(jnp.bfloat16)
        grad_conv = (grad.astype(jnp.float32) * outp.astype(jnp.float32)).astype(jnp.bfloat16)
        signals = jnp.stack([gated, grad_conv])
        section_re = flat_dot(signals, cos_one)
        section_im = -flat_dot(signals, sin_one)
        turned_re = (section_re * tw_cos + section_im * tw_sin).astype(jnp.bfloat16)
        turned_im = (section_im * tw_cos - section_re * tw_sin).astype(jnp.bfloat16)
        spec_re = (forward_mix(turned_re, cos_two) + forward_mix(turned_im, sin_two)).astype(jnp.bfloat16)
        spec_im = (forward_mix(turned_im, cos_two) - forward_mix(turned_re, sin_two)).astype(jnp.bfloat16)
        u_re = spec_re[0].astype(jnp.float32)
        u_im = spec_im[0].astype(jnp.float32)
        d_re = spec_re[1].astype(jnp.float32)
        d_im = spec_im[1].astype(jnp.float32)
        p_re = (u_re * h_re - u_im * h_im).astype(jnp.bfloat16)
        p_im = (u_re * h_im + u_im * h_re).astype(jnp.bfloat16)
        q_re = (h_re * d_re + h_im * d_im).astype(jnp.bfloat16)
        q_im = (h_re * d_im - h_im * d_re).astype(jnp.bfloat16)
        grad_re = (u_re * d_re + u_im * d_im) * scale
        grad_im = (u_re * d_im - u_im * d_re) * scale
        inv_re = jnp.stack([p_re, q_re])
        inv_im = jnp.stack([p_im, q_im])
        back_re = flat_dot(inv_re, cos_two) - flat_dot(inv_im, sin_two)
        back_im = flat_dot(inv_re, sin_two) + flat_dot(inv_im, cos_two)
        unturned_re = (back_re * un_cos - back_im * un_sin).astype(jnp.bfloat16)
        unturned_im = (back_re * un_sin + back_im * un_cos).astype(jnp.bfloat16)
        result = (inverse_mix(unturned_re, cos_one) - inverse_mix(unturned_im, sin_one)) * scale
        conv_out = result[0]
        grad_gated = result[1]
        grad_oproj = (grad.astype(jnp.float32) * conv_out).astype(jnp.bfloat16)
        grad_inp = (grad_gated * val.astype(jnp.float32)).astype(jnp.bfloat16)
        grad_val = (grad_gated * inp.astype(jnp.float32)).astype(jnp.bfloat16)
        return grad_inp, grad_val, grad_oproj, grad_re, grad_im

    def one_sequence(carry, sequence):
        inp, val, outp, grad = sequence
        outs = lax.map(one_channel, (inp, val, outp, grad, filter_spectrum[:, 0], filter_spectrum[:, 1]))
        return (carry[0] + outs[3], carry[1] + outs[4]), (outs[0], outs[1], outs[2])

    start = (jnp.zeros((CH, N1, N2), jnp.float32), jnp.zeros((CH, N1, N2), jnp.float32))
    inputs = (natural(input_proj), natural(value_proj), natural(output_proj), natural(grad_out))
    totals, outputs = lax.scan(one_sequence, start, inputs)
    return stored(outputs[0]), stored(outputs[1]), stored(outputs[2]), jnp.stack([totals[0], totals[1]], axis=1)
```

```python
import functools

import jax
import jax.numpy as jnp
import ml_dtypes
import numpy as np
from jax import lax
from jax.experimental import pallas as pl
from jax.experimental.pallas import tpu as pltpu
from jax.sharding import Mesh
from jax.sharding import PartitionSpec as P

N = 1024
TOTAL = N * N
RANKS = 16
ROWS = 64
SLOTS = 32
SCALE = 1.0 / TOTAL
BF = jnp.bfloat16
F32 = jnp.float32
NT = (((1,), (1,)), ((), ()))
BLOCKS = 4
WIDE = N // BLOCKS


def kept_rows():
    rank = np.arange(RANKS)
    return (ROWS * rank + (rank >= RANKS // 2))[:, None] + np.arange(SLOTS)[None, :]


def dft_tables():
    index = np.arange(N, dtype=np.int64)
    phase = (index[:, None] * index[None, :] % N).astype(np.float64) * (2.0 * np.pi / N)
    return np.cos(phase), np.sin(phase)


def section_table():
    cos, sin = dft_tables()
    rows = kept_rows()
    imag = -sin[rows]
    imag[0, 0] = 1.0 - 2.0 * (np.arange(N) % 2)
    both = np.stack([cos[rows], imag])
    both = both.reshape(2, RANKS // 2, 2, SLOTS, N).transpose(1, 0, 2, 3, 4)
    return both.reshape(N, N).astype(ml_dtypes.bfloat16)


def forward_turn():
    rows = kept_rows().reshape(1, -1, 1)
    place = np.arange(N).reshape(RANKS, 1, ROWS)
    phase = (rows * place % TOTAL).astype(np.float64) * (2.0 * np.pi / TOTAL)
    return np.concatenate([np.cos(phase), np.sin(phase)], axis=2).astype(np.float32)


def inverse_turn():
    rows = kept_rows().reshape(RANKS, 1, SLOTS)
    place = np.arange(N).reshape(1, N, 1)
    phase = (rows * place % TOTAL).astype(np.float64) * (2.0 * np.pi / TOTAL)
    cos, sin = np.cos(phase), np.sin(phase)
    return np.concatenate([cos, cos, sin, sin], axis=2).astype(np.float32)


def half_turn():
    phase = np.arange(N) * (np.pi / N)
    return np.cos(phase), np.sin(phase)


def lanes_of(shape):
    return lax.broadcasted_iota(jnp.int32, shape, len(shape) - 1)


def rows_of(shape):
    return lax.broadcasted_iota(jnp.int32, shape, len(shape) - 2)


def swap_halves(value):
    half = value.shape[-1] // 2
    return jnp.concatenate([value[..., half:], value[..., :half]], axis=-1)


def split_turn(packed):
    swapped = swap_halves(packed)
    low = lanes_of(packed.shape) < packed.shape[-1] // 2
    return jnp.where(low, packed, swapped), jnp.where(low, swapped, packed)


def section_kernel(rank, inp, val, outp, grad, table, turn, out, signals):
    @pl.when(pl.program_id(0) == 0)
    def _():
        for chan in range(2):
            gated = inp[chan].astype(F32) * val[chan].astype(F32)
            conv = grad[chan].astype(F32) * outp[chan].astype(F32)
            signals[128 * chan : 128 * chan + 64, :] = gated.astype(BF)
            signals[128 * chan + 64 : 128 * chan + 128, :] = conv.astype(BF)

    section = lax.dot_general(table[...], signals[...], NT, preferred_element_type=F32)
    for pair in range(2):
        cos, sin = split_turn(turn[0, 64 * pair : 64 * pair + 64, :])
        for chan in range(2):
            lanes = slice(128 * chan, 128 * chan + 128)
            real = section[128 * pair : 128 * pair + 64, lanes]
            imag = section[128 * pair + 64 : 128 * pair + 128, lanes]
            turned_re = (real * cos + imag * sin).astype(BF)
            turned_im = (imag * cos - real * sin).astype(BF)
            for odd in range(2):
                rows = slice(32 * odd, 32 * odd + 32)
                out[chan, 2 * pair + odd, 0:32, :] = turned_re[rows]
                out[chan, 2 * pair + odd, 32:64, :] = turned_im[rows]


def reverse_lanes(value):
    shape = (128, 128)
    flip = jnp.where(rows_of(shape) + lanes_of(shape) == 127, 1.0, 0.0).astype(BF)
    value = value.astype(BF)
    parts = [
        jnp.dot(value[:, 128 * part : 128 * part + 128], flip, preferred_element_type=F32)
        for part in reversed(range(N // 128))
    ]
    return jnp.concatenate(parts, axis=1)


def filter_kernel(rank, own, other, special, out):
    me = rank[0]
    low = me < RANKS // 2
    shape = (SLOTS, SLOTS)
    wanted = jnp.where(low, 32, 31)
    pick = jnp.where(rows_of(shape) + lanes_of(shape) == wanted, 1.0, 0.0).astype(BF)
    top = rows_of((SLOTS, N)) == 0
    for part in range(2):
        sign = 1.0 if part == 0 else -1.0
        mine = jnp.where(low, own[0, part, 0:32, :], own[0, part, 1:33, :])
        moved = jnp.dot(pick, other[part], preferred_element_type=F32)
        mirror = reverse_lanes(moved)
        first = own[0, part, 0:8, :]
        extra = jnp.broadcast_to(special[part : part + 1, :].astype(F32), (8, N))
        flipped = reverse_lanes(jnp.concatenate([first, extra], axis=0))
        around = pltpu.roll(flipped[0:8], 1, 1)
        head = jnp.where(me == 0, around, flipped[8:16])[0:1]
        mirror = jnp.where(jnp.logical_and(top, low), head, mirror)
        out[part, 0:32, :] = 0.5 * (mine + sign * mirror)
        out[part, 32:40, :] = 0.5 * (extra + sign * flipped[8:16])


def spectrum_kernel(rank, turned, cos, sin, half, spec, grad, grad_low, grad_row, left):
    me = rank[0]

    @pl.when(pl.program_id(0) == 0)
    def _():
        for seq in range(2):
            for pair in range(RANKS // 2):
                even = turned[RANKS * seq + 2 * pair]
                odd = turned[RANKS * seq + 2 * pair + 1]
                here = slice(128 * pair, 128 * pair + 128)
                there = slice(N + 128 * pair, N + 128 * pair + 128)
                for sig in range(2):
                    lanes = slice(64 * sig, 64 * sig + 64)
                    both = jnp.concatenate([even[:, lanes], odd[:, lanes]], axis=1)
                    base = 32 * (2 * seq + sig)
                    left[base : base + 32, here] = both[0:32]
                    left[base : base + 32, there] = both[32:64]
                    left[128 + base : 160 + base, here] = both[32:64]
                    left[128 + base : 160 + base, there] = -both[0:32]
        heads = []
        packed = jnp.logical_and(rows_of((16, N)) == 0, me == 0)
        for which in range(4):
            base = 32 * which
            block = left[base : base + 16, N:].astype(F32)
            heads.append(block[0:1])
            kept = jnp.where(packed, 0.0, block).astype(BF)
            left[base : base + 16, N:] = kept
            left[128 + base : 144 + base, :N] = kept
        head = jnp.concatenate(heads + heads, axis=0)
        real = head * half[0:1, :]
        imag = -head * half[1:2, :]
        left[256:272, :N] = jnp.concatenate([real, imag], axis=0).astype(BF)
        left[256:272, N:] = jnp.concatenate([imag, -real], axis=0).astype(BF)

    result = jnp.dot(left[:, :N], cos[...], preferred_element_type=F32)
    result = result + jnp.dot(left[:, N:], sin[...], preferred_element_type=F32)
    spec[...] = result.astype(BF)
    real = 0.0
    imag = 0.0
    row_re = 0.0
    row_im = 0.0
    for seq in range(2):
        base = 64 * seq
        u_re, u_im = result[base : base + 32], result[base + 128 : base + 160]
        d_re, d_im = result[base + 32 : base + 64], result[base + 160 : base + 192]
        real = real + (u_re * d_re + u_im * d_im)
        imag = imag + (u_re * d_im - u_im * d_re)
        base = 256 + 2 * seq
        u_re, u_im = result[base : base + 1], result[base + 8 : base + 9]
        d_re, d_im = result[base + 1 : base + 2], result[base + 9 : base + 10]
        row_re = row_re + (u_re * d_re + u_im * d_im)
        row_im = row_im + (u_re * d_im - u_im * d_re)
    real = real * SCALE
    imag = imag * SCALE
    grad[0] = real
    grad[1] = imag
    grad_low[0] = real.astype(BF)
    grad_low[1] = imag.astype(BF)
    row_re = jnp.where(me == 0, row_re * SCALE, real[0:1])
    row_im = jnp.where(me == 0, row_im * SCALE, imag[0:1])
    grad_row[...] = jnp.concatenate([row_re, row_im], axis=0).astype(BF)


def inverse_kernel(rank, spec, filt, cos, sin, turn, half, out, total, extra):
    me = rank[0]
    step = pl.program_id(0)

    def products(u_re, u_im, d_re, d_im, h_re, h_im):
        return (
            u_re * h_re - u_im * h_im,
            u_re * h_im + u_im * h_re,
            h_re * d_re + h_im * d_im,
            h_re * d_im - h_im * d_re,
        )

    def back(real, imag):
        straight = jnp.concatenate([real, imag], axis=0).astype(BF)
        crossed = jnp.concatenate([-imag, real], axis=0).astype(BF)
        return lax.dot_general(
            cos[...], straight, NT, preferred_element_type=F32
        ) + lax.dot_general(sin[...], crossed, NT, preferred_element_type=F32)

    values = spec[...].astype(F32)
    h_re, h_im = filt[0, 0:32, :], filt[1, 0:32, :]
    reals, imags = [], []
    for seq in range(2):
        base = 64 * seq
        p_re, p_im, q_re, q_im = products(
            values[base : base + 32],
            values[base + 128 : base + 160],
            values[base + 32 : base + 64],
            values[base + 160 : base + 192],
            h_re,
            h_im,
        )
        reals += [p_re, q_re]
        imags += [p_im, q_im]
    part = back(jnp.concatenate(reals, axis=0), jnp.concatenate(imags, axis=0))

    @pl.when(step == 0)
    def _():
        total[...] = part

    @pl.when(step != 0)
    def _():
        total[...] += part

    @pl.when(me == 0)
    def _():
        h_re, h_im = filt[0, 32:33, :], filt[1, 32:33, :]
        top = rows_of((SLOTS, WIDE)) == 0
        reals, imags = [], []
        for seq in range(2):
            base = 256 + 2 * seq
            p_re, p_im, q_re, q_im = products(
                values[base : base + 1],
                values[base + 8 : base + 9],
                values[base + 1 : base + 2],
                values[base + 9 : base + 10],
                h_re,
                h_im,
            )
            reals += [jnp.where(top, p_re, 0.0), jnp.where(top, q_re, 0.0)]
            imags += [jnp.where(top, p_im, 0.0), jnp.where(top, q_im, 0.0)]
        more = back(jnp.concatenate(reals, axis=0), jnp.concatenate(imags, axis=0))
        more = more[:, :128] * half[:, 0:1] - more[:, 128:] * half[:, 1:2]

        @pl.when(step == 0)
        def _():
            extra[...] = more

        @pl.when(step != 0)
        def _():
            extra[...] += more

    @pl.when(step == BLOCKS - 1)
    def _():
        turn_cos, turn_sin = split_turn(turn[0])
        real = total[:, :128]
        imag = total[:, 128:]
        un_re = real * turn_cos - imag * turn_sin
        un_im = real * turn_sin + imag * turn_cos
        packed = jnp.logical_and(lanes_of((N, 128)) % SLOTS == 0, me == 0)
        un_re = jnp.where(packed, un_re, 2.0 * un_re).astype(BF)
        un_im = jnp.where(packed, extra[...], 2.0 * un_im).astype(BF)
        out[0] = jnp.concatenate([un_re[:, :64], un_im[:, :64]], axis=1)
        out[1] = jnp.concatenate([un_re[:, 64:], un_im[:, 64:]], axis=1)


def result_kernel(arrived, table, inp, val, grad, d_inp, d_val, d_outp, left):
    @pl.when(pl.program_id(0) == 0)
    def _():
        for chan in range(2):
            for pair in range(RANKS // 2):
                even = arrived[RANKS * chan + 2 * pair]
                odd = arrived[RANKS * chan + 2 * pair + 1]
                for sig in range(2):
                    low = slice(32 * sig, 32 * sig + 32)
                    high = slice(64 + 32 * sig, 96 + 32 * sig)
                    base = 64 * (2 * chan + sig)
                    left[base : base + 64, 128 * pair : 128 * pair + 128] = jnp.concatenate(
                        [even[:, low], odd[:, low], even[:, high], odd[:, high]], axis=1
                    )

    result = jnp.dot(left[...], table[...], preferred_element_type=F32) * SCALE
    for chan in range(2):
        conv = result[128 * chan : 128 * chan + 64]
        gated = result[128 * chan + 64 : 128 * chan + 128]
        d_outp[chan] = (grad[chan].astype(F32) * conv).astype(BF)
        d_inp[chan] = (gated * val[chan].astype(F32)).astype(BF)
        d_val[chan] = (gated * inp[chan].astype(F32)).astype(BF)


def assemble_kernel(rank, own, other, special, out):
    me = rank[0]
    low = me < RANKS // 2
    shape = (SLOTS, SLOTS)
    wanted = jnp.where(low, 31, 32)
    pick = jnp.where(rows_of(shape) + lanes_of(shape) == wanted, 1.0, 0.0).astype(BF)
    top = rows_of((SLOTS, N)) == 0
    for part in range(2):
        sign = 1.0 if part == 0 else -1.0
        mine = own[part]
        shifted = pltpu.roll(mine, 1, 0)
        moved = jnp.dot(pick, other[part], preferred_element_type=F32)
        mirror = sign * reverse_lanes(moved)
        row = jnp.broadcast_to(special[part : part + 1, :].astype(F32), (16, N))
        turned = sign * reverse_lanes(row)
        head = jnp.where(me == RANKS // 2, row, turned)[0:1]
        out[0, part, 0:32, :] = jnp.where(low, mine, jnp.where(top, head, shifted))
        out[0, part, 32:64, :] = jnp.where(jnp.logical_and(top, ~low), shifted, mirror)


def whole(shape):
    return pl.BlockSpec(shape, lambda *_: (0,) * len(shape))


def sizes(flops, count):
    return pl.CostEstimate(flops=flops, bytes_accessed=count, transcendentals=0)


def params(mib):
    return pltpu.CompilerParams(vmem_limit_bytes=mib * 2**20)


def local(input_proj, value_proj, output_proj, grad_out, filter_spectrum):
    cos64, sin64 = dft_tables()
    cos_table = jnp.asarray(cos64.astype(ml_dtypes.bfloat16))
    sin_table = jnp.asarray(sin64.astype(ml_dtypes.bfloat16))
    sections = jnp.asarray(section_table())
    turn_out = jnp.asarray(forward_turn())
    turn_back = jnp.asarray(inverse_turn())
    half_rows = jnp.asarray(np.stack(half_turn()).astype(np.float32))
    half_columns = jnp.asarray(np.stack(half_turn(), axis=1).astype(np.float32))
    ctx_rank = lax.axis_index("ctx")
    rank = ctx_rank.astype(jnp.int32).reshape(1)
    half_ranks = RANKS // 2
    mirror_of = [(r, RANKS - 1 - r) for r in range(RANKS)]
    special_of = [(r, RANKS - r) for r in range(1, RANKS) if r != half_ranks]
    special_of += [(0, half_ranks), (half_ranks, 0)]

    other_rows = lax.ppermute(filter_spectrum[0, :, 32:64, :].astype(BF), "ctx", mirror_of)
    other_row = lax.ppermute(filter_spectrum[0, :, 0, :].astype(BF), "ctx", special_of)

    turned = pl.pallas_call(
        section_kernel,
        out_shape=jax.ShapeDtypeStruct((2, RANKS, ROWS, 128), BF),
        grid_spec=pltpu.PrefetchScalarGridSpec(
            num_scalar_prefetch=1,
            grid=(BLOCKS,),
            in_specs=[whole((2, ROWS, N))] * 4
            + [
                pl.BlockSpec((WIDE, N), lambda i, r: (i, 0)),
                pl.BlockSpec((1, WIDE // 2, 128), lambda i, r: (r[0], i, 0)),
            ],
            out_specs=pl.BlockSpec((2, RANKS // BLOCKS, ROWS, 128), lambda i, r: (0, i, 0, 0)),
            scratch_shapes=[pltpu.VMEM((256, N), BF)],
        ),
        compiler_params=params(24),
        cost_estimate=sizes(2 * 256 * N * N, 4 * 2**20),
        name="sections",
    )(rank, input_proj, value_proj, output_proj, grad_out, sections, turn_out)
    arrived = lax.all_to_all(
        turned.reshape(2 * RANKS, ROWS, 128), ("core", "ctx"), 0, 0, tiled=True
    )

    folded_filter = pl.pallas_call(
        filter_kernel,
        out_shape=jax.ShapeDtypeStruct((2, 40, N), F32),
        grid_spec=pltpu.PrefetchScalarGridSpec(
            num_scalar_prefetch=1,
            grid=(1,),
            in_specs=[whole((1, 2, ROWS, N)), whole((2, SLOTS, N)), whole((2, N))],
            out_specs=whole((2, 40, N)),
        ),
        compiler_params=params(16),
        cost_estimate=sizes(2**24, 2**20),
        name="fold_filter",
    )(rank, filter_spectrum, other_rows, other_row)

    spectra, grad_own, grad_low, grad_row = pl.pallas_call(
        spectrum_kernel,
        out_shape=[
            jax.ShapeDtypeStruct((272, N), BF),
            jax.ShapeDtypeStruct((2, SLOTS, N), F32),
            jax.ShapeDtypeStruct((2, SLOTS, N), BF),
            jax.ShapeDtypeStruct((2, N), BF),
        ],
        grid_spec=pltpu.PrefetchScalarGridSpec(
            num_scalar_prefetch=1,
            grid=(BLOCKS,),
            in_specs=[
                whole((2 * RANKS, ROWS, 128)),
                pl.BlockSpec((N, WIDE), lambda i, r: (0, i)),
                pl.BlockSpec((N, WIDE), lambda i, r: (0, i)),
                whole((2, N)),
            ],
            out_specs=[
                pl.BlockSpec((272, WIDE), lambda i, r: (0, i)),
                pl.BlockSpec((2, SLOTS, WIDE), lambda i, r: (0, 0, i)),
                pl.BlockSpec((2, SLOTS, WIDE), lambda i, r: (0, 0, i)),
                pl.BlockSpec((2, WIDE), lambda i, r: (0, i)),
            ],
            scratch_shapes=[pltpu.VMEM((272, 2 * N), BF)],
        ),
        compiler_params=params(24),
        cost_estimate=sizes(4 * 256 * N * N, 6 * 2**20),
        name="spectra",
    )(rank, arrived, cos_table, sin_table, half_rows)

    mirror_grad = lax.ppermute(grad_low, "ctx", mirror_of)
    mirror_row = lax.ppermute(grad_row, "ctx", special_of)

    unturned = pl.pallas_call(
        inverse_kernel,
        out_shape=jax.ShapeDtypeStruct((2, N, 128), BF),
        grid_spec=pltpu.PrefetchScalarGridSpec(
            num_scalar_prefetch=1,
            grid=(BLOCKS,),
            in_specs=[
                pl.BlockSpec((272, WIDE), lambda i, r: (0, i)),
                pl.BlockSpec((2, 40, WIDE), lambda i, r: (0, 0, i)),
                pl.BlockSpec((N, WIDE), lambda i, r: (0, i)),
                pl.BlockSpec((N, WIDE), lambda i, r: (0, i)),
                pl.BlockSpec((1, N, 128), lambda i, r: (r[0], 0, 0)),
                whole((N, 2)),
            ],
            out_specs=whole((2, N, 128)),
            scratch_shapes=[pltpu.VMEM((N, 256), F32), pltpu.VMEM((N, 128), F32)],
        ),
        compiler_params=params(32),
        cost_estimate=sizes(4 * 256 * N * N, 6 * 2**20),
        name="inverse",
    )(rank, spectra, folded_filter, cos_table, sin_table, turn_back, half_columns)
    returned = lax.all_to_all(
        unturned.reshape(2 * RANKS, ROWS, 128), ("core", "ctx"), 0, 0, tiled=True
    )

    grad_filter = pl.pallas_call(
        assemble_kernel,
        out_shape=jax.ShapeDtypeStruct((1, 2, ROWS, N), F32),
        grid_spec=pltpu.PrefetchScalarGridSpec(
            num_scalar_prefetch=1,
            grid=(1,),
            in_specs=[whole((2, SLOTS, N)), whole((2, SLOTS, N)), whole((2, N))],
            out_specs=whole((1, 2, ROWS, N)),
        ),
        compiler_params=params(16),
        cost_estimate=sizes(2**24, 2**20),
        name="assemble",
    )(rank, grad_own, mirror_grad, mirror_row)

    column = pl.BlockSpec((2, ROWS, WIDE), lambda i: (0, 0, i))
    grad_input, grad_value, grad_output_proj = pl.pallas_call(
        result_kernel,
        out_shape=[jax.ShapeDtypeStruct((2, ROWS, N), BF)] * 3,
        grid=(BLOCKS,),
        in_specs=[
            whole((2 * RANKS, ROWS, 128)),
            pl.BlockSpec((N, WIDE), lambda i: (0, i)),
            column,
            column,
            column,
        ],
        out_specs=[column] * 3,
        scratch_shapes=[pltpu.VMEM((256, N), BF)],
        compiler_params=params(24),
        cost_estimate=sizes(2 * 256 * N * N, 4 * 2**20),
        name="results",
    )(returned, sections, input_proj, value_proj, grad_out)
    return (grad_input, grad_value, grad_output_proj, grad_filter)


def solution(mesh):
    split = Mesh(mesh.devices.reshape(-1, 2, RANKS), ("group", "core", "ctx"))
    data = P(("group", "core"), "ctx", None)
    filt = P(("group", "core"), None, "ctx", None)
    return jax.shard_map(
        local,
        mesh=split,
        in_specs=(data, data, data, data, filt),
        out_specs=(data, data, data, filt),
        check_vma=False,
    )
```

```python
import functools

import jax
import jax.numpy as jnp
import ml_dtypes
import numpy as np
from jax import lax
from jax.experimental import pallas as pl
from jax.experimental.pallas import tpu as pltpu
from jax.sharding import Mesh
from jax.sharding import PartitionSpec as P

N = 1024
TOTAL = N * N
RANKS = 16
ROWS = 64
SLOTS = 32
SCALE = 1.0 / TOTAL
BF = jnp.bfloat16
F32 = jnp.float32
NT = (((1,), (1,)), ((), ()))
BLOCKS = 4
WIDE = N // BLOCKS
A_COST = 10**10
B_COST = 10**10
W_COST = 4 * 10**10


def kept_rows():
    rank = np.arange(RANKS)
    return (ROWS * rank + (rank >= RANKS // 2))[:, None] + np.arange(SLOTS)[None, :]


def dft_tables():
    index = np.arange(N, dtype=np.int64)
    phase = (index[:, None] * index[None, :] % N).astype(np.float64) * (2.0 * np.pi / N)
    return np.cos(phase), np.sin(phase)


def section_table():
    cos, sin = dft_tables()
    rows = kept_rows()
    imag = -sin[rows]
    imag[0, 0] = 1.0 - 2.0 * (np.arange(N) % 2)
    both = np.stack([cos[rows], imag])
    both = both.reshape(2, RANKS // 2, 2, SLOTS, N).transpose(1, 0, 2, 3, 4)
    return both.reshape(N, N).astype(ml_dtypes.bfloat16)


def forward_turn():
    rows = kept_rows().reshape(1, -1, 1)
    place = np.arange(N).reshape(RANKS, 1, ROWS)
    phase = (rows * place % TOTAL).astype(np.float64) * (2.0 * np.pi / TOTAL)
    return np.concatenate([np.cos(phase), np.sin(phase)], axis=2).astype(np.float32)


def inverse_turn():
    rows = kept_rows().reshape(RANKS, 1, SLOTS)
    place = np.arange(N).reshape(1, N, 1)
    phase = (rows * place % TOTAL).astype(np.float64) * (2.0 * np.pi / TOTAL)
    cos, sin = np.cos(phase), np.sin(phase)
    return np.concatenate([cos, cos, sin, sin], axis=2).astype(np.float32)


def half_turn():
    phase = np.arange(N) * (np.pi / N)
    return np.cos(phase), np.sin(phase)


def lanes_of(shape):
    return lax.broadcasted_iota(jnp.int32, shape, len(shape) - 1)


def rows_of(shape):
    return lax.broadcasted_iota(jnp.int32, shape, len(shape) - 2)


def swap_halves(value):
    half = value.shape[-1] // 2
    return jnp.concatenate([value[..., half:], value[..., :half]], axis=-1)


def split_turn(packed):
    swapped = swap_halves(packed)
    low = lanes_of(packed.shape) < packed.shape[-1] // 2
    return jnp.where(low, packed, swapped), jnp.where(low, swapped, packed)


def start_all(copies):
    for copy in copies:
        copy.start()


def section_kernel(
    rank, inp, val, outp, grad, table, turn, filt, out, row,
    gates, sections, turns, ready, signals, lines, sems
):
    gate_copies = [
        pltpu.make_async_copy(source, gates.at[which], sems.at[which])
        for which, source in enumerate((inp, val, outp, grad))
    ]
    turn_copy = pltpu.make_async_copy(turn.at[rank[0]], turns, sems.at[4])
    blocks = [pl.ds(WIDE * block, WIDE) for block in range(BLOCKS)]
    table_copies = [
        pltpu.make_async_copy(table.at[rows], sections.at[rows], sems.at[5 + block])
        for block, rows in enumerate(blocks)
    ]
    row_copy = pltpu.make_async_copy(
        filt.at[0, :, pl.ds(0, 8)], lines, sems.at[9 + 2 * BLOCKS]
    )
    start_all(gate_copies + table_copies[:1] + [turn_copy] + table_copies[1:] + [row_copy])
    for copy in gate_copies:
        copy.wait()
    for chan in range(2):
        gated = gates[0, chan].astype(F32) * gates[1, chan].astype(F32)
        conv = gates[3, chan].astype(F32) * gates[2, chan].astype(F32)
        signals[128 * chan : 128 * chan + 64, :] = gated.astype(BF)
        signals[128 * chan + 64 : 128 * chan + 128, :] = conv.astype(BF)
    out_copies = []
    for block, rows in enumerate(blocks):
        table_copies[block].wait()
        section = lax.dot_general(
            sections[rows, :], signals[...], NT, preferred_element_type=F32
        )
        if block == 0:
            turn_copy.wait()
        for pair in range(2):
            base = WIDE // 2 * block + 64 * pair
            cos, sin = split_turn(turns[base : base + 64, :])
            for chan in range(2):
                lanes = slice(128 * chan, 128 * chan + 128)
                real = section[128 * pair : 128 * pair + 64, lanes]
                imag = section[128 * pair + 64 : 128 * pair + 128, lanes]
                turned_re = (real * cos + imag * sin).astype(BF)
                turned_im = (imag * cos - real * sin).astype(BF)
                for odd in range(2):
                    some = slice(32 * odd, 32 * odd + 32)
                    peer = 4 * block + 2 * pair + odd
                    ready[chan, peer, 0:32, :] = turned_re[some]
                    ready[chan, peer, 32:64, :] = turned_im[some]
        peers = pl.ds(4 * block, 4)
        for chan in range(2):
            copy = pltpu.make_async_copy(
                ready.at[chan, peers], out.at[chan, peers], sems.at[9 + 2 * block + chan]
            )
            copy.start()
            out_copies.append(copy)
    row_copy.wait()
    row[...] = jnp.concatenate([lines[0, 0:1], lines[1, 0:1]], axis=0).astype(BF)
    for copy in out_copies:
        copy.wait()


def reverse_lanes(value):
    shape = (128, 128)
    flip = jnp.where(rows_of(shape) + lanes_of(shape) == 127, 1.0, 0.0).astype(BF)
    value = value.astype(BF)
    parts = [
        jnp.dot(value[:, 128 * part : 128 * part + 128], flip, preferred_element_type=F32)
        for part in reversed(range(N // 128))
    ]
    return jnp.concatenate(parts, axis=1)


def near_kernel_one(after, table, table_out, sems):
    copy = pltpu.make_async_copy(table, table_out, sems.at[0])
    copy.start()
    copy.wait()


def near_kernel(after, table, first, second, third, table_out, stack, sems):
    copies = [pltpu.make_async_copy(table, table_out, sems.at[0])] + [
        pltpu.make_async_copy(source, stack.at[which], sems.at[1 + which])
        for which, source in enumerate((first, second, third))
    ]
    start_all(copies)
    for copy in copies:
        copy.wait()


def bring_near(after, table, *others):
    shapes = [pltpu.VMEM(table.shape, table.dtype)]
    if others:
        shapes.append(pltpu.VMEM((len(others),) + others[0].shape, others[0].dtype))
    return pl.pallas_call(
        near_kernel if others else near_kernel_one,
        out_shape=shapes,
        in_specs=[HBM] * (2 + len(others)),
        out_specs=[VMEM] * len(shapes),
        scratch_shapes=[pltpu.SemaphoreType.DMA((1 + len(others),))],
        compiler_params=params(16),
        cost_estimate=sizes(W_COST),
        name="bring_near",
    )(after, kept(table), *[kept(value) for value in others])


def filter_kernel(rank, own, other, special, out, mine, sem):
    me = rank[0]
    copy = pltpu.make_async_copy(own.at[0], mine, sem)
    copy.start()
    low = me < RANKS // 2
    shape = (SLOTS, SLOTS)
    wanted = jnp.where(low, 32, 31)
    pick = jnp.where(rows_of(shape) + lanes_of(shape) == wanted, 1.0, 0.0).astype(BF)
    top = rows_of((SLOTS, N)) == 0
    copy.wait()
    for part in range(2):
        sign = 1.0 if part == 0 else -1.0
        kept = jnp.where(low, mine[part, 0:32, :], mine[part, 1:33, :])
        moved = jnp.dot(pick, other[32 * part : 32 * part + 32], preferred_element_type=F32)
        mirror = reverse_lanes(moved)
        first = mine[part, 0:8, :]
        extra = jnp.broadcast_to(special[part : part + 1, :].astype(F32), (8, N))
        flipped = reverse_lanes(jnp.concatenate([first, extra], axis=0))
        around = pltpu.roll(flipped[0:8], 1, 1)
        head = jnp.where(me == 0, around, flipped[8:16])[0:1]
        mirror = jnp.where(jnp.logical_and(top, low), head, mirror)
        out[part, 0:32, :] = 0.5 * (kept + sign * mirror)
        out[part, 32:40, :] = 0.5 * (extra + sign * flipped[8:16])


def alternating(shape):
    return 1 - 2 * (lanes_of(shape) % 2)


def spectrum_kernel(
    rank, turned, tables, filt_far, turn_far, half,
    spec, grad, grad_low, grad_row, tables_out, filt, turn, left, sems
):
    me = rank[0]
    middle = N // 2
    copies = [
        pltpu.make_async_copy(tables, tables_out, sems.at[0]),
        pltpu.make_async_copy(filt_far, filt, sems.at[1]),
        pltpu.make_async_copy(turn_far.at[me], turn, sems.at[2]),
    ]
    start_all(copies)
    for seq in range(2):
        for pair in range(RANKS // 2):
            even = turned[RANKS * seq + 2 * pair]
            odd = turned[RANKS * seq + 2 * pair + 1]
            here = slice(128 * (pair % 4), 128 * (pair % 4) + 128)
            there = slice(middle + 128 * (pair % 4), middle + 128 * (pair % 4) + 128)
            for sig in range(2):
                lanes = slice(64 * sig, 64 * sig + 64)
                both = jnp.concatenate([even[:, lanes], odd[:, lanes]], axis=1)
                base = 272 * (pair // 4) + 32 * (2 * seq + sig)
                left[base : base + 32, here] = both[0:32]
                left[base : base + 32, there] = both[32:64]
                left[128 + base : 160 + base, here] = both[32:64]
                left[128 + base : 160 + base, there] = -both[0:32]
    packed = jnp.logical_and(rows_of((16, middle)) == 0, me == 0)
    for part in range(2):
        heads = []
        for which in range(4):
            base = 272 * part + 32 * which
            block = left[base : base + 16, middle:].astype(F32)
            heads.append(block[0:1])
            cleared = jnp.where(packed, 0.0, block).astype(BF)
            left[base : base + 16, middle:] = cleared
            left[128 + base : 144 + base, :middle] = cleared
        head = jnp.concatenate(heads + heads, axis=0)
        places = slice(middle * part, middle * part + middle)
        real = head * half[0:1, places]
        imag = -head * half[1:2, places]
        lines = slice(272 * part + 256, 272 * part + 272)
        left[lines, :middle] = jnp.concatenate([real, imag], axis=0).astype(BF)
        left[lines, middle:] = jnp.concatenate([imag, -real], axis=0).astype(BF)

    sign = alternating((1, WIDE)).astype(F32)
    for block in range(BLOCKS):
        wide = slice(WIDE * block, WIDE * block + WIDE)
        halves = jnp.dot(left[...], tables[:, wide], preferred_element_type=F32)
        result = halves[:272] + sign * halves[272:]
        spec[:, wide] = result.astype(BF)
        real = 0.0
        imag = 0.0
        row_re = 0.0
        row_im = 0.0
        for seq in range(2):
            base = 64 * seq
            u_re, u_im = result[base : base + 32], result[base + 128 : base + 160]
            d_re, d_im = result[base + 32 : base + 64], result[base + 160 : base + 192]
            real = real + (u_re * d_re + u_im * d_im)
            imag = imag + (u_re * d_im - u_im * d_re)
            base = 256 + 2 * seq
            u_re, u_im = result[base : base + 1], result[base + 8 : base + 9]
            d_re, d_im = result[base + 1 : base + 2], result[base + 9 : base + 10]
            row_re = row_re + (u_re * d_re + u_im * d_im)
            row_im = row_im + (u_re * d_im - u_im * d_re)
        real = real * SCALE
        imag = imag * SCALE
        grad[0, :, wide] = real
        grad[1, :, wide] = imag
        grad_low[0:32, wide] = real.astype(BF)
        grad_low[32:64, wide] = imag.astype(BF)
        row_re = jnp.where(me == 0, row_re * SCALE, real[0:1])
        row_im = jnp.where(me == 0, row_im * SCALE, imag[0:1])
        grad_row[:, wide] = jnp.concatenate([row_re, row_im], axis=0).astype(BF)
    for copy in copies:
        copy.wait()


def products(u_re, u_im, d_re, d_im, h_re, h_im):
    return (
        u_re * h_re - u_im * h_im,
        u_re * h_im + u_im * h_re,
        h_re * d_re + h_im * d_im,
        h_re * d_im - h_im * d_re,
    )


def inverse_kernel(rank, spec, filt, tables, turn, half, grad, out, grad_far, total, sem):
    me = rank[0]
    copy = pltpu.make_async_copy(grad, grad_far, sem)
    copy.start()
    outer, inner = (0, 3), (1, 2)
    sign = alternating((1, WIDE)).astype(BF)
    packed_row = jnp.logical_and(rows_of((SLOTS, WIDE)) == 0, me == 0)
    for block in range(BLOCKS):
        wide = slice(WIDE * block, WIDE * block + WIDE)
        values = spec[:, wide].astype(F32)
        h_re, h_im = filt[0, 0:32, wide], filt[1, 0:32, wide]
        x_re, x_im = filt[0, 32:33, wide], filt[1, 32:33, wide]
        reals, imags, extra_re, extra_im = [], [], [], []
        for seq in range(2):
            base = 64 * seq
            p_re, p_im, q_re, q_im = products(
                values[base : base + 32],
                values[base + 128 : base + 160],
                values[base + 32 : base + 64],
                values[base + 160 : base + 192],
                h_re,
                h_im,
            )
            reals += [p_re, q_re]
            imags += [p_im, q_im]
            base = 256 + 2 * seq
            p_re, p_im, q_re, q_im = products(
                values[base : base + 1],
                values[base + 8 : base + 9],
                values[base + 1 : base + 2],
                values[base + 9 : base + 10],
                x_re,
                x_im,
            )
            extra_re += [p_re, q_re]
            extra_im += [p_im, q_im]

        def mixed(plain, extra, sign):
            return [jnp.where(packed_row, sign * e, p) for p, e in zip(plain, extra)]

        def joined(first, second):
            return jnp.concatenate(first + second, axis=0).astype(BF)

        less = [-value for value in imags]
        for parts, extra, crossed in (
            (outer, extra_re, mixed(reals, extra_im, -1.0)),
            (inner, extra_im, mixed(reals, extra_re, 1.0)),
        ):
            straight = joined(reals, mixed(imags, extra, 1.0))
            crossing = joined(less, crossed)
            for quarter in parts:
                rows = slice(WIDE * quarter, WIDE * quarter + WIDE)
                start = WIDE * (quarter % 2)
                cos = tables[start : start + WIDE, wide]
                sin = tables[N // 2 + start : N // 2 + start + WIDE, wide]
                if quarter >= 2:
                    cos, sin = cos * sign, sin * sign
                part = lax.dot_general(
                    cos, straight, NT, preferred_element_type=F32
                ) + lax.dot_general(sin, crossing, NT, preferred_element_type=F32)
                if block == 0:
                    total[rows, :] = part
                else:
                    total[rows, :] += part

    for piece in range(BLOCKS):
        rows = slice(WIDE * piece, WIDE * piece + WIDE)
        turn_cos, turn_sin = split_turn(turn[rows, :])
        real = total[rows, :128]
        imag = total[rows, 128:]
        un_re = real * turn_cos - imag * turn_sin
        un_im = real * turn_sin + imag * turn_cos
        packed = jnp.logical_and(lanes_of((WIDE, 128)) % SLOTS == 0, me == 0)
        un_im = jnp.where(packed, imag * half[rows, 0:1], 2.0 * un_im).astype(BF)
        un_re = jnp.where(packed, real, 2.0 * un_re).astype(BF)
        out[0, rows, :] = jnp.concatenate([un_re[:, :64], un_im[:, :64]], axis=1)
        out[1, rows, :] = jnp.concatenate([un_re[:, 64:], un_im[:, 64:]], axis=1)
    copy.wait()


def result_kernel(arrived, table, gates, d_inp, d_val, d_outp, left, ready, sems):
    for chan in range(2):
        for pair in range(RANKS // 2):
            even = arrived[RANKS * chan + 2 * pair]
            odd = arrived[RANKS * chan + 2 * pair + 1]
            for sig in range(2):
                low = slice(32 * sig, 32 * sig + 32)
                high = slice(64 + 32 * sig, 96 + 32 * sig)
                base = 64 * (2 * chan + sig)
                left[base : base + 64, 128 * pair : 128 * pair + 128] = jnp.concatenate(
                    [even[:, low], odd[:, low], even[:, high], odd[:, high]], axis=1
                )
    copies = []
    for block in range(BLOCKS):
        wide = slice(WIDE * block, WIDE * block + WIDE)
        result = jnp.dot(left[...], table[:, wide], preferred_element_type=F32) * SCALE
        for chan in range(2):
            conv = result[128 * chan : 128 * chan + 64]
            gated = result[128 * chan + 64 : 128 * chan + 128]
            ready[2, chan, :, wide] = (gates[2, chan, :, wide].astype(F32) * conv).astype(BF)
            ready[0, chan, :, wide] = (gated * gates[1, chan, :, wide].astype(F32)).astype(BF)
            ready[1, chan, :, wide] = (gated * gates[0, chan, :, wide].astype(F32)).astype(BF)
        for which, target in enumerate((d_inp, d_val, d_outp)):
            copy = pltpu.make_async_copy(
                ready.at[which, :, :, pl.ds(WIDE * block, WIDE)],
                target.at[:, :, pl.ds(WIDE * block, WIDE)],
                sems.at[3 * block + which],
            )
            copy.start()
            copies.append(copy)
    for copy in copies:
        copy.wait()


def assemble_kernel(rank, own, other, special, out):
    me = rank[0]
    low = me < RANKS // 2
    shape = (SLOTS, SLOTS)
    wanted = jnp.where(low, 31, 32)
    pick = jnp.where(rows_of(shape) + lanes_of(shape) == wanted, 1.0, 0.0).astype(BF)
    top = rows_of((SLOTS, N)) == 0
    for part in range(2):
        sign = 1.0 if part == 0 else -1.0
        mine = own[part]
        shifted = pltpu.roll(mine, 1, 0)
        moved = jnp.dot(pick, other[32 * part : 32 * part + 32], preferred_element_type=F32)
        mirror = sign * reverse_lanes(moved)
        row = jnp.broadcast_to(special[part : part + 1, :].astype(F32), (16, N))
        turned = sign * reverse_lanes(row)
        head = jnp.where(me == RANKS // 2, row, turned)[0:1]
        out[0, part, 0:32, :] = jnp.where(low, mine, jnp.where(top, head, shifted))
        out[0, part, 32:64, :] = jnp.where(jnp.logical_and(top, ~low), shifted, mirror)


HBM = pl.BlockSpec(memory_space=pltpu.HBM)
VMEM = pl.BlockSpec(memory_space=pltpu.VMEM)
SMEM = pl.BlockSpec(memory_space=pltpu.SMEM)


def kept(value):
    return pltpu.with_memory_space_constraint(value, pltpu.HBM)


def sizes(flops, count=2**20):
    return pl.CostEstimate(flops=flops, bytes_accessed=count, transcendentals=0)


def params(mib):
    return pltpu.CompilerParams(vmem_limit_bytes=mib * 2**20)


def local(input_proj, value_proj, output_proj, grad_out, filter_spectrum):
    cos64, sin64 = dft_tables()
    half_tables = np.concatenate([cos64[: N // 2], sin64[: N // 2]]).astype(ml_dtypes.bfloat16)
    half_tables = jnp.asarray(half_tables)
    sections = jnp.asarray(section_table())
    turn_out = jnp.asarray(forward_turn())
    turn_back = jnp.asarray(inverse_turn())
    half_rows = jnp.asarray(np.stack(half_turn()).astype(np.float32))
    cosine, sine = half_turn()
    middle = np.abs(np.arange(N) - N // 2 + 0.5) < N // 4
    spread = np.where(middle, -1.0 / np.where(middle, sine, 1.0), 1.0 / np.where(middle, 1.0, cosine))
    half_columns = jnp.asarray(spread[:, None].astype(np.float32))
    ctx_rank = lax.axis_index("ctx")
    rank = ctx_rank.astype(jnp.int32).reshape(1)
    half_ranks = RANKS // 2
    mirror_of = [(r, RANKS - 1 - r) for r in range(RANKS)]
    special_of = [(r, RANKS - r) for r in range(1, RANKS) if r != half_ranks]
    special_of += [(0, half_ranks), (half_ranks, 0)]

    filter_rows = filter_spectrum.reshape(2, ROWS, N)[:, 32:64, :].astype(BF)
    other_rows = lax.ppermute(filter_rows.reshape(2 * SLOTS, N), "ctx", mirror_of)

    turned, filter_row = pl.pallas_call(
        section_kernel,
        out_shape=[pltpu.HBM((2, RANKS, ROWS, 128), BF), pltpu.VMEM((2, N), BF)],
        in_specs=[SMEM] + [HBM] * 7,
        out_specs=[HBM, VMEM],
        scratch_shapes=[
            pltpu.VMEM((4, 2, ROWS, N), BF),
            pltpu.VMEM((N, N), BF),
            pltpu.VMEM((N // 2, 128), F32),
            pltpu.VMEM((2, RANKS, ROWS, 128), BF),
            pltpu.VMEM((256, N), BF),
            pltpu.VMEM((2, 8, N), F32),
            pltpu.SemaphoreType.DMA((10 + 2 * BLOCKS,)),
        ],
        compiler_params=params(24),
        cost_estimate=sizes(A_COST),
        name="sections",
    )(
        rank,
        kept(input_proj),
        kept(value_proj),
        kept(output_proj),
        kept(grad_out),
        kept(sections),
        kept(turn_out),
        kept(filter_spectrum),
    )
    other_row = lax.ppermute(filter_row, "ctx", special_of)
    arrived = lax.all_to_all(
        turned.reshape(2 * RANKS, ROWS, 128), ("core", "ctx"), 0, 0, tiled=True
    )

    (tables,) = bring_near(other_rows, half_tables)
    folded_filter = pl.pallas_call(
        filter_kernel,
        out_shape=pltpu.HBM((2, 40, N), F32),
        in_specs=[SMEM, HBM, VMEM, VMEM],
        out_specs=VMEM,
        scratch_shapes=[pltpu.VMEM((2, ROWS, N), F32), pltpu.SemaphoreType.DMA(())],
        compiler_params=params(16),
        cost_estimate=sizes(2**24),
        name="fold_filter",
    )(rank, kept(filter_spectrum), other_rows, other_row)

    spectra, grad_own, grad_low, grad_row, tables_again, filter_near, turn_near = pl.pallas_call(
        spectrum_kernel,
        out_shape=[
            pltpu.VMEM((272, N), BF),
            pltpu.VMEM((2, SLOTS, N), F32),
            pltpu.VMEM((2 * SLOTS, N), BF),
            pltpu.VMEM((2, N), BF),
            pltpu.VMEM((N, N), BF),
            pltpu.VMEM((2, 40, N), F32),
            pltpu.VMEM((N, 128), F32),
        ],
        in_specs=[SMEM, VMEM, VMEM, HBM, HBM, VMEM],
        out_specs=[VMEM] * 7,
        scratch_shapes=[
            pltpu.VMEM((544, N), BF),
            pltpu.SemaphoreType.DMA((3,)),
        ],
        compiler_params=params(20),
        cost_estimate=sizes(B_COST),
        name="spectra",
    )(
        rank,
        arrived,
        pltpu.with_memory_space_constraint(tables, pltpu.VMEM),
        kept(folded_filter),
        kept(turn_back),
        half_rows,
    )

    mirror_grad = lax.ppermute(grad_low, "ctx", mirror_of)
    mirror_row = lax.ppermute(grad_row, "ctx", special_of)

    unturned, grad_far = pl.pallas_call(
        inverse_kernel,
        out_shape=[
            jax.ShapeDtypeStruct((2, N, 128), BF),
            pltpu.HBM((2, SLOTS, N), F32),
        ],
        in_specs=[SMEM] + [VMEM] * 6,
        out_specs=[VMEM, HBM],
        scratch_shapes=[pltpu.VMEM((N, 256), F32), pltpu.SemaphoreType.DMA(())],
        compiler_params=params(24),
        cost_estimate=sizes(B_COST),
        name="inverse",
    )(rank, spectra, filter_near, tables_again, turn_near, half_columns, grad_own)
    returned = lax.all_to_all(
        unturned.reshape(2 * RANKS, ROWS, 128), ("core", "ctx"), 0, 0, tiled=True
    )

    sections_near, gates_near = bring_near(
        mirror_grad, sections, input_proj, value_proj, grad_out
    )
    grad_filter = pl.pallas_call(
        assemble_kernel,
        out_shape=jax.ShapeDtypeStruct((1, 2, ROWS, N), F32),
        in_specs=[SMEM] + [VMEM] * 3,
        out_specs=VMEM,
        compiler_params=params(16),
        cost_estimate=sizes(2**24),
        name="assemble",
    )(rank, grad_far, mirror_grad, mirror_row)

    grad_input, grad_value, grad_output_proj = pl.pallas_call(
        result_kernel,
        out_shape=[pltpu.HBM((2, ROWS, N), BF)] * 3,
        in_specs=[VMEM] * 3,
        out_specs=[HBM] * 3,
        scratch_shapes=[
            pltpu.VMEM((256, N), BF),
            pltpu.VMEM((3, 2, ROWS, N), BF),
            pltpu.SemaphoreType.DMA((3 * BLOCKS,)),
        ],
        compiler_params=params(20),
        cost_estimate=sizes(2 * 256 * N * N),
        name="results",
    )(returned, sections_near, gates_near)
    return (grad_input, grad_value, grad_output_proj, grad_filter)


def solution(mesh):
    split = Mesh(mesh.devices.reshape(-1, 2, RANKS), ("group", "core", "ctx"))
    data = P(("group", "core"), "ctx", None)
    filt = P(("group", "core"), None, "ctx", None)
    return jax.shard_map(
        local,
        mesh=split,
        in_specs=(data, data, data, data, filt),
        out_specs=(data, data, data, filt),
        check_vma=False,
    )
```

```python
import functools

import jax
import jax.numpy as jnp
import ml_dtypes
import numpy as np
from jax import lax
from jax.experimental import pallas as pl
from jax.experimental.pallas import tpu as pltpu
from jax.sharding import Mesh
from jax.sharding import PartitionSpec as P

N = 1024
TOTAL = N * N
RANKS = 16
ROWS = 64
SLOTS = 32
SCALE = 1.0 / TOTAL
BF = jnp.bfloat16
F32 = jnp.float32
NT = (((1,), (1,)), ((), ()))
BLOCKS = 4
WIDE = N // BLOCKS
A_COST = 10**10
B_COST = 10**10
W_COST = 4 * 10**10


def kept_rows():
    rank = np.arange(RANKS)
    return (ROWS * rank + (rank >= RANKS // 2))[:, None] + np.arange(SLOTS)[None, :]


def dft_tables():
    index = np.arange(N, dtype=np.int64)
    phase = (index[:, None] * index[None, :] % N).astype(np.float64) * (2.0 * np.pi / N)
    return np.cos(phase), np.sin(phase)


def section_table():
    cos, sin = dft_tables()
    rows = kept_rows()
    imag = -sin[rows]
    imag[0, 0] = 1.0 - 2.0 * (np.arange(N) % 2)
    both = np.stack([cos[rows], imag])
    both = both.reshape(2, RANKS // 2, 2, SLOTS, N).transpose(1, 0, 2, 3, 4)
    return both.reshape(N, N).astype(ml_dtypes.bfloat16)


def forward_turn():
    rows = kept_rows().reshape(1, -1, 1)
    place = np.arange(N).reshape(RANKS, 1, ROWS)
    phase = (rows * place % TOTAL).astype(np.float64) * (2.0 * np.pi / TOTAL)
    return np.concatenate([np.cos(phase), np.sin(phase)], axis=2).astype(np.float32)


def inverse_turn():
    rows = kept_rows().reshape(RANKS, 1, SLOTS)
    place = np.arange(N).reshape(1, N, 1)
    phase = (rows * place % TOTAL).astype(np.float64) * (2.0 * np.pi / TOTAL)
    cos, sin = np.cos(phase), np.sin(phase)
    sin[0, :, 0] = packed_turn()
    return np.concatenate([cos, cos, sin, sin], axis=2).astype(np.float32)


def half_turn():
    phase = np.arange(N) * (np.pi / N)
    return np.cos(phase), np.sin(phase)


def packed_turn():
    cos, sin = half_turn()
    middle = np.abs(np.arange(N) - N // 2 + 0.5) < N // 4
    return np.where(middle, -1.0 / np.where(middle, sin, 1.0), 1.0 / np.where(middle, 1.0, cos))


def lanes_of(shape):
    return lax.broadcasted_iota(jnp.int32, shape, len(shape) - 1)


def rows_of(shape):
    return lax.broadcasted_iota(jnp.int32, shape, len(shape) - 2)


def swap_halves(value):
    half = value.shape[-1] // 2
    return jnp.concatenate([value[..., half:], value[..., :half]], axis=-1)


def split_turn(packed):
    swapped = swap_halves(packed)
    low = lanes_of(packed.shape) < packed.shape[-1] // 2
    return jnp.where(low, packed, swapped), jnp.where(low, swapped, packed)


def start_all(copies):
    for copy in copies:
        copy.start()


def section_kernel(
    rank, inp, val, outp, grad, table, turn, filt, out, row,
    gates, sections, turns, ready, signals, lines, sems
):
    gate_copies = [
        pltpu.make_async_copy(source, gates.at[which], sems.at[which])
        for which, source in enumerate((inp, val, outp, grad))
    ]
    turn_copy = pltpu.make_async_copy(turn.at[rank[0]], turns, sems.at[4])
    blocks = [pl.ds(WIDE * block, WIDE) for block in range(BLOCKS)]
    table_copies = [
        pltpu.make_async_copy(table.at[rows], sections.at[rows], sems.at[5 + block])
        for block, rows in enumerate(blocks)
    ]
    row_copy = pltpu.make_async_copy(
        filt.at[0, :, pl.ds(0, 8)], lines, sems.at[9 + 2 * BLOCKS]
    )
    start_all(gate_copies + table_copies[:1] + [turn_copy] + table_copies[1:] + [row_copy])
    middle = N // 2
    for copy in gate_copies:
        copy.wait()
    for chan in range(2):
        gated = gates[0, chan].astype(F32) * gates[1, chan].astype(F32)
        conv = gates[3, chan].astype(F32) * gates[2, chan].astype(F32)
        for part in range(2):
            base = 256 * part + 128 * chan
            lanes = slice(middle * part, middle * part + middle)
            signals[base : base + 64, :] = gated[:, lanes].astype(BF)
            signals[base + 64 : base + 128, :] = conv[:, lanes].astype(BF)
    out_copies = []
    for block, rows in enumerate(blocks):
        table_copies[block].wait()
        halves = lax.dot_general(
            sections[rows, :], signals[...], NT, preferred_element_type=F32
        )
        odd_rows = (rows_of((WIDE, 1)) + (block >= BLOCKS // 2)) % 2
        section = halves[:, :256] + (1 - 2 * odd_rows).astype(F32) * halves[:, 256:]
        if block == 0:
            turn_copy.wait()
        for pair in range(2):
            base = WIDE // 2 * block + 64 * pair
            cos, sin = split_turn(turns[base : base + 64, :])
            for chan in range(2):
                lanes = slice(128 * chan, 128 * chan + 128)
                real = section[128 * pair : 128 * pair + 64, lanes]
                imag = section[128 * pair + 64 : 128 * pair + 128, lanes]
                turned_re = (real * cos + imag * sin).astype(BF)
                turned_im = (imag * cos - real * sin).astype(BF)
                for odd in range(2):
                    some = slice(32 * odd, 32 * odd + 32)
                    peer = 4 * block + 2 * pair + odd
                    ready[chan, peer, 0:32, :] = turned_re[some]
                    ready[chan, peer, 32:64, :] = turned_im[some]
        peers = pl.ds(4 * block, 4)
        for chan in range(2):
            copy = pltpu.make_async_copy(
                ready.at[chan, peers], out.at[chan, peers], sems.at[9 + 2 * block + chan]
            )
            copy.start()
            out_copies.append(copy)
    row_copy.wait()
    row[...] = jnp.concatenate([lines[0, 0:1], lines[1, 0:1]], axis=0).astype(BF)
    for copy in out_copies:
        copy.wait()


def reverse_lanes(value):
    shape = (128, 128)
    flip = jnp.where(rows_of(shape) + lanes_of(shape) == 127, 1.0, 0.0).astype(BF)
    value = value.astype(BF)
    parts = [
        jnp.dot(value[:, 128 * part : 128 * part + 128], flip, preferred_element_type=F32)
        for part in reversed(range(N // 128))
    ]
    return jnp.concatenate(parts, axis=1)


def table_kernel(after, *refs):
    copies = [
        pltpu.make_async_copy(refs[0].at[which], refs[1 + which], refs[-1].at[which])
        for which in range(4)
    ]
    start_all(copies)
    for copy in copies:
        copy.wait()


def near_kernel(after, table, first, second, third, table_out, stack, sems):
    copies = [pltpu.make_async_copy(table, table_out, sems.at[0])] + [
        pltpu.make_async_copy(source, stack.at[which], sems.at[1 + which])
        for which, source in enumerate((first, second, third))
    ]
    start_all(copies)
    for copy in copies:
        copy.wait()


def filter_kernel(rank, own, other, special, out, mine, sem):
    me = rank[0]
    copy = pltpu.make_async_copy(own.at[0], mine, sem)
    copy.start()
    low = me < RANKS // 2
    shape = (SLOTS, SLOTS)
    wanted = jnp.where(low, 32, 31)
    pick = jnp.where(rows_of(shape) + lanes_of(shape) == wanted, 1.0, 0.0).astype(BF)
    top = rows_of((SLOTS, N)) == 0
    copy.wait()
    for part in range(2):
        sign = 1.0 if part == 0 else -1.0
        kept = jnp.where(low, mine[part, 0:32, :], mine[part, 1:33, :])
        moved = jnp.dot(pick, other[32 * part : 32 * part + 32], preferred_element_type=F32)
        mirror = reverse_lanes(moved)
        first = mine[part, 0:8, :]
        extra = jnp.broadcast_to(special[part : part + 1, :].astype(F32), (8, N))
        flipped = reverse_lanes(jnp.concatenate([first, extra], axis=0))
        around = pltpu.roll(flipped[0:8], 1, 1)
        head = jnp.where(me == 0, around, flipped[8:16])[0:1]
        mirror = jnp.where(jnp.logical_and(top, low), head, mirror)
        out[part, 0:32, :] = 0.5 * (kept + sign * mirror)
        out[part, 32:40, :] = 0.5 * (extra + sign * flipped[8:16])


def alternating(shape):
    return 1 - 2 * (lanes_of(shape) % 2)


def spectrum_kernel(
    rank, turned, cos_0, cos_1, sin_0, sin_1, filt_far, turn_far, half,
    spec, grad, grad_low, grad_row, filt, turn, left, sems
):
    me = rank[0]
    middle = N // 2
    copies = [
        pltpu.make_async_copy(filt_far, filt, sems.at[0]),
        pltpu.make_async_copy(turn_far.at[me], turn, sems.at[1]),
    ]
    start_all(copies)
    for seq in range(2):
        for pair in range(RANKS // 2):
            even = turned[RANKS * seq + 2 * pair]
            odd = turned[RANKS * seq + 2 * pair + 1]
            here = slice(128 * (pair % 4), 128 * (pair % 4) + 128)
            there = slice(middle + 128 * (pair % 4), middle + 128 * (pair % 4) + 128)
            for sig in range(2):
                lanes = slice(64 * sig, 64 * sig + 64)
                both = jnp.concatenate([even[:, lanes], odd[:, lanes]], axis=1)
                base = 272 * (pair // 4) + 32 * (2 * seq + sig)
                left[base : base + 32, here] = both[0:32]
                left[base : base + 32, there] = both[32:64]
                left[128 + base : 160 + base, here] = both[32:64]
                left[128 + base : 160 + base, there] = -both[0:32]
    packed = jnp.logical_and(rows_of((16, middle)) == 0, me == 0)
    for part in range(2):
        heads = []
        for which in range(4):
            base = 272 * part + 32 * which
            block = left[base : base + 16, middle:].astype(F32)
            heads.append(block[0:1])
            cleared = jnp.where(packed, 0.0, block).astype(BF)
            left[base : base + 16, middle:] = cleared
            left[128 + base : 144 + base, :middle] = cleared
        head = jnp.concatenate(heads + heads, axis=0)
        places = slice(middle * part, middle * part + middle)
        real = head * half[0:1, places]
        imag = -head * half[1:2, places]
        lines = slice(272 * part + 256, 272 * part + 272)
        left[lines, :middle] = jnp.concatenate([real, imag], axis=0).astype(BF)
        left[lines, middle:] = jnp.concatenate([imag, -real], axis=0).astype(BF)

    sign = alternating((1, WIDE)).astype(F32)
    for block in range(BLOCKS):
        wide = slice(WIDE * block, WIDE * block + WIDE)
        pieces = [table[:, wide] for table in (cos_0, cos_1, sin_0, sin_1)]
        halves = jnp.dot(
            left[...], jnp.concatenate(pieces, axis=0), preferred_element_type=F32
        )
        result = halves[:272] + sign * halves[272:]
        spec[:, wide] = result.astype(BF)
        real = 0.0
        imag = 0.0
        row_re = 0.0
        row_im = 0.0
        for seq in range(2):
            base = 64 * seq
            u_re, u_im = result[base : base + 32], result[base + 128 : base + 160]
            d_re, d_im = result[base + 32 : base + 64], result[base + 160 : base + 192]
            real = real + (u_re * d_re + u_im * d_im)
            imag = imag + (u_re * d_im - u_im * d_re)
            base = 256 + 2 * seq
            u_re, u_im = result[base : base + 1], result[base + 8 : base + 9]
            d_re, d_im = result[base + 1 : base + 2], result[base + 9 : base + 10]
            row_re = row_re + (u_re * d_re + u_im * d_im)
            row_im = row_im + (u_re * d_im - u_im * d_re)
        real = real * SCALE
        imag = imag * SCALE
        grad[0, :, wide] = real
        grad[1, :, wide] = imag
        grad_low[0:32, wide] = real.astype(BF)
        grad_low[32:64, wide] = imag.astype(BF)
        row_re = jnp.where(me == 0, row_re * SCALE, real[0:1])
        row_im = jnp.where(me == 0, row_im * SCALE, imag[0:1])
        grad_row[:, wide] = jnp.concatenate([row_re, row_im], axis=0).astype(BF)
    for copy in copies:
        copy.wait()


def products(u_re, u_im, d_re, d_im, h_re, h_im):
    return (
        u_re * h_re - u_im * h_im,
        u_re * h_im + u_im * h_re,
        h_re * d_re + h_im * d_im,
        h_re * d_im - h_im * d_re,
    )


def inverse_kernel(
    rank, spec, filt, cos_0, cos_1, sin_0, sin_1, turn, grad, out, grad_far, total, sem
):
    me = rank[0]
    copy = pltpu.make_async_copy(grad, grad_far, sem)
    copy.start()
    outer, inner = (0, 3), (1, 2)
    sign = alternating((1, WIDE)).astype(BF)
    packed_row = jnp.logical_and(rows_of((SLOTS, WIDE)) == 0, me == 0)
    for block in range(BLOCKS):
        wide = slice(WIDE * block, WIDE * block + WIDE)
        values = spec[:, wide].astype(F32)
        h_re, h_im = filt[0, 0:32, wide], filt[1, 0:32, wide]
        x_re, x_im = filt[0, 32:33, wide], filt[1, 32:33, wide]
        reals, imags, extra_re, extra_im = [], [], [], []
        for seq in range(2):
            base = 64 * seq
            p_re, p_im, q_re, q_im = products(
                values[base : base + 32],
                values[base + 128 : base + 160],
                values[base + 32 : base + 64],
                values[base + 160 : base + 192],
                h_re,
                h_im,
            )
            reals += [p_re, q_re]
            imags += [p_im, q_im]
            base = 256 + 2 * seq
            p_re, p_im, q_re, q_im = products(
                values[base : base + 1],
                values[base + 8 : base + 9],
                values[base + 1 : base + 2],
                values[base + 9 : base + 10],
                x_re,
                x_im,
            )
            extra_re += [p_re, q_re]
            extra_im += [p_im, q_im]

        def mixed(plain, extra, sign):
            return [jnp.where(packed_row, sign * e, p) for p, e in zip(plain, extra)]

        def joined(first, second):
            return jnp.concatenate(first + second, axis=0).astype(BF)

        less = [-value for value in imags]
        for parts, extra, crossed in (
            (outer, extra_re, mixed(reals, extra_im, -1.0)),
            (inner, extra_im, mixed(reals, extra_re, 1.0)),
        ):
            straight = joined(reals, mixed(imags, extra, 1.0))
            crossing = joined(less, crossed)
            for quarter in parts:
                rows = slice(WIDE * quarter, WIDE * quarter + WIDE)
                cos = (cos_0, cos_1)[quarter % 2][:, wide]
                sin = (sin_0, sin_1)[quarter % 2][:, wide]
                if quarter >= 2:
                    cos, sin = cos * sign, sin * sign
                part = lax.dot_general(
                    cos, straight, NT, preferred_element_type=F32
                ) + lax.dot_general(sin, crossing, NT, preferred_element_type=F32)
                if block == 0:
                    total[rows, :] = part
                else:
                    total[rows, :] += part

    for piece in range(BLOCKS):
        rows = slice(WIDE * piece, WIDE * piece + WIDE)
        turn_cos, turn_sin = split_turn(turn[rows, :])
        real = total[rows, :128]
        imag = total[rows, 128:]
        un_re = real * turn_cos - imag * turn_sin
        un_im = real * turn_sin + imag * turn_cos
        packed = jnp.logical_and(lanes_of((WIDE, 128)) % SLOTS == 0, me == 0)
        un_im = jnp.where(packed, imag * turn_sin, 2.0 * un_im).astype(BF)
        un_re = jnp.where(packed, real, 2.0 * un_re).astype(BF)
        out[0, rows, :] = jnp.concatenate([un_re[:, :64], un_im[:, :64]], axis=1)
        out[1, rows, :] = jnp.concatenate([un_re[:, 64:], un_im[:, 64:]], axis=1)
    copy.wait()


def result_kernel(arrived, table, gates, d_inp, d_val, d_outp, left, ready, sems):
    for chan in range(2):
        for pair in range(RANKS // 2):
            even = arrived[RANKS * chan + 2 * pair]
            odd = arrived[RANKS * chan + 2 * pair + 1]
            for sig in range(2):
                low = slice(32 * sig, 32 * sig + 32)
                high = slice(64 + 32 * sig, 96 + 32 * sig)
                base = 64 * (2 * chan + sig)
                left[base : base + 64, 128 * pair : 128 * pair + 128] = jnp.concatenate(
                    [even[:, low], odd[:, low], even[:, high], odd[:, high]], axis=1
                )
    copies = []
    for block in range(BLOCKS):
        wide = slice(WIDE * block, WIDE * block + WIDE)
        result = jnp.dot(left[...], table[:, wide], preferred_element_type=F32) * SCALE
        for chan in range(2):
            conv = result[128 * chan : 128 * chan + 64]
            gated = result[128 * chan + 64 : 128 * chan + 128]
            ready[2, chan, :, wide] = (gates[2, chan, :, wide].astype(F32) * conv).astype(BF)
            ready[0, chan, :, wide] = (gated * gates[1, chan, :, wide].astype(F32)).astype(BF)
            ready[1, chan, :, wide] = (gated * gates[0, chan, :, wide].astype(F32)).astype(BF)
        for which, target in enumerate((d_inp, d_val, d_outp)):
            copy = pltpu.make_async_copy(
                ready.at[which, :, :, pl.ds(WIDE * block, WIDE)],
                target.at[:, :, pl.ds(WIDE * block, WIDE)],
                sems.at[3 * block + which],
            )
            copy.start()
            copies.append(copy)
    for copy in copies:
        copy.wait()


def assemble_kernel(rank, own, other, special, out):
    me = rank[0]
    low = me < RANKS // 2
    shape = (SLOTS, SLOTS)
    wanted = jnp.where(low, 31, 32)
    pick = jnp.where(rows_of(shape) + lanes_of(shape) == wanted, 1.0, 0.0).astype(BF)
    top = rows_of((SLOTS, N)) == 0
    for part in range(2):
        sign = 1.0 if part == 0 else -1.0
        mine = own[part]
        shifted = pltpu.roll(mine, 1, 0)
        moved = jnp.dot(pick, other[32 * part : 32 * part + 32], preferred_element_type=F32)
        mirror = sign * reverse_lanes(moved)
        row = jnp.broadcast_to(special[part : part + 1, :].astype(F32), (16, N))
        turned = sign * reverse_lanes(row)
        head = jnp.where(me == RANKS // 2, row, turned)[0:1]
        out[0, part, 0:32, :] = jnp.where(low, mine, jnp.where(top, head, shifted))
        out[0, part, 32:64, :] = jnp.where(jnp.logical_and(top, ~low), shifted, mirror)


HBM = pl.BlockSpec(memory_space=pltpu.HBM)
VMEM = pl.BlockSpec(memory_space=pltpu.VMEM)
SMEM = pl.BlockSpec(memory_space=pltpu.SMEM)


def kept(value):
    return pltpu.with_memory_space_constraint(value, pltpu.HBM)


def sizes(flops, count=2**20):
    return pl.CostEstimate(flops=flops, bytes_accessed=count, transcendentals=0)


def params(mib):
    return pltpu.CompilerParams(vmem_limit_bytes=mib * 2**20)


def local(input_proj, value_proj, output_proj, grad_out, filter_spectrum):
    cos64, sin64 = dft_tables()
    half_tables = np.concatenate([cos64[: N // 2], sin64[: N // 2]]).reshape(4, WIDE, N)
    half_tables = jnp.asarray(half_tables.astype(ml_dtypes.bfloat16))
    sections = section_table()
    half_sections = jnp.asarray(sections[:, : N // 2])
    sections = jnp.asarray(sections)
    turn_out = jnp.asarray(forward_turn())
    turn_back = jnp.asarray(inverse_turn())
    half_rows = jnp.asarray(np.stack(half_turn()).astype(np.float32))
    ctx_rank = lax.axis_index("ctx")
    rank = ctx_rank.astype(jnp.int32).reshape(1)
    half_ranks = RANKS // 2
    mirror_of = [(r, RANKS - 1 - r) for r in range(RANKS)]
    special_of = [(r, RANKS - r) for r in range(1, RANKS) if r != half_ranks]
    special_of += [(0, half_ranks), (half_ranks, 0)]

    filter_rows = filter_spectrum.reshape(2, ROWS, N)[:, 32:64, :].astype(BF)
    other_rows = lax.ppermute(filter_rows.reshape(2 * SLOTS, N), "ctx", mirror_of)

    turned, filter_row = pl.pallas_call(
        section_kernel,
        out_shape=[pltpu.HBM((2, RANKS, ROWS, 128), BF), pltpu.VMEM((2, N), BF)],
        in_specs=[SMEM] + [HBM] * 7,
        out_specs=[HBM, VMEM],
        scratch_shapes=[
            pltpu.VMEM((4, 2, ROWS, N), BF),
            pltpu.VMEM((N, N // 2), BF),
            pltpu.VMEM((N // 2, 128), F32),
            pltpu.VMEM((2, RANKS, ROWS, 128), BF),
            pltpu.VMEM((512, N // 2), BF),
            pltpu.VMEM((2, 8, N), F32),
            pltpu.SemaphoreType.DMA((10 + 2 * BLOCKS,)),
        ],
        compiler_params=params(24),
        cost_estimate=sizes(A_COST),
        name="sections",
    )(
        rank,
        kept(input_proj),
        kept(value_proj),
        kept(output_proj),
        kept(grad_out),
        kept(half_sections),
        kept(turn_out),
        kept(filter_spectrum),
    )
    other_row = lax.ppermute(filter_row, "ctx", special_of)
    arrived = lax.all_to_all(
        turned.reshape(2 * RANKS, ROWS, 128), ("core", "ctx"), 0, 0, tiled=True
    )

    tables = pl.pallas_call(
        table_kernel,
        out_shape=[pltpu.VMEM((WIDE, N), BF)] * 4,
        in_specs=[HBM] * 2,
        out_specs=[VMEM] * 4,
        scratch_shapes=[pltpu.SemaphoreType.DMA((4,))],
        compiler_params=params(16),
        cost_estimate=sizes(W_COST),
        name="bring_tables",
    )(other_rows, kept(half_tables))
    folded_filter = pl.pallas_call(
        filter_kernel,
        out_shape=pltpu.HBM((2, 40, N), F32),
        in_specs=[SMEM, HBM, VMEM, VMEM],
        out_specs=VMEM,
        scratch_shapes=[pltpu.VMEM((2, ROWS, N), F32), pltpu.SemaphoreType.DMA(())],
        compiler_params=params(16),
        cost_estimate=sizes(2**24),
        name="fold_filter",
    )(rank, kept(filter_spectrum), other_rows, other_row)

    spectra, grad_own, grad_low, grad_row, filter_near, turn_near = pl.pallas_call(
        spectrum_kernel,
        out_shape=[
            pltpu.VMEM((272, N), BF),
            pltpu.VMEM((2, SLOTS, N), F32),
            pltpu.VMEM((2 * SLOTS, N), BF),
            pltpu.VMEM((2, N), BF),
            pltpu.VMEM((2, 40, N), F32),
            pltpu.VMEM((N, 128), F32),
        ],
        in_specs=[SMEM] + [VMEM] * 5 + [HBM, HBM, VMEM],
        out_specs=[VMEM] * 6,
        scratch_shapes=[
            pltpu.VMEM((544, N), BF),
            pltpu.SemaphoreType.DMA((2,)),
        ],
        compiler_params=params(20),
        cost_estimate=sizes(B_COST),
        name="spectra",
    )(
        rank,
        arrived,
        *tables,
        kept(folded_filter),
        kept(turn_back),
        half_rows,
    )

    mirror_grad = lax.ppermute(grad_low, "ctx", mirror_of)
    mirror_row = lax.ppermute(grad_row, "ctx", special_of)

    unturned, grad_far = pl.pallas_call(
        inverse_kernel,
        out_shape=[
            jax.ShapeDtypeStruct((2, N, 128), BF),
            pltpu.HBM((2, SLOTS, N), F32),
        ],
        in_specs=[SMEM] + [VMEM] * 8,
        out_specs=[VMEM, HBM],
        scratch_shapes=[pltpu.VMEM((N, 256), F32), pltpu.SemaphoreType.DMA(())],
        compiler_params=params(24),
        cost_estimate=sizes(B_COST),
        name="inverse",
    )(rank, spectra, filter_near, *tables, turn_near, grad_own)
    returned = lax.all_to_all(
        unturned.reshape(2 * RANKS, ROWS, 128), ("core", "ctx"), 0, 0, tiled=True
    )

    sections_near, gates_near = pl.pallas_call(
        near_kernel,
        out_shape=[pltpu.VMEM((N, N), BF), pltpu.VMEM((3, 2, ROWS, N), BF)],
        in_specs=[HBM] * 5,
        out_specs=[VMEM] * 2,
        scratch_shapes=[pltpu.SemaphoreType.DMA((4,))],
        compiler_params=params(16),
        cost_estimate=sizes(W_COST),
        name="bring_near",
    )(mirror_grad, kept(sections), kept(input_proj), kept(value_proj), kept(grad_out))
    grad_filter = pl.pallas_call(
        assemble_kernel,
        out_shape=jax.ShapeDtypeStruct((1, 2, ROWS, N), F32),
        in_specs=[SMEM] + [VMEM] * 3,
        out_specs=VMEM,
        compiler_params=params(16),
        cost_estimate=sizes(2**24),
        name="assemble",
    )(rank, grad_far, mirror_grad, mirror_row)

    grad_input, grad_value, grad_output_proj = pl.pallas_call(
        result_kernel,
        out_shape=[pltpu.HBM((2, ROWS, N), BF)] * 3,
        in_specs=[VMEM] * 3,
        out_specs=[HBM] * 3,
        scratch_shapes=[
            pltpu.VMEM((256, N), BF),
            pltpu.VMEM((3, 2, ROWS, N), BF),
            pltpu.SemaphoreType.DMA((3 * BLOCKS,)),
        ],
        compiler_params=params(20),
        cost_estimate=sizes(2 * 256 * N * N),
        name="results",
    )(returned, sections_near, gates_near)
    return (grad_input, grad_value, grad_output_proj, grad_filter)


def solution(mesh):
    split = Mesh(mesh.devices.reshape(-1, 2, RANKS), ("group", "core", "ctx"))
    data = P(("group", "core"), "ctx", None)
    filt = P(("group", "core"), None, "ctx", None)
    return jax.shard_map(
        local,
        mesh=split,
        in_specs=(data, data, data, data, filt),
        out_specs=(data, data, data, filt),
        check_vma=False,
    )
```

```python
import functools

import jax
import jax.numpy as jnp
import ml_dtypes
import numpy as np
from jax import lax
from jax.experimental import pallas as pl
from jax.experimental.pallas import tpu as pltpu
from jax.sharding import Mesh
from jax.sharding import PartitionSpec as P

N = 1024
TOTAL = N * N
RANKS = 16
ROWS = 64
SLOTS = 32
SCALE = 1.0 / TOTAL
BF = jnp.bfloat16
F32 = jnp.float32
NT = (((1,), (1,)), ((), ()))
BLOCKS = 4
WIDE = N // BLOCKS
A_COST = 10**10
B_COST = 10**10
W_COST = 4 * 10**10


def kept_rows():
    rank = np.arange(RANKS)
    return (ROWS * rank + (rank >= RANKS // 2))[:, None] + np.arange(SLOTS)[None, :]


def dft_tables():
    index = np.arange(N, dtype=np.int64)
    phase = (index[:, None] * index[None, :] % N).astype(np.float64) * (2.0 * np.pi / N)
    return np.cos(phase), np.sin(phase)


def section_table():
    cos, sin = dft_tables()
    rows = kept_rows()
    imag = -sin[rows]
    imag[0, 0] = 1.0 - 2.0 * (np.arange(N) % 2)
    both = np.stack([cos[rows], imag])
    both = both.reshape(2, RANKS // 2, 2, SLOTS, N).transpose(1, 0, 2, 3, 4)
    return both.reshape(N, N).astype(ml_dtypes.bfloat16)


def forward_turn():
    rows = kept_rows().reshape(1, -1, 1)
    place = np.arange(N).reshape(RANKS, 1, ROWS)
    phase = (rows * place % TOTAL).astype(np.float64) * (2.0 * np.pi / TOTAL)
    return np.concatenate([np.cos(phase), np.sin(phase)], axis=2).astype(np.float32)


def inverse_turn():
    rows = kept_rows().reshape(RANKS, 1, SLOTS)
    place = np.arange(N).reshape(1, N, 1)
    phase = (rows * place % TOTAL).astype(np.float64) * (2.0 * np.pi / TOTAL)
    cos, sin = np.cos(phase), np.sin(phase)
    sin[0, :, 0] = packed_turn()
    return np.concatenate([cos, cos, sin, sin], axis=2).astype(np.float32)


def half_turn():
    phase = np.arange(N) * (np.pi / N)
    return np.cos(phase), np.sin(phase)


def packed_turn():
    cos, sin = half_turn()
    middle = np.abs(np.arange(N) - N // 2 + 0.5) < N // 4
    return np.where(middle, -1.0 / np.where(middle, sin, 1.0), 1.0 / np.where(middle, 1.0, cos))


def lanes_of(shape):
    return lax.broadcasted_iota(jnp.int32, shape, len(shape) - 1)


def rows_of(shape):
    return lax.broadcasted_iota(jnp.int32, shape, len(shape) - 2)


def swap_halves(value):
    half = value.shape[-1] // 2
    return jnp.concatenate([value[..., half:], value[..., :half]], axis=-1)


def split_turn(packed):
    swapped = swap_halves(packed)
    low = lanes_of(packed.shape) < packed.shape[-1] // 2
    return jnp.where(low, packed, swapped), jnp.where(low, swapped, packed)


def start_all(copies):
    for copy in copies:
        copy.start()


def section_kernel(
    rank, inp, val, outp, grad, table, turn, filt, out, row,
    gates, sections, turns, ready, signals, lines, sems
):
    gate_copies = [
        pltpu.make_async_copy(source, gates.at[which], sems.at[which])
        for which, source in enumerate((inp, val, outp, grad))
    ]
    turn_copy = pltpu.make_async_copy(turn.at[rank[0]], turns, sems.at[4])
    blocks = [pl.ds(WIDE * block, WIDE) for block in range(BLOCKS)]
    table_copies = [
        pltpu.make_async_copy(table.at[rows], sections.at[rows], sems.at[5 + block])
        for block, rows in enumerate(blocks)
    ]
    row_copy = pltpu.make_async_copy(
        filt.at[0, :, pl.ds(0, 8)], lines, sems.at[9 + 2 * BLOCKS]
    )
    start_all(gate_copies + table_copies[:1] + [turn_copy] + table_copies[1:] + [row_copy])
    middle = N // 2
    for copy in gate_copies:
        copy.wait()
    for chan in range(2):
        gated = gates[0, chan].astype(F32) * gates[1, chan].astype(F32)
        conv = gates[3, chan].astype(F32) * gates[2, chan].astype(F32)
        for part in range(2):
            base = 256 * part + 128 * chan
            lanes = slice(middle * part, middle * part + middle)
            signals[base : base + 64, :] = gated[:, lanes].astype(BF)
            signals[base + 64 : base + 128, :] = conv[:, lanes].astype(BF)
    out_copies = []
    for block, rows in enumerate(blocks):
        table_copies[block].wait()
        halves = lax.dot_general(
            sections[rows, :], signals[...], NT, preferred_element_type=F32
        )
        odd_rows = (rows_of((WIDE, 1)) + (block >= BLOCKS // 2)) % 2
        section = halves[:, :256] + (1 - 2 * odd_rows).astype(F32) * halves[:, 256:]
        if block == 0:
            turn_copy.wait()
        for pair in range(2):
            base = WIDE // 2 * block + 64 * pair
            cos, sin = split_turn(turns[base : base + 64, :])
            for chan in range(2):
                lanes = slice(128 * chan, 128 * chan + 128)
                real = section[128 * pair : 128 * pair + 64, lanes]
                imag = section[128 * pair + 64 : 128 * pair + 128, lanes]
                turned_re = (real * cos + imag * sin).astype(BF)
                turned_im = (imag * cos - real * sin).astype(BF)
                for odd in range(2):
                    some = slice(32 * odd, 32 * odd + 32)
                    peer = 4 * block + 2 * pair + odd
                    ready[chan, peer, 0:32, :] = turned_re[some]
                    ready[chan, peer, 32:64, :] = turned_im[some]
        peers = pl.ds(4 * block, 4)
        for chan in range(2):
            copy = pltpu.make_async_copy(
                ready.at[chan, peers], out.at[chan, peers], sems.at[9 + 2 * block + chan]
            )
            copy.start()
            out_copies.append(copy)
    row_copy.wait()
    row[...] = jnp.concatenate([lines[0, 0:1], lines[1, 0:1]], axis=0).astype(BF)
    for copy in out_copies:
        copy.wait()


def reverse_lanes(value):
    shape = (128, 128)
    flip = jnp.where(rows_of(shape) + lanes_of(shape) == 127, 1.0, 0.0).astype(BF)
    value = value.astype(BF)
    parts = [
        jnp.dot(value[:, 128 * part : 128 * part + 128], flip, preferred_element_type=F32)
        for part in reversed(range(N // 128))
    ]
    return jnp.concatenate(parts, axis=1)


def table_kernel(after, *refs):
    copies = [
        pltpu.make_async_copy(refs[0].at[which], refs[1 + which], refs[-1].at[which])
        for which in range(4)
    ]
    start_all(copies)
    for copy in copies:
        copy.wait()


def near_kernel(after, table, first, second, third, table_out, stack, sems):
    copies = [pltpu.make_async_copy(table, table_out, sems.at[0])] + [
        pltpu.make_async_copy(source, stack.at[which], sems.at[1 + which])
        for which, source in enumerate((first, second, third))
    ]
    start_all(copies)
    for copy in copies:
        copy.wait()


def filter_kernel(rank, own, other, out, mine, sem):
    me = rank[0]
    copy = pltpu.make_async_copy(own.at[0], mine, sem)
    copy.start()
    low = me < RANKS // 2
    shape = (SLOTS, SLOTS)
    wanted = jnp.where(low, 32, 31)
    pick = jnp.where(rows_of(shape) + lanes_of(shape) == wanted, 1.0, 0.0).astype(BF)
    top = rows_of((SLOTS, N)) == 0
    copy.wait()
    for part in range(2):
        sign = 1.0 if part == 0 else -1.0
        kept = jnp.where(low, mine[part, 0:32, :], mine[part, 1:33, :])
        moved = jnp.dot(pick, other[32 * part : 32 * part + 32], preferred_element_type=F32)
        mirror = reverse_lanes(moved)
        first = mine[part, 0:8, :]
        flipped = reverse_lanes(jnp.concatenate([first, first], axis=0))
        head = jnp.where(me == 0, pltpu.roll(flipped[0:8], 1, 1)[0:1], 0.0)
        mirror = jnp.where(jnp.logical_and(top, low), head, mirror)
        out[part] = 0.5 * (kept + sign * mirror)


def special_rows(special):
    rows = [jnp.broadcast_to(special[part : part + 1, :], (8, N)) for part in range(2)]
    both = jnp.concatenate(rows, axis=0)
    return both.astype(F32), reverse_lanes(both)


def alternating(shape):
    return 1 - 2 * (lanes_of(shape) % 2)


def spectrum_kernel(
    rank, turned, cos_0, cos_1, sin_0, sin_1, filt_far, turn_far, half,
    spec, grad, grad_low, grad_row, filt, turn, left, sems
):
    me = rank[0]
    middle = N // 2
    copies = [
        pltpu.make_async_copy(filt_far, filt, sems.at[0]),
        pltpu.make_async_copy(turn_far.at[me], turn, sems.at[1]),
    ]
    start_all(copies)
    for seq in range(2):
        for pair in range(RANKS // 2):
            even = turned[RANKS * seq + 2 * pair]
            odd = turned[RANKS * seq + 2 * pair + 1]
            here = slice(128 * (pair % 4), 128 * (pair % 4) + 128)
            there = slice(middle + 128 * (pair % 4), middle + 128 * (pair % 4) + 128)
            for sig in range(2):
                lanes = slice(64 * sig, 64 * sig + 64)
                both = jnp.concatenate([even[:, lanes], odd[:, lanes]], axis=1)
                base = 272 * (pair // 4) + 32 * (2 * seq + sig)
                left[base : base + 32, here] = both[0:32]
                left[base : base + 32, there] = both[32:64]
                left[128 + base : 160 + base, here] = both[32:64]
                left[128 + base : 160 + base, there] = -both[0:32]
    packed = jnp.logical_and(rows_of((16, middle)) == 0, me == 0)
    for part in range(2):
        heads = []
        for which in range(4):
            base = 272 * part + 32 * which
            block = left[base : base + 16, middle:].astype(F32)
            heads.append(block[0:1])
            cleared = jnp.where(packed, 0.0, block).astype(BF)
            left[base : base + 16, middle:] = cleared
            left[128 + base : 144 + base, :middle] = cleared
        head = jnp.concatenate(heads + heads, axis=0)
        places = slice(middle * part, middle * part + middle)
        real = head * half[0:1, places]
        imag = -head * half[1:2, places]
        lines = slice(272 * part + 256, 272 * part + 272)
        left[lines, :middle] = jnp.concatenate([real, imag], axis=0).astype(BF)
        left[lines, middle:] = jnp.concatenate([imag, -real], axis=0).astype(BF)

    sign = alternating((1, WIDE)).astype(F32)
    for block in range(BLOCKS):
        wide = slice(WIDE * block, WIDE * block + WIDE)
        pieces = [table[:, wide] for table in (cos_0, cos_1, sin_0, sin_1)]
        halves = jnp.dot(
            left[...], jnp.concatenate(pieces, axis=0), preferred_element_type=F32
        )
        result = halves[:272] + sign * halves[272:]
        spec[:, wide] = result.astype(BF)
        real = 0.0
        imag = 0.0
        row_re = 0.0
        row_im = 0.0
        for seq in range(2):
            base = 64 * seq
            u_re, u_im = result[base : base + 32], result[base + 128 : base + 160]
            d_re, d_im = result[base + 32 : base + 64], result[base + 160 : base + 192]
            real = real + (u_re * d_re + u_im * d_im)
            imag = imag + (u_re * d_im - u_im * d_re)
            base = 256 + 2 * seq
            u_re, u_im = result[base : base + 1], result[base + 8 : base + 9]
            d_re, d_im = result[base + 1 : base + 2], result[base + 9 : base + 10]
            row_re = row_re + (u_re * d_re + u_im * d_im)
            row_im = row_im + (u_re * d_im - u_im * d_re)
        real = real * SCALE
        imag = imag * SCALE
        grad[0, :, wide] = real
        grad[1, :, wide] = imag
        grad_low[0:32, wide] = real.astype(BF)
        grad_low[32:64, wide] = imag.astype(BF)
        row_re = jnp.where(me == 0, row_re * SCALE, real[0:1])
        row_im = jnp.where(me == 0, row_im * SCALE, imag[0:1])
        grad_row[:, wide] = jnp.concatenate([row_re, row_im], axis=0).astype(BF)
    for copy in copies:
        copy.wait()


def products(u_re, u_im, d_re, d_im, h_re, h_im):
    return (
        u_re * h_re - u_im * h_im,
        u_re * h_im + u_im * h_re,
        h_re * d_re + h_im * d_im,
        h_re * d_im - h_im * d_re,
    )


def inverse_kernel(
    rank, spec, filt, special, cos_0, cos_1, sin_0, sin_1, turn, grad, out, grad_far, total, sem
):
    me = rank[0]
    copy = pltpu.make_async_copy(grad, grad_far, sem)
    copy.start()
    outer, inner = (0, 3), (1, 2)
    sign = alternating((1, WIDE)).astype(BF)
    top = rows_of((SLOTS, WIDE)) == 0
    packed_row = jnp.logical_and(top, me == 0)
    lone, flipped = special_rows(special)
    lone_re, lone_im = 0.5 * lone[0:1], 0.5 * lone[8:9]
    flip_re, flip_im = 0.5 * flipped[0:1], -0.5 * flipped[8:9]
    patched_row = jnp.logical_and(top, jnp.logical_and(me > 0, me < RANKS // 2))
    for block in range(BLOCKS):
        wide = slice(WIDE * block, WIDE * block + WIDE)
        values = spec[:, wide].astype(F32)
        h_re = filt[0, :, wide] + jnp.where(patched_row, flip_re[:, wide], 0.0)
        h_im = filt[1, :, wide] + jnp.where(patched_row, flip_im[:, wide], 0.0)
        x_re, x_im = (lone_re + flip_re)[:, wide], (lone_im + flip_im)[:, wide]
        reals, imags, extra_re, extra_im = [], [], [], []
        for seq in range(2):
            base = 64 * seq
            p_re, p_im, q_re, q_im = products(
                values[base : base + 32],
                values[base + 128 : base + 160],
                values[base + 32 : base + 64],
                values[base + 160 : base + 192],
                h_re,
                h_im,
            )
            reals += [p_re, q_re]
            imags += [p_im, q_im]
            base = 256 + 2 * seq
            p_re, p_im, q_re, q_im = products(
                values[base : base + 1],
                values[base + 8 : base + 9],
                values[base + 1 : base + 2],
                values[base + 9 : base + 10],
                x_re,
                x_im,
            )
            extra_re += [p_re, q_re]
            extra_im += [p_im, q_im]

        def mixed(plain, extra, sign):
            return [jnp.where(packed_row, sign * e, p) for p, e in zip(plain, extra)]

        def joined(first, second):
            return jnp.concatenate(first + second, axis=0).astype(BF)

        less = [-value for value in imags]
        for parts, extra, crossed in (
            (outer, extra_re, mixed(reals, extra_im, -1.0)),
            (inner, extra_im, mixed(reals, extra_re, 1.0)),
        ):
            straight = joined(reals, mixed(imags, extra, 1.0))
            crossing = joined(less, crossed)
            for quarter in parts:
                rows = slice(WIDE * quarter, WIDE * quarter + WIDE)
                cos = (cos_0, cos_1)[quarter % 2][:, wide]
                sin = (sin_0, sin_1)[quarter % 2][:, wide]
                if quarter >= 2:
                    cos, sin = cos * sign, sin * sign
                part = lax.dot_general(
                    cos, straight, NT, preferred_element_type=F32
                ) + lax.dot_general(sin, crossing, NT, preferred_element_type=F32)
                if block == 0:
                    total[rows, :] = part
                else:
                    total[rows, :] += part

    for piece in range(BLOCKS):
        rows = slice(WIDE * piece, WIDE * piece + WIDE)
        turn_cos, turn_sin = split_turn(turn[rows, :])
        real = total[rows, :128]
        imag = total[rows, 128:]
        un_re = real * turn_cos - imag * turn_sin
        un_im = real * turn_sin + imag * turn_cos
        packed = jnp.logical_and(lanes_of((WIDE, 128)) % SLOTS == 0, me == 0)
        un_im = jnp.where(packed, imag * turn_sin, 2.0 * un_im).astype(BF)
        un_re = jnp.where(packed, real, 2.0 * un_re).astype(BF)
        out[0, rows, :] = jnp.concatenate([un_re[:, :64], un_im[:, :64]], axis=1)
        out[1, rows, :] = jnp.concatenate([un_re[:, 64:], un_im[:, 64:]], axis=1)
    copy.wait()


def result_kernel(
    rank, arrived, table, gates, most, first, special,
    d_inp, d_val, d_outp, d_filt, left, ready, patch, sems
):
    me = rank[0]
    lone, flipped = special_rows(special)
    top = jnp.logical_and(rows_of((8, N)) == 0, me >= RANKS // 2)
    for part in range(2):
        lines = slice(8 * part, 8 * part + 8)
        sign = 1.0 if part == 0 else -1.0
        head = jnp.where(me == RANKS // 2, lone[lines], sign * flipped[lines])
        patch[part] = jnp.where(top, head, first[part])
    patch_copy = pltpu.make_async_copy(
        patch, d_filt.at[0, :, pl.ds(0, 8)], sems.at[3 * BLOCKS]
    )
    patch_copy.start()
    half = N // 2
    for chan in range(2):
        for pair in range(RANKS // 2):
            even = arrived[RANKS * chan + 2 * pair]
            odd = arrived[RANKS * chan + 2 * pair + 1]
            sign = alternating((1, 128)) * (1 if pair < RANKS // 4 else -1)
            for sig in range(2):
                low = slice(32 * sig, 32 * sig + 32)
                high = slice(64 + 32 * sig, 96 + 32 * sig)
                base = 64 * (2 * chan + sig)
                lanes = slice(128 * pair, 128 * pair + 128)
                block = jnp.concatenate(
                    [even[:, low], odd[:, low], even[:, high], odd[:, high]], axis=1
                )
                left[base : base + 64, lanes] = block
                left[256 + base : 320 + base, lanes] = block * sign.astype(BF)
    copies = []
    for block in range(BLOCKS // 2):
        near = slice(WIDE * block, WIDE * block + WIDE)
        halves = jnp.dot(left[...], table[:, near], preferred_element_type=F32) * SCALE
        for part in range(2):
            start = half * part + WIDE * block
            wide = slice(start, start + WIDE)
            result = halves[256 * part : 256 * part + 256]
            for chan in range(2):
                conv = result[128 * chan : 128 * chan + 64]
                gated = result[128 * chan + 64 : 128 * chan + 128]
                out_grad = gates[2, chan, :, wide].astype(F32) * conv
                ready[2, chan, :, wide] = out_grad.astype(BF)
                in_grad = gated * gates[1, chan, :, wide].astype(F32)
                ready[0, chan, :, wide] = in_grad.astype(BF)
                val_grad = gated * gates[0, chan, :, wide].astype(F32)
                ready[1, chan, :, wide] = val_grad.astype(BF)
            for which, target in enumerate((d_inp, d_val, d_outp)):
                copy = pltpu.make_async_copy(
                    ready.at[which, :, :, pl.ds(start, WIDE)],
                    target.at[:, :, pl.ds(start, WIDE)],
                    sems.at[3 * (2 * block + part) + which],
                )
                copy.start()
                copies.append(copy)
    for copy in copies:
        copy.wait()
    patch_copy.wait()


def assemble_kernel(rank, own, other, out, first, ready, sem):
    me = rank[0]
    low = me < RANKS // 2
    shape = (SLOTS, SLOTS)
    wanted = jnp.where(low, 31, 32)
    pick = jnp.where(rows_of(shape) + lanes_of(shape) == wanted, 1.0, 0.0).astype(BF)
    top = rows_of((SLOTS, N)) == 0
    for part in range(2):
        sign = 1.0 if part == 0 else -1.0
        mine = own[part]
        shifted = pltpu.roll(mine, 1, 0)
        moved = jnp.dot(pick, other[32 * part : 32 * part + 32], preferred_element_type=F32)
        mirror = sign * reverse_lanes(moved)
        lines = jnp.where(low, mine, shifted)
        first[part] = lines[0:8]
        ready[part, 0:32, :] = lines
        ready[part, 32:64, :] = jnp.where(jnp.logical_and(top, ~low), shifted, mirror)
    copy = pltpu.make_async_copy(
        ready.at[:, pl.ds(8, ROWS - 8)], out.at[0, :, pl.ds(8, ROWS - 8)], sem
    )
    copy.start()
    copy.wait()


HBM = pl.BlockSpec(memory_space=pltpu.HBM)
VMEM = pl.BlockSpec(memory_space=pltpu.VMEM)
SMEM = pl.BlockSpec(memory_space=pltpu.SMEM)


def kept(value):
    return pltpu.with_memory_space_constraint(value, pltpu.HBM)


def sizes(flops, count=2**20):
    return pl.CostEstimate(flops=flops, bytes_accessed=count, transcendentals=0)


def params(mib):
    return pltpu.CompilerParams(vmem_limit_bytes=mib * 2**20)


def local(input_proj, value_proj, output_proj, grad_out, filter_spectrum):
    cos64, sin64 = dft_tables()
    half_tables = np.concatenate([cos64[: N // 2], sin64[: N // 2]]).reshape(4, WIDE, N)
    half_tables = jnp.asarray(half_tables.astype(ml_dtypes.bfloat16))
    half_sections = jnp.asarray(section_table()[:, : N // 2])
    turn_out = jnp.asarray(forward_turn())
    turn_back = jnp.asarray(inverse_turn())
    half_rows = jnp.asarray(np.stack(half_turn()).astype(np.float32))
    ctx_rank = lax.axis_index("ctx")
    rank = ctx_rank.astype(jnp.int32).reshape(1)
    half_ranks = RANKS // 2
    mirror_of = [(r, RANKS - 1 - r) for r in range(RANKS)]
    special_of = [(r, RANKS - r) for r in range(1, RANKS) if r != half_ranks]
    special_of += [(0, half_ranks), (half_ranks, 0)]

    filter_rows = filter_spectrum.reshape(2, ROWS, N)[:, 32:64, :].astype(BF)
    other_rows = lax.ppermute(filter_rows.reshape(2 * SLOTS, N), "ctx", mirror_of)

    turned, filter_row = pl.pallas_call(
        section_kernel,
        out_shape=[pltpu.HBM((2, RANKS, ROWS, 128), BF), pltpu.VMEM((2, N), BF)],
        in_specs=[SMEM] + [HBM] * 7,
        out_specs=[HBM, VMEM],
        scratch_shapes=[
            pltpu.VMEM((4, 2, ROWS, N), BF),
            pltpu.VMEM((N, N // 2), BF),
            pltpu.VMEM((N // 2, 128), F32),
            pltpu.VMEM((2, RANKS, ROWS, 128), BF),
            pltpu.VMEM((512, N // 2), BF),
            pltpu.VMEM((2, 8, N), F32),
            pltpu.SemaphoreType.DMA((10 + 2 * BLOCKS,)),
        ],
        compiler_params=params(24),
        cost_estimate=sizes(A_COST),
        name="sections",
    )(
        rank,
        kept(input_proj),
        kept(value_proj),
        kept(output_proj),
        kept(grad_out),
        kept(half_sections),
        kept(turn_out),
        kept(filter_spectrum),
    )
    other_row = lax.ppermute(filter_row, "ctx", special_of)
    arrived = lax.all_to_all(
        turned.reshape(2 * RANKS, ROWS, 128), ("core", "ctx"), 0, 0, tiled=True
    )

    tables = pl.pallas_call(
        table_kernel,
        out_shape=[pltpu.VMEM((WIDE, N), BF)] * 4,
        in_specs=[HBM] * 2,
        out_specs=[VMEM] * 4,
        scratch_shapes=[pltpu.SemaphoreType.DMA((4,))],
        compiler_params=params(16),
        cost_estimate=sizes(W_COST),
        name="bring_tables",
    )(other_rows, kept(half_tables))
    folded_filter = pl.pallas_call(
        filter_kernel,
        out_shape=pltpu.HBM((2, SLOTS, N), F32),
        in_specs=[SMEM, HBM, VMEM],
        out_specs=VMEM,
        scratch_shapes=[pltpu.VMEM((2, ROWS, N), F32), pltpu.SemaphoreType.DMA(())],
        compiler_params=params(16),
        cost_estimate=sizes(2**24),
        name="fold_filter",
    )(rank, kept(filter_spectrum), other_rows)

    spectra, grad_own, grad_low, grad_row, filter_near, turn_near = pl.pallas_call(
        spectrum_kernel,
        out_shape=[
            pltpu.VMEM((272, N), BF),
            pltpu.VMEM((2, SLOTS, N), F32),
            pltpu.VMEM((2 * SLOTS, N), BF),
            pltpu.VMEM((2, N), BF),
            pltpu.VMEM((2, SLOTS, N), F32),
            pltpu.VMEM((N, 128), F32),
        ],
        in_specs=[SMEM] + [VMEM] * 5 + [HBM, HBM, VMEM],
        out_specs=[VMEM] * 6,
        scratch_shapes=[
            pltpu.VMEM((544, N), BF),
            pltpu.SemaphoreType.DMA((2,)),
        ],
        compiler_params=params(20),
        cost_estimate=sizes(2**24),
        name="spectra",
    )(
        rank,
        arrived,
        *tables,
        kept(folded_filter),
        kept(turn_back),
        half_rows,
    )

    mirror_grad = lax.ppermute(grad_low, "ctx", mirror_of)
    mirror_row = lax.ppermute(grad_row, "ctx", special_of)

    unturned, grad_far = pl.pallas_call(
        inverse_kernel,
        out_shape=[
            jax.ShapeDtypeStruct((2, N, 128), BF),
            pltpu.HBM((2, SLOTS, N), F32),
        ],
        in_specs=[SMEM] + [VMEM] * 9,
        out_specs=[VMEM, HBM],
        scratch_shapes=[pltpu.VMEM((N, 256), F32), pltpu.SemaphoreType.DMA(())],
        compiler_params=params(24),
        cost_estimate=sizes(B_COST),
        name="inverse",
    )(rank, spectra, filter_near, other_row, *tables, turn_near, grad_own)
    returned = lax.all_to_all(
        unturned.reshape(2 * RANKS, ROWS, 128), ("core", "ctx"), 0, 0, tiled=True
    )

    sections_near, gates_near = pl.pallas_call(
        near_kernel,
        out_shape=[pltpu.VMEM((N, N // 2), BF), pltpu.VMEM((3, 2, ROWS, N), BF)],
        in_specs=[HBM] * 5,
        out_specs=[VMEM] * 2,
        scratch_shapes=[pltpu.SemaphoreType.DMA((4,))],
        compiler_params=params(16),
        cost_estimate=sizes(W_COST),
        name="bring_near",
    )(mirror_grad, kept(half_sections), kept(input_proj), kept(value_proj), kept(grad_out))
    most_rows, first_rows = pl.pallas_call(
        assemble_kernel,
        out_shape=[
            pltpu.HBM((1, 2, ROWS, N), F32),
            pltpu.VMEM((2, 8, N), F32),
        ],
        in_specs=[SMEM] + [VMEM] * 2,
        out_specs=[HBM, VMEM],
        scratch_shapes=[pltpu.VMEM((2, ROWS, N), F32), pltpu.SemaphoreType.DMA(())],
        compiler_params=params(16),
        cost_estimate=sizes(2**24),
        name="assemble",
    )(rank, grad_far, mirror_grad)

    grad_input, grad_value, grad_output_proj, grad_filter = pl.pallas_call(
        result_kernel,
        out_shape=[pltpu.HBM((2, ROWS, N), BF)] * 3 + [pltpu.HBM((1, 2, ROWS, N), F32)],
        in_specs=[SMEM] + [VMEM] * 3 + [HBM, VMEM, VMEM],
        out_specs=[HBM] * 4,
        input_output_aliases={4: 3},
        scratch_shapes=[
            pltpu.VMEM((512, N), BF),
            pltpu.VMEM((3, 2, ROWS, N), BF),
            pltpu.VMEM((2, 8, N), F32),
            pltpu.SemaphoreType.DMA((3 * BLOCKS + 1,)),
        ],
        compiler_params=params(20),
        cost_estimate=sizes(2 * 256 * N * N),
        name="results",
    )(rank, returned, sections_near, gates_near, most_rows, first_rows, mirror_row)
    return (grad_input, grad_value, grad_output_proj, grad_filter)


def solution(mesh):
    split = Mesh(mesh.devices.reshape(-1, 2, RANKS), ("group", "core", "ctx"))
    data = P(("group", "core"), "ctx", None)
    filt = P(("group", "core"), None, "ctx", None)
    return jax.shard_map(
        local,
        mesh=split,
        in_specs=(data, data, data, data, filt),
        out_specs=(data, data, data, filt),
        check_vma=False,
    )
```

```python
import functools

import jax
import jax.numpy as jnp
import ml_dtypes
import numpy as np
from jax import lax
from jax.experimental import pallas as pl
from jax.experimental.pallas import tpu as pltpu
from jax.sharding import Mesh
from jax.sharding import PartitionSpec as P

N = 1024
TOTAL = N * N
RANKS = 16
ROWS = 64
SLOTS = 32
SCALE = 1.0 / TOTAL
BF = jnp.bfloat16
F32 = jnp.float32
NT = (((1,), (1,)), ((), ()))
BLOCKS = 4
WIDE = N // BLOCKS
A_COST = 10**10
B_COST = 10**10
W_COST = 4 * 10**10


def kept_rows():
    rank = np.arange(RANKS)
    return (ROWS * rank + (rank >= RANKS // 2))[:, None] + np.arange(SLOTS)[None, :]


def dft_tables():
    index = np.arange(N, dtype=np.int64)
    phase = (index[:, None] * index[None, :] % N).astype(np.float64) * (2.0 * np.pi / N)
    return np.cos(phase), np.sin(phase)


def section_table():
    cos, sin = dft_tables()
    rows = kept_rows()
    imag = -sin[rows]
    imag[0, 0] = 1.0 - 2.0 * (np.arange(N) % 2)
    both = np.stack([cos[rows], imag])
    both = both.reshape(2, RANKS // 2, 2, SLOTS, N).transpose(1, 0, 2, 3, 4)
    return both.reshape(N, N).astype(ml_dtypes.bfloat16)


def forward_turn():
    rows = kept_rows().reshape(1, -1, 1)
    place = np.arange(N).reshape(RANKS, 1, ROWS)
    phase = (rows * place % TOTAL).astype(np.float64) * (2.0 * np.pi / TOTAL)
    return np.concatenate([np.cos(phase), np.sin(phase)], axis=2).astype(np.float32)


def inverse_turn():
    rows = kept_rows().reshape(RANKS, 1, SLOTS)
    place = np.arange(N).reshape(1, N, 1)
    phase = (rows * place % TOTAL).astype(np.float64) * (2.0 * np.pi / TOTAL)
    cos, sin = np.cos(phase), np.sin(phase)
    sin[0, :, 0] = packed_turn()
    return np.concatenate([cos, cos, sin, sin], axis=2).astype(np.float32)


def half_turn():
    phase = np.arange(N) * (np.pi / N)
    return np.cos(phase), np.sin(phase)


def packed_turn():
    cos, sin = half_turn()
    middle = np.abs(np.arange(N) - N // 2 + 0.5) < N // 4
    return np.where(middle, -1.0 / np.where(middle, sin, 1.0), 1.0 / np.where(middle, 1.0, cos))


def lanes_of(shape):
    return lax.broadcasted_iota(jnp.int32, shape, len(shape) - 1)


def rows_of(shape):
    return lax.broadcasted_iota(jnp.int32, shape, len(shape) - 2)


def swap_halves(value):
    half = value.shape[-1] // 2
    return jnp.concatenate([value[..., half:], value[..., :half]], axis=-1)


def split_turn(packed):
    swapped = swap_halves(packed)
    low = lanes_of(packed.shape) < packed.shape[-1] // 2
    return jnp.where(low, packed, swapped), jnp.where(low, swapped, packed)


def start_all(copies):
    for copy in copies:
        copy.start()


def gather_kernel(
    rank, inp, val, outp, grad, table, turn, filt,
    rows, row, signals, sections, turns, gates, lines, first, sems
):
    line_copy = pltpu.make_async_copy(filt.at[0, :, pl.ds(SLOTS, SLOTS)], lines, sems.at[0])
    row_copy = pltpu.make_async_copy(filt.at[0, :, pl.ds(0, 8)], first, sems.at[1])
    gate_copies = [
        pltpu.make_async_copy(source, gates.at[which], sems.at[2 + which])
        for which, source in enumerate((inp, val, outp, grad))
    ]
    table_copy = pltpu.make_async_copy(table, sections, sems.at[6])
    turn_copy = pltpu.make_async_copy(turn.at[rank[0]], turns, sems.at[7])
    start_all([line_copy] + gate_copies + [table_copy, turn_copy, row_copy])
    middle = N // 2
    line_copy.wait()
    for part in range(2):
        rows[SLOTS * part : SLOTS * part + SLOTS, :] = lines[part].astype(BF)
    for copy in gate_copies:
        copy.wait()
    for chan in range(2):
        gated = gates[0, chan].astype(F32) * gates[1, chan].astype(F32)
        conv = gates[3, chan].astype(F32) * gates[2, chan].astype(F32)
        for part in range(2):
            base = 256 * part + 128 * chan
            lanes = slice(middle * part, middle * part + middle)
            signals[base : base + 64, :] = gated[:, lanes].astype(BF)
            signals[base + 64 : base + 128, :] = conv[:, lanes].astype(BF)
    row_copy.wait()
    row[...] = jnp.concatenate([first[0, 0:1], first[1, 0:1]], axis=0).astype(BF)
    table_copy.wait()
    turn_copy.wait()


def section_kernel(signals, sections, turns, row, out, row_out, ready, sems):
    row_out[...] = row[...]
    out_copies = []
    for block in range(BLOCKS):
        rows = slice(WIDE * block, WIDE * block + WIDE)
        halves = lax.dot_general(
            sections[rows, :], signals[...], NT, preferred_element_type=F32
        )
        odd_rows = (rows_of((WIDE, 1)) + (block >= BLOCKS // 2)) % 2
        section = halves[:, :256] + (1 - 2 * odd_rows).astype(F32) * halves[:, 256:]
        for pair in range(2):
            base = WIDE // 2 * block + 64 * pair
            cos, sin = split_turn(turns[base : base + 64, :])
            for chan in range(2):
                lanes = slice(128 * chan, 128 * chan + 128)
                real = section[128 * pair : 128 * pair + 64, lanes]
                imag = section[128 * pair + 64 : 128 * pair + 128, lanes]
                turned_re = (real * cos + imag * sin).astype(BF)
                turned_im = (imag * cos - real * sin).astype(BF)
                for odd in range(2):
                    some = slice(32 * odd, 32 * odd + 32)
                    peer = 4 * block + 2 * pair + odd
                    ready[chan, peer, 0:32, :] = turned_re[some]
                    ready[chan, peer, 32:64, :] = turned_im[some]
        peers = pl.ds(4 * block, 4)
        for chan in range(2):
            copy = pltpu.make_async_copy(
                ready.at[chan, peers], out.at[chan, peers], sems.at[2 * block + chan]
            )
            copy.start()
            out_copies.append(copy)
    for copy in out_copies:
        copy.wait()


def reverse_lanes(value):
    shape = (128, 128)
    flip = jnp.where(rows_of(shape) + lanes_of(shape) == 127, 1.0, 0.0).astype(BF)
    value = value.astype(BF)
    parts = [
        jnp.dot(value[:, 128 * part : 128 * part + 128], flip, preferred_element_type=F32)
        for part in reversed(range(N // 128))
    ]
    return jnp.concatenate(parts, axis=1)


def table_kernel(after, *refs):
    copies = [
        pltpu.make_async_copy(refs[0].at[which], refs[1 + which], refs[-1].at[which])
        for which in range(4)
    ]
    start_all(copies)
    for copy in copies:
        copy.wait()


def near_kernel(after, table, first, second, third, table_out, stack, sems):
    copies = [pltpu.make_async_copy(table, table_out, sems.at[0])] + [
        pltpu.make_async_copy(source, stack.at[which], sems.at[1 + which])
        for which, source in enumerate((first, second, third))
    ]
    start_all(copies)
    for copy in copies:
        copy.wait()


def filter_kernel(rank, own, other, out, mine, sem):
    me = rank[0]
    copy = pltpu.make_async_copy(own.at[0], mine, sem)
    copy.start()
    low = me < RANKS // 2
    shape = (SLOTS, SLOTS)
    wanted = jnp.where(low, 32, 31)
    pick = jnp.where(rows_of(shape) + lanes_of(shape) == wanted, 1.0, 0.0).astype(BF)
    top = rows_of((SLOTS, N)) == 0
    copy.wait()
    for part in range(2):
        sign = 1.0 if part == 0 else -1.0
        kept = jnp.where(low, mine[part, 0:32, :], mine[part, 1:33, :])
        moved = jnp.dot(pick, other[32 * part : 32 * part + 32], preferred_element_type=F32)
        mirror = reverse_lanes(moved)
        first = mine[part, 0:8, :]
        flipped = reverse_lanes(jnp.concatenate([first, first], axis=0))
        head = jnp.where(me == 0, pltpu.roll(flipped[0:8], 1, 1)[0:1], 0.0)
        mirror = jnp.where(jnp.logical_and(top, low), head, mirror)
        out[part] = 0.5 * (kept + sign * mirror)


def special_rows(special):
    rows = [jnp.broadcast_to(special[part : part + 1, :], (8, N)) for part in range(2)]
    both = jnp.concatenate(rows, axis=0)
    return both.astype(F32), reverse_lanes(both)


def alternating(shape):
    return 1 - 2 * (lanes_of(shape) % 2)


def spectrum_kernel(
    rank, turned, cos_0, cos_1, sin_0, sin_1, filt_far, turn_far, half,
    spec, grad, grad_low, grad_row, filt, turn, left, sems
):
    me = rank[0]
    middle = N // 2
    copies = [
        pltpu.make_async_copy(filt_far, filt, sems.at[0]),
        pltpu.make_async_copy(turn_far.at[me], turn, sems.at[1]),
    ]
    start_all(copies)
    for seq in range(2):
        for pair in range(RANKS // 2):
            even = turned[RANKS * seq + 2 * pair]
            odd = turned[RANKS * seq + 2 * pair + 1]
            here = slice(128 * (pair % 4), 128 * (pair % 4) + 128)
            there = slice(middle + 128 * (pair % 4), middle + 128 * (pair % 4) + 128)
            for sig in range(2):
                lanes = slice(64 * sig, 64 * sig + 64)
                both = jnp.concatenate([even[:, lanes], odd[:, lanes]], axis=1)
                base = 272 * (pair // 4) + 32 * (2 * seq + sig)
                left[base : base + 32, here] = both[0:32]
                left[base : base + 32, there] = both[32:64]
                left[128 + base : 160 + base, here] = both[32:64]
                left[128 + base : 160 + base, there] = -both[0:32]
    packed = jnp.logical_and(rows_of((16, middle)) == 0, me == 0)
    for part in range(2):
        heads = []
        for which in range(4):
            base = 272 * part + 32 * which
            block = left[base : base + 16, middle:].astype(F32)
            heads.append(block[0:1])
            cleared = jnp.where(packed, 0.0, block).astype(BF)
            left[base : base + 16, middle:] = cleared
            left[128 + base : 144 + base, :middle] = cleared
        head = jnp.concatenate(heads + heads, axis=0)
        places = slice(middle * part, middle * part + middle)
        real = head * half[0:1, places]
        imag = -head * half[1:2, places]
        lines = slice(272 * part + 256, 272 * part + 272)
        left[lines, :middle] = jnp.concatenate([real, imag], axis=0).astype(BF)
        left[lines, middle:] = jnp.concatenate([imag, -real], axis=0).astype(BF)

    sign = alternating((1, WIDE)).astype(F32)
    for block in range(BLOCKS):
        wide = slice(WIDE * block, WIDE * block + WIDE)
        pieces = [table[:, wide] for table in (cos_0, cos_1, sin_0, sin_1)]
        halves = jnp.dot(
            left[...], jnp.concatenate(pieces, axis=0), preferred_element_type=F32
        )
        result = halves[:272] + sign * halves[272:]
        spec[:, wide] = result.astype(BF)
        real = 0.0
        imag = 0.0
        row_re = 0.0
        row_im = 0.0
        for seq in range(2):
            base = 64 * seq
            u_re, u_im = result[base : base + 32], result[base + 128 : base + 160]
            d_re, d_im = result[base + 32 : base + 64], result[base + 160 : base + 192]
            real = real + (u_re * d_re + u_im * d_im)
            imag = imag + (u_re * d_im - u_im * d_re)
            base = 256 + 2 * seq
            u_re, u_im = result[base : base + 1], result[base + 8 : base + 9]
            d_re, d_im = result[base + 1 : base + 2], result[base + 9 : base + 10]
            row_re = row_re + (u_re * d_re + u_im * d_im)
            row_im = row_im + (u_re * d_im - u_im * d_re)
        real = real * SCALE
        imag = imag * SCALE
        grad[0, :, wide] = real
        grad[1, :, wide] = imag
        grad_low[0:32, wide] = real.astype(BF)
        grad_low[32:64, wide] = imag.astype(BF)
        row_re = jnp.where(me == 0, row_re * SCALE, real[0:1])
        row_im = jnp.where(me == 0, row_im * SCALE, imag[0:1])
        grad_row[:, wide] = jnp.concatenate([row_re, row_im], axis=0).astype(BF)
    for copy in copies:
        copy.wait()


def products(u_re, u_im, d_re, d_im, h_re, h_im):
    return (
        u_re * h_re - u_im * h_im,
        u_re * h_im + u_im * h_re,
        h_re * d_re + h_im * d_im,
        h_re * d_im - h_im * d_re,
    )


def inverse_kernel(
    rank, spec, filt, special, cos_0, cos_1, sin_0, sin_1, turn, grad, out, grad_far, total, sem
):
    me = rank[0]
    copy = pltpu.make_async_copy(grad, grad_far, sem)
    copy.start()
    outer, inner = (0, 3), (1, 2)
    sign = alternating((1, WIDE)).astype(BF)
    top = rows_of((SLOTS, WIDE)) == 0
    packed_row = jnp.logical_and(top, me == 0)
    lone, flipped = special_rows(special)
    lone_re, lone_im = 0.5 * lone[0:1], 0.5 * lone[8:9]
    flip_re, flip_im = 0.5 * flipped[0:1], -0.5 * flipped[8:9]
    patched_row = jnp.logical_and(top, jnp.logical_and(me > 0, me < RANKS // 2))
    for block in range(BLOCKS):
        wide = slice(WIDE * block, WIDE * block + WIDE)
        values = spec[:, wide].astype(F32)
        h_re = filt[0, :, wide] + jnp.where(patched_row, flip_re[:, wide], 0.0)
        h_im = filt[1, :, wide] + jnp.where(patched_row, flip_im[:, wide], 0.0)
        x_re, x_im = (lone_re + flip_re)[:, wide], (lone_im + flip_im)[:, wide]
        reals, imags, extra_re, extra_im = [], [], [], []
        for seq in range(2):
            base = 64 * seq
            p_re, p_im, q_re, q_im = products(
                values[base : base + 32],
                values[base + 128 : base + 160],
                values[base + 32 : base + 64],
                values[base + 160 : base + 192],
                h_re,
                h_im,
            )
            reals += [p_re, q_re]
            imags += [p_im, q_im]
            base = 256 + 2 * seq
            p_re, p_im, q_re, q_im = products(
                values[base : base + 1],
                values[base + 8 : base + 9],
                values[base + 1 : base + 2],
                values[base + 9 : base + 10],
                x_re,
                x_im,
            )
            extra_re += [p_re, q_re]
            extra_im += [p_im, q_im]

        def mixed(plain, extra, sign):
            return [jnp.where(packed_row, sign * e, p) for p, e in zip(plain, extra)]

        def joined(first, second):
            return jnp.concatenate(first + second, axis=0).astype(BF)

        less = [-value for value in imags]
        for parts, extra, crossed in (
            (outer, extra_re, mixed(reals, extra_im, -1.0)),
            (inner, extra_im, mixed(reals, extra_re, 1.0)),
        ):
            straight = joined(reals, mixed(imags, extra, 1.0))
            crossing = joined(less, crossed)
            for quarter in parts:
                rows = slice(WIDE * quarter, WIDE * quarter + WIDE)
                cos = (cos_0, cos_1)[quarter % 2][:, wide]
                sin = (sin_0, sin_1)[quarter % 2][:, wide]
                if quarter >= 2:
                    cos, sin = cos * sign, sin * sign
                part = lax.dot_general(
                    cos, straight, NT, preferred_element_type=F32
                ) + lax.dot_general(sin, crossing, NT, preferred_element_type=F32)
                if block == 0:
                    total[rows, :] = part
                else:
                    total[rows, :] += part

    for piece in range(BLOCKS):
        rows = slice(WIDE * piece, WIDE * piece + WIDE)
        turn_cos, turn_sin = split_turn(turn[rows, :])
        real = total[rows, :128]
        imag = total[rows, 128:]
        un_re = real * turn_cos - imag * turn_sin
        un_im = real * turn_sin + imag * turn_cos
        packed = jnp.logical_and(lanes_of((WIDE, 128)) % SLOTS == 0, me == 0)
        un_im = jnp.where(packed, imag * turn_sin, 2.0 * un_im).astype(BF)
        un_re = jnp.where(packed, real, 2.0 * un_re).astype(BF)
        out[0, rows, :] = jnp.concatenate([un_re[:, :64], un_im[:, :64]], axis=1)
        out[1, rows, :] = jnp.concatenate([un_re[:, 64:], un_im[:, 64:]], axis=1)
    copy.wait()


def result_kernel(
    rank, arrived, table, gates, most, first, special,
    d_inp, d_val, d_outp, d_filt, left, ready, patch, sems
):
    me = rank[0]
    lone, flipped = special_rows(special)
    top = jnp.logical_and(rows_of((8, N)) == 0, me >= RANKS // 2)
    for part in range(2):
        lines = slice(8 * part, 8 * part + 8)
        sign = 1.0 if part == 0 else -1.0
        head = jnp.where(me == RANKS // 2, lone[lines], sign * flipped[lines])
        patch[part] = jnp.where(top, head, first[part])
    patch_copy = pltpu.make_async_copy(
        patch, d_filt.at[0, :, pl.ds(0, 8)], sems.at[3 * BLOCKS]
    )
    patch_copy.start()
    half = N // 2
    for chan in range(2):
        for pair in range(RANKS // 2):
            even = arrived[RANKS * chan + 2 * pair]
            odd = arrived[RANKS * chan + 2 * pair + 1]
            sign = alternating((1, 128)) * (1 if pair < RANKS // 4 else -1)
            for sig in range(2):
                low = slice(32 * sig, 32 * sig + 32)
                high = slice(64 + 32 * sig, 96 + 32 * sig)
                base = 64 * (2 * chan + sig)
                lanes = slice(128 * pair, 128 * pair + 128)
                block = jnp.concatenate(
                    [even[:, low], odd[:, low], even[:, high], odd[:, high]], axis=1
                )
                left[base : base + 64, lanes] = block
                left[256 + base : 320 + base, lanes] = block * sign.astype(BF)
    copies = []
    for block in range(BLOCKS // 2):
        near = slice(WIDE * block, WIDE * block + WIDE)
        halves = jnp.dot(left[...], table[:, near], preferred_element_type=F32) * SCALE
        for part in range(2):
            start = half * part + WIDE * block
            wide = slice(start, start + WIDE)
            result = halves[256 * part : 256 * part + 256]
            for chan in range(2):
                conv = result[128 * chan : 128 * chan + 64]
                gated = result[128 * chan + 64 : 128 * chan + 128]
                out_grad = gates[2, chan, :, wide].astype(F32) * conv
                ready[2, chan, :, wide] = out_grad.astype(BF)
                in_grad = gated * gates[1, chan, :, wide].astype(F32)
                ready[0, chan, :, wide] = in_grad.astype(BF)
                val_grad = gated * gates[0, chan, :, wide].astype(F32)
                ready[1, chan, :, wide] = val_grad.astype(BF)
            for which, target in enumerate((d_inp, d_val, d_outp)):
                copy = pltpu.make_async_copy(
                    ready.at[which, :, :, pl.ds(start, WIDE)],
                    target.at[:, :, pl.ds(start, WIDE)],
                    sems.at[3 * (2 * block + part) + which],
                )
                copy.start()
                copies.append(copy)
    for copy in copies:
        copy.wait()
    patch_copy.wait()


def assemble_kernel(rank, own, other, out, first, ready, sem):
    me = rank[0]
    low = me < RANKS // 2
    shape = (SLOTS, SLOTS)
    wanted = jnp.where(low, 31, 32)
    pick = jnp.where(rows_of(shape) + lanes_of(shape) == wanted, 1.0, 0.0).astype(BF)
    top = rows_of((SLOTS, N)) == 0
    for part in range(2):
        sign = 1.0 if part == 0 else -1.0
        mine = own[part]
        shifted = pltpu.roll(mine, 1, 0)
        moved = jnp.dot(pick, other[32 * part : 32 * part + 32], preferred_element_type=F32)
        mirror = sign * reverse_lanes(moved)
        lines = jnp.where(low, mine, shifted)
        first[part] = lines[0:8]
        ready[part, 0:32, :] = lines
        ready[part, 32:64, :] = jnp.where(jnp.logical_and(top, ~low), shifted, mirror)
    copy = pltpu.make_async_copy(
        ready.at[:, pl.ds(8, ROWS - 8)], out.at[0, :, pl.ds(8, ROWS - 8)], sem
    )
    copy.start()
    copy.wait()


HBM = pl.BlockSpec(memory_space=pltpu.HBM)
VMEM = pl.BlockSpec(memory_space=pltpu.VMEM)
SMEM = pl.BlockSpec(memory_space=pltpu.SMEM)


def kept(value):
    return pltpu.with_memory_space_constraint(value, pltpu.HBM)


def sizes(flops, count=2**20):
    return pl.CostEstimate(flops=flops, bytes_accessed=count, transcendentals=0)


def params(mib):
    return pltpu.CompilerParams(vmem_limit_bytes=mib * 2**20)


def local(input_proj, value_proj, output_proj, grad_out, filter_spectrum):
    cos64, sin64 = dft_tables()
    half_tables = np.concatenate([cos64[: N // 2], sin64[: N // 2]]).reshape(4, WIDE, N)
    half_tables = jnp.asarray(half_tables.astype(ml_dtypes.bfloat16))
    half_sections = jnp.asarray(section_table()[:, : N // 2])
    turn_out = jnp.asarray(forward_turn())
    turn_back = jnp.asarray(inverse_turn())
    half_rows = jnp.asarray(np.stack(half_turn()).astype(np.float32))
    ctx_rank = lax.axis_index("ctx")
    rank = ctx_rank.astype(jnp.int32).reshape(1)
    half_ranks = RANKS // 2
    mirror_of = [(r, RANKS - 1 - r) for r in range(RANKS)]
    special_of = [(r, RANKS - r) for r in range(1, RANKS) if r != half_ranks]
    special_of += [(0, half_ranks), (half_ranks, 0)]

    filter_rows, filter_row, signals, sections, turns = pl.pallas_call(
        gather_kernel,
        out_shape=[
            pltpu.VMEM((2 * SLOTS, N), BF),
            pltpu.VMEM((2, N), BF),
            pltpu.VMEM((512, N // 2), BF),
            pltpu.VMEM((N, N // 2), BF),
            pltpu.VMEM((N // 2, 128), F32),
        ],
        in_specs=[SMEM] + [HBM] * 7,
        out_specs=[VMEM] * 5,
        scratch_shapes=[
            pltpu.VMEM((4, 2, ROWS, N), BF),
            pltpu.VMEM((2, SLOTS, N), F32),
            pltpu.VMEM((2, 8, N), F32),
            pltpu.SemaphoreType.DMA((8,)),
        ],
        compiler_params=params(16),
        cost_estimate=sizes(2**24),
        name="gather",
    )(
        rank,
        kept(input_proj),
        kept(value_proj),
        kept(output_proj),
        kept(grad_out),
        kept(half_sections),
        kept(turn_out),
        kept(filter_spectrum),
    )
    other_rows = lax.ppermute(filter_rows, "ctx", mirror_of)
    turned, filter_row = pl.pallas_call(
        section_kernel,
        out_shape=[pltpu.HBM((2, RANKS, ROWS, 128), BF), pltpu.VMEM((2, N), BF)],
        in_specs=[VMEM] * 4,
        out_specs=[HBM, VMEM],
        scratch_shapes=[
            pltpu.VMEM((2, RANKS, ROWS, 128), BF),
            pltpu.SemaphoreType.DMA((2 * BLOCKS,)),
        ],
        compiler_params=params(16),
        cost_estimate=sizes(A_COST),
        name="sections",
    )(signals, sections, turns, filter_row)
    other_row = lax.ppermute(filter_row, "ctx", special_of)
    arrived = lax.all_to_all(
        turned.reshape(2 * RANKS, ROWS, 128), ("core", "ctx"), 0, 0, tiled=True
    )

    tables = pl.pallas_call(
        table_kernel,
        out_shape=[pltpu.VMEM((WIDE, N), BF)] * 4,
        in_specs=[HBM] * 2,
        out_specs=[VMEM] * 4,
        scratch_shapes=[pltpu.SemaphoreType.DMA((4,))],
        compiler_params=params(16),
        cost_estimate=sizes(W_COST),
        name="bring_tables",
    )(other_rows, kept(half_tables))
    folded_filter = pl.pallas_call(
        filter_kernel,
        out_shape=pltpu.HBM((2, SLOTS, N), F32),
        in_specs=[SMEM, HBM, VMEM],
        out_specs=VMEM,
        scratch_shapes=[pltpu.VMEM((2, ROWS, N), F32), pltpu.SemaphoreType.DMA(())],
        compiler_params=params(16),
        cost_estimate=sizes(2**24),
        name="fold_filter",
    )(rank, kept(filter_spectrum), other_rows)

    spectra, grad_own, grad_low, grad_row, filter_near, turn_near = pl.pallas_call(
        spectrum_kernel,
        out_shape=[
            pltpu.VMEM((272, N), BF),
            pltpu.VMEM((2, SLOTS, N), F32),
            pltpu.VMEM((2 * SLOTS, N), BF),
            pltpu.VMEM((2, N), BF),
            pltpu.VMEM((2, SLOTS, N), F32),
            pltpu.VMEM((N, 128), F32),
        ],
        in_specs=[SMEM] + [VMEM] * 5 + [HBM, HBM, VMEM],
        out_specs=[VMEM] * 6,
        scratch_shapes=[
            pltpu.VMEM((544, N), BF),
            pltpu.SemaphoreType.DMA((2,)),
        ],
        compiler_params=params(20),
        cost_estimate=sizes(2**24),
        name="spectra",
    )(
        rank,
        arrived,
        *tables,
        kept(folded_filter),
        kept(turn_back),
        half_rows,
    )

    mirror_grad = lax.ppermute(grad_low, "ctx", mirror_of)
    mirror_row = lax.ppermute(grad_row, "ctx", special_of)

    unturned, grad_far = pl.pallas_call(
        inverse_kernel,
        out_shape=[
            jax.ShapeDtypeStruct((2, N, 128), BF),
            pltpu.HBM((2, SLOTS, N), F32),
        ],
        in_specs=[SMEM] + [VMEM] * 9,
        out_specs=[VMEM, HBM],
        scratch_shapes=[pltpu.VMEM((N, 256), F32), pltpu.SemaphoreType.DMA(())],
        compiler_params=params(24),
        cost_estimate=sizes(B_COST),
        name="inverse",
    )(rank, spectra, filter_near, other_row, *tables, turn_near, grad_own)
    returned = lax.all_to_all(
        unturned.reshape(2 * RANKS, ROWS, 128), ("core", "ctx"), 0, 0, tiled=True
    )

    sections_near, gates_near = pl.pallas_call(
        near_kernel,
        out_shape=[pltpu.VMEM((N, N // 2), BF), pltpu.VMEM((3, 2, ROWS, N), BF)],
        in_specs=[HBM] * 5,
        out_specs=[VMEM] * 2,
        scratch_shapes=[pltpu.SemaphoreType.DMA((4,))],
        compiler_params=params(16),
        cost_estimate=sizes(W_COST),
        name="bring_near",
    )(mirror_grad, kept(half_sections), kept(input_proj), kept(value_proj), kept(grad_out))
    most_rows, first_rows = pl.pallas_call(
        assemble_kernel,
        out_shape=[
            pltpu.HBM((1, 2, ROWS, N), F32),
            pltpu.VMEM((2, 8, N), F32),
        ],
        in_specs=[SMEM] + [VMEM] * 2,
        out_specs=[HBM, VMEM],
        scratch_shapes=[pltpu.VMEM((2, ROWS, N), F32), pltpu.SemaphoreType.DMA(())],
        compiler_params=params(16),
        cost_estimate=sizes(2**24),
        name="assemble",
    )(rank, grad_far, mirror_grad)

    grad_input, grad_value, grad_output_proj, grad_filter = pl.pallas_call(
        result_kernel,
        out_shape=[pltpu.HBM((2, ROWS, N), BF)] * 3 + [pltpu.HBM((1, 2, ROWS, N), F32)],
        in_specs=[SMEM] + [VMEM] * 3 + [HBM, VMEM, VMEM],
        out_specs=[HBM] * 4,
        input_output_aliases={4: 3},
        scratch_shapes=[
            pltpu.VMEM((512, N), BF),
            pltpu.VMEM((3, 2, ROWS, N), BF),
            pltpu.VMEM((2, 8, N), F32),
            pltpu.SemaphoreType.DMA((3 * BLOCKS + 1,)),
        ],
        compiler_params=params(20),
        cost_estimate=sizes(2 * 256 * N * N),
        name="results",
    )(rank, returned, sections_near, gates_near, most_rows, first_rows, mirror_row)
    return (grad_input, grad_value, grad_output_proj, grad_filter)


def solution(mesh):
    split = Mesh(mesh.devices.reshape(-1, 2, RANKS), ("group", "core", "ctx"))
    data = P(("group", "core"), "ctx", None)
    filt = P(("group", "core"), None, "ctx", None)
    return jax.shard_map(
        local,
        mesh=split,
        in_specs=(data, data, data, data, filt),
        out_specs=(data, data, data, filt),
        check_vma=False,
    )
```

```python
import functools

import jax
import jax.numpy as jnp
import ml_dtypes
import numpy as np
from jax import lax
from jax.experimental import pallas as pl
from jax.experimental.pallas import tpu as pltpu
from jax.sharding import Mesh
from jax.sharding import PartitionSpec as P

N = 1024
TOTAL = N * N
RANKS = 16
ROWS = 64
SLOTS = 32
SCALE = 1.0 / TOTAL
BF = jnp.bfloat16
F32 = jnp.float32
NT = (((1,), (1,)), ((), ()))
BLOCKS = 4
WIDE = N // BLOCKS
BROAD = N // 2
A_COST = 10**10
B_COST = 10**10
W_COST = 4 * 10**10


def kept_rows():
    rank = np.arange(RANKS)
    return (ROWS * rank + (rank >= RANKS // 2))[:, None] + np.arange(SLOTS)[None, :]


def dft_tables():
    index = np.arange(N, dtype=np.int64)
    phase = (index[:, None] * index[None, :] % N).astype(np.float64) * (2.0 * np.pi / N)
    return np.cos(phase), np.sin(phase)


def section_table():
    cos, sin = dft_tables()
    rows = kept_rows()
    imag = -sin[rows]
    imag[0, 0] = 1.0 - 2.0 * (np.arange(N) % 2)
    both = np.stack([cos[rows], imag])
    both = both.reshape(2, RANKS // 2, 2, SLOTS, N).transpose(1, 0, 2, 3, 4)
    return both.reshape(N, N).astype(ml_dtypes.bfloat16)


def forward_turn():
    rows = kept_rows().reshape(1, -1, 1)
    place = np.arange(N).reshape(RANKS, 1, ROWS)
    phase = (rows * place % TOTAL).astype(np.float64) * (2.0 * np.pi / TOTAL)
    return np.concatenate([np.cos(phase), np.sin(phase)], axis=2).astype(np.float32)


def inverse_turn():
    rows = kept_rows().reshape(RANKS, 1, SLOTS)
    place = np.arange(N).reshape(1, N, 1)
    phase = (rows * place % TOTAL).astype(np.float64) * (2.0 * np.pi / TOTAL)
    cos, sin = np.cos(phase), np.sin(phase)
    sin[0, :, 0] = packed_turn()
    return np.concatenate([cos, cos, sin, sin], axis=2).astype(np.float32)


def half_turn():
    phase = np.arange(N) * (np.pi / N)
    return np.cos(phase), np.sin(phase)


def packed_turn():
    cos, sin = half_turn()
    middle = np.abs(np.arange(N) - N // 2 + 0.5) < N // 4
    return np.where(middle, -1.0 / np.where(middle, sin, 1.0), 1.0 / np.where(middle, 1.0, cos))


def lanes_of(shape):
    return lax.broadcasted_iota(jnp.int32, shape, len(shape) - 1)


def rows_of(shape):
    return lax.broadcasted_iota(jnp.int32, shape, len(shape) - 2)


def swap_halves(value):
    half = value.shape[-1] // 2
    return jnp.concatenate([value[..., half:], value[..., :half]], axis=-1)


def split_turn(packed):
    swapped = swap_halves(packed)
    low = lanes_of(packed.shape) < packed.shape[-1] // 2
    return jnp.where(low, packed, swapped), jnp.where(low, swapped, packed)


def start_all(copies):
    for copy in copies:
        copy.start()


def gather_kernel(
    rank, inp, val, outp, grad, table, turn, filt,
    rows, row, signals, sections, turns, gates, lines, first, sems
):
    line_copy = pltpu.make_async_copy(filt.at[0, :, pl.ds(SLOTS, SLOTS)], lines, sems.at[0])
    row_copy = pltpu.make_async_copy(filt.at[0, :, pl.ds(0, 8)], first, sems.at[1])
    gate_copies = [
        pltpu.make_async_copy(source, gates.at[which], sems.at[2 + which])
        for which, source in enumerate((inp, val, outp, grad))
    ]
    table_copy = pltpu.make_async_copy(table, sections, sems.at[6])
    turn_copy = pltpu.make_async_copy(turn.at[rank[0]], turns, sems.at[7])
    start_all([line_copy] + gate_copies + [table_copy, turn_copy, row_copy])
    middle = N // 2
    line_copy.wait()
    for part in range(2):
        rows[SLOTS * part : SLOTS * part + SLOTS, :] = lines[part].astype(BF)
    for copy in gate_copies:
        copy.wait()
    for chan in range(2):
        gated = gates[0, chan].astype(F32) * gates[1, chan].astype(F32)
        conv = gates[3, chan].astype(F32) * gates[2, chan].astype(F32)
        for part in range(2):
            base = 256 * part + 128 * chan
            lanes = slice(middle * part, middle * part + middle)
            signals[base : base + 64, :] = gated[:, lanes].astype(BF)
            signals[base + 64 : base + 128, :] = conv[:, lanes].astype(BF)
    row_copy.wait()
    row[...] = jnp.concatenate([first[0, 0:1], first[1, 0:1]], axis=0).astype(BF)
    table_copy.wait()
    turn_copy.wait()


def section_kernel(signals, sections, turns, row, out, row_out, ready, sems):
    row_out[...] = row[...]
    out_copies = []
    for block in range(BLOCKS):
        rows = slice(WIDE * block, WIDE * block + WIDE)
        halves = lax.dot_general(
            sections[rows, :], signals[...], NT, preferred_element_type=F32
        )
        odd_rows = (rows_of((WIDE, 1)) + (block >= BLOCKS // 2)) % 2
        section = halves[:, :256] + (1 - 2 * odd_rows).astype(F32) * halves[:, 256:]
        for pair in range(2):
            base = WIDE // 2 * block + 64 * pair
            cos, sin = split_turn(turns[base : base + 64, :])
            for chan in range(2):
                lanes = slice(128 * chan, 128 * chan + 128)
                real = section[128 * pair : 128 * pair + 64, lanes]
                imag = section[128 * pair + 64 : 128 * pair + 128, lanes]
                turned_re = (real * cos + imag * sin).astype(BF)
                turned_im = (imag * cos - real * sin).astype(BF)
                for odd in range(2):
                    some = slice(32 * odd, 32 * odd + 32)
                    peer = 4 * block + 2 * pair + odd
                    ready[chan, peer, 0:32, :] = turned_re[some]
                    ready[chan, peer, 32:64, :] = turned_im[some]
        peers = pl.ds(4 * block, 4)
        for chan in range(2):
            copy = pltpu.make_async_copy(
                ready.at[chan, peers], out.at[chan, peers], sems.at[2 * block + chan]
            )
            copy.start()
            out_copies.append(copy)
    for copy in out_copies:
        copy.wait()


def reverse_lanes(value):
    shape = (128, 128)
    flip = jnp.where(rows_of(shape) + lanes_of(shape) == 127, 1.0, 0.0).astype(BF)
    value = value.astype(BF)
    parts = [
        jnp.dot(value[:, 128 * part : 128 * part + 128], flip, preferred_element_type=F32)
        for part in reversed(range(N // 128))
    ]
    return jnp.concatenate(parts, axis=1)


def table_kernel(after, *refs):
    copies = [
        pltpu.make_async_copy(refs[0].at[which], refs[1 + which], refs[-1].at[which])
        for which in range(4)
    ]
    start_all(copies)
    for copy in copies:
        copy.wait()


def near_kernel(after, table, first, second, third, table_out, stack, sems):
    copies = [pltpu.make_async_copy(table, table_out, sems.at[0])] + [
        pltpu.make_async_copy(source, stack.at[which], sems.at[1 + which])
        for which, source in enumerate((first, second, third))
    ]
    start_all(copies)
    for copy in copies:
        copy.wait()


def filter_kernel(rank, own, other, out, mine, sem):
    me = rank[0]
    copy = pltpu.make_async_copy(own.at[0], mine, sem)
    copy.start()
    low = me < RANKS // 2
    shape = (SLOTS, SLOTS)
    wanted = jnp.where(low, 32, 31)
    pick = jnp.where(rows_of(shape) + lanes_of(shape) == wanted, 1.0, 0.0).astype(BF)
    top = rows_of((SLOTS, N)) == 0
    copy.wait()
    for part in range(2):
        sign = 1.0 if part == 0 else -1.0
        kept = jnp.where(low, mine[part, 0:32, :], mine[part, 1:33, :])
        moved = jnp.dot(pick, other[32 * part : 32 * part + 32], preferred_element_type=F32)
        mirror = reverse_lanes(moved)
        first = mine[part, 0:8, :]
        flipped = reverse_lanes(jnp.concatenate([first, first], axis=0))
        head = jnp.where(me == 0, pltpu.roll(flipped[0:8], 1, 1)[0:1], 0.0)
        mirror = jnp.where(jnp.logical_and(top, low), head, mirror)
        out[part] = 0.5 * (kept + sign * mirror)


def special_rows(special):
    rows = [jnp.broadcast_to(special[part : part + 1, :], (8, N)) for part in range(2)]
    both = jnp.concatenate(rows, axis=0)
    return both.astype(F32), reverse_lanes(both)


def alternating(shape):
    return 1 - 2 * (lanes_of(shape) % 2)


def spectrum_kernel(
    rank, turned, cos_0, cos_1, sin_0, sin_1, filt_far, turn_far, half,
    spec, grad, grad_low, grad_row, filt, turn, left, sems
):
    me = rank[0]
    middle = N // 2
    copies = [
        pltpu.make_async_copy(filt_far, filt, sems.at[0]),
        pltpu.make_async_copy(turn_far.at[me], turn, sems.at[1]),
    ]
    start_all(copies)
    for seq in range(2):
        for pair in range(RANKS // 2):
            even = turned[RANKS * seq + 2 * pair]
            odd = turned[RANKS * seq + 2 * pair + 1]
            here = slice(128 * (pair % 4), 128 * (pair % 4) + 128)
            there = slice(middle + 128 * (pair % 4), middle + 128 * (pair % 4) + 128)
            for sig in range(2):
                lanes = slice(64 * sig, 64 * sig + 64)
                both = jnp.concatenate([even[:, lanes], odd[:, lanes]], axis=1)
                base = 272 * (pair // 4) + 32 * (2 * seq + sig)
                left[base : base + 32, here] = both[0:32]
                left[base : base + 32, there] = both[32:64]
                left[128 + base : 160 + base, here] = both[32:64]
                left[128 + base : 160 + base, there] = -both[0:32]
    packed = jnp.logical_and(rows_of((16, middle)) == 0, me == 0)
    for part in range(2):
        heads = []
        for which in range(4):
            base = 272 * part + 32 * which
            block = left[base : base + 16, middle:].astype(F32)
            heads.append(block[0:1])
            cleared = jnp.where(packed, 0.0, block).astype(BF)
            left[base : base + 16, middle:] = cleared
            left[128 + base : 144 + base, :middle] = cleared
        head = jnp.concatenate(heads + heads, axis=0)
        places = slice(middle * part, middle * part + middle)
        real = head * half[0:1, places]
        imag = -head * half[1:2, places]
        lines = slice(272 * part + 256, 272 * part + 272)
        left[lines, :middle] = jnp.concatenate([real, imag], axis=0).astype(BF)
        left[lines, middle:] = jnp.concatenate([imag, -real], axis=0).astype(BF)

    sign = alternating((1, BROAD)).astype(F32)
    for block in range(N // BROAD):
        wide = slice(BROAD * block, BROAD * block + BROAD)
        pieces = [table[:, wide] for table in (cos_0, cos_1, sin_0, sin_1)]
        halves = jnp.dot(
            left[...], jnp.concatenate(pieces, axis=0), preferred_element_type=F32
        )
        result = halves[:272] + sign * halves[272:]
        spec[:, wide] = result.astype(BF)
        real = 0.0
        imag = 0.0
        row_re = 0.0
        row_im = 0.0
        for seq in range(2):
            base = 64 * seq
            u_re, u_im = result[base : base + 32], result[base + 128 : base + 160]
            d_re, d_im = result[base + 32 : base + 64], result[base + 160 : base + 192]
            real = real + (u_re * d_re + u_im * d_im)
            imag = imag + (u_re * d_im - u_im * d_re)
            base = 256 + 2 * seq
            u_re, u_im = result[base : base + 1], result[base + 8 : base + 9]
            d_re, d_im = result[base + 1 : base + 2], result[base + 9 : base + 10]
            row_re = row_re + (u_re * d_re + u_im * d_im)
            row_im = row_im + (u_re * d_im - u_im * d_re)
        real = real * SCALE
        imag = imag * SCALE
        grad[0, :, wide] = real
        grad[1, :, wide] = imag
        grad_low[0:32, wide] = real.astype(BF)
        grad_low[32:64, wide] = imag.astype(BF)
        row_re = jnp.where(me == 0, row_re * SCALE, real[0:1])
        row_im = jnp.where(me == 0, row_im * SCALE, imag[0:1])
        grad_row[:, wide] = jnp.concatenate([row_re, row_im], axis=0).astype(BF)
    for copy in copies:
        copy.wait()


def products(u_re, u_im, d_re, d_im, h_re, h_im):
    return (
        u_re * h_re - u_im * h_im,
        u_re * h_im + u_im * h_re,
        h_re * d_re + h_im * d_im,
        h_re * d_im - h_im * d_re,
    )


def inverse_kernel(
    rank, spec, filt, special, cos_0, cos_1, sin_0, sin_1, turn, grad, out, grad_far, total, sem
):
    me = rank[0]
    copy = pltpu.make_async_copy(grad, grad_far, sem)
    copy.start()
    outer, inner = (0, 3), (1, 2)
    sign = alternating((1, BROAD)).astype(BF)
    top = rows_of((SLOTS, BROAD)) == 0
    packed_row = jnp.logical_and(top, me == 0)
    lone, flipped = special_rows(special)
    lone_re, lone_im = 0.5 * lone[0:1], 0.5 * lone[8:9]
    flip_re, flip_im = 0.5 * flipped[0:1], -0.5 * flipped[8:9]
    patched_row = jnp.logical_and(top, jnp.logical_and(me > 0, me < RANKS // 2))
    for block in range(N // BROAD):
        wide = slice(BROAD * block, BROAD * block + BROAD)
        values = spec[:, wide].astype(F32)
        h_re = filt[0, :, wide] + jnp.where(patched_row, flip_re[:, wide], 0.0)
        h_im = filt[1, :, wide] + jnp.where(patched_row, flip_im[:, wide], 0.0)
        x_re, x_im = (lone_re + flip_re)[:, wide], (lone_im + flip_im)[:, wide]
        reals, imags, extra_re, extra_im = [], [], [], []
        for seq in range(2):
            base = 64 * seq
            p_re, p_im, q_re, q_im = products(
                values[base : base + 32],
                values[base + 128 : base + 160],
                values[base + 32 : base + 64],
                values[base + 160 : base + 192],
                h_re,
                h_im,
            )
            reals += [p_re, q_re]
            imags += [p_im, q_im]
            base = 256 + 2 * seq
            p_re, p_im, q_re, q_im = products(
                values[base : base + 1],
                values[base + 8 : base + 9],
                values[base + 1 : base + 2],
                values[base + 9 : base + 10],
                x_re,
                x_im,
            )
            extra_re += [p_re, q_re]
            extra_im += [p_im, q_im]

        def mixed(plain, extra, sign):
            return [jnp.where(packed_row, sign * e, p) for p, e in zip(plain, extra)]

        def joined(first, second):
            return jnp.concatenate(first + second, axis=0).astype(BF)

        less = [-value for value in imags]
        for parts, extra, crossed in (
            (outer, extra_re, mixed(reals, extra_im, -1.0)),
            (inner, extra_im, mixed(reals, extra_re, 1.0)),
        ):
            straight = joined(reals, mixed(imags, extra, 1.0))
            crossing = joined(less, crossed)
            for quarter in parts:
                rows = slice(WIDE * quarter, WIDE * quarter + WIDE)
                cos = (cos_0, cos_1)[quarter % 2][:, wide]
                sin = (sin_0, sin_1)[quarter % 2][:, wide]
                if quarter >= 2:
                    cos, sin = cos * sign, sin * sign
                part = lax.dot_general(
                    cos, straight, NT, preferred_element_type=F32
                ) + lax.dot_general(sin, crossing, NT, preferred_element_type=F32)
                if block == 0:
                    total[rows, :] = part
                else:
                    total[rows, :] += part

    for piece in range(BLOCKS):
        rows = slice(WIDE * piece, WIDE * piece + WIDE)
        turn_cos, turn_sin = split_turn(turn[rows, :])
        real = total[rows, :128]
        imag = total[rows, 128:]
        un_re = real * turn_cos - imag * turn_sin
        un_im = real * turn_sin + imag * turn_cos
        packed = jnp.logical_and(lanes_of((WIDE, 128)) % SLOTS == 0, me == 0)
        un_im = jnp.where(packed, imag * turn_sin, 2.0 * un_im).astype(BF)
        un_re = jnp.where(packed, real, 2.0 * un_re).astype(BF)
        out[0, rows, :] = jnp.concatenate([un_re[:, :64], un_im[:, :64]], axis=1)
        out[1, rows, :] = jnp.concatenate([un_re[:, 64:], un_im[:, 64:]], axis=1)
    copy.wait()


def result_kernel(
    rank, arrived, table, gates, most, first, special,
    d_inp, d_val, d_outp, d_filt, left, ready, patch, sems
):
    me = rank[0]
    lone, flipped = special_rows(special)
    top = jnp.logical_and(rows_of((8, N)) == 0, me >= RANKS // 2)
    for part in range(2):
        lines = slice(8 * part, 8 * part + 8)
        sign = 1.0 if part == 0 else -1.0
        head = jnp.where(me == RANKS // 2, lone[lines], sign * flipped[lines])
        patch[part] = jnp.where(top, head, first[part])
    patch_copy = pltpu.make_async_copy(
        patch, d_filt.at[0, :, pl.ds(0, 8)], sems.at[3 * BLOCKS]
    )
    patch_copy.start()
    half = N // 2
    for chan in range(2):
        for pair in range(RANKS // 2):
            even = arrived[RANKS * chan + 2 * pair]
            odd = arrived[RANKS * chan + 2 * pair + 1]
            sign = alternating((1, 128)) * (1 if pair < RANKS // 4 else -1)
            for sig in range(2):
                low = slice(32 * sig, 32 * sig + 32)
                high = slice(64 + 32 * sig, 96 + 32 * sig)
                base = 64 * (2 * chan + sig)
                lanes = slice(128 * pair, 128 * pair + 128)
                block = jnp.concatenate(
                    [even[:, low], odd[:, low], even[:, high], odd[:, high]], axis=1
                )
                left[base : base + 64, lanes] = block
                left[256 + base : 320 + base, lanes] = block * sign.astype(BF)
    copies = []
    for block in range(BLOCKS // 2):
        near = slice(WIDE * block, WIDE * block + WIDE)
        halves = jnp.dot(left[...], table[:, near], preferred_element_type=F32) * SCALE
        for part in range(2):
            start = half * part + WIDE * block
            wide = slice(start, start + WIDE)
            result = halves[256 * part : 256 * part + 256]
            for chan in range(2):
                conv = result[128 * chan : 128 * chan + 64]
                gated = result[128 * chan + 64 : 128 * chan + 128]
                out_grad = gates[2, chan, :, wide].astype(F32) * conv
                ready[2, chan, :, wide] = out_grad.astype(BF)
                in_grad = gated * gates[1, chan, :, wide].astype(F32)
                ready[0, chan, :, wide] = in_grad.astype(BF)
                val_grad = gated * gates[0, chan, :, wide].astype(F32)
                ready[1, chan, :, wide] = val_grad.astype(BF)
            for which, target in enumerate((d_inp, d_val, d_outp)):
                copy = pltpu.make_async_copy(
                    ready.at[which, :, :, pl.ds(start, WIDE)],
                    target.at[:, :, pl.ds(start, WIDE)],
                    sems.at[3 * (2 * block + part) + which],
                )
                copy.start()
                copies.append(copy)
    for copy in copies:
        copy.wait()
    patch_copy.wait()


def assemble_kernel(rank, own, other, out, first, ready, sem):
    me = rank[0]
    low = me < RANKS // 2
    shape = (SLOTS, SLOTS)
    wanted = jnp.where(low, 31, 32)
    pick = jnp.where(rows_of(shape) + lanes_of(shape) == wanted, 1.0, 0.0).astype(BF)
    top = rows_of((SLOTS, N)) == 0
    for part in range(2):
        sign = 1.0 if part == 0 else -1.0
        mine = own[part]
        shifted = pltpu.roll(mine, 1, 0)
        moved = jnp.dot(pick, other[32 * part : 32 * part + 32], preferred_element_type=F32)
        mirror = sign * reverse_lanes(moved)
        lines = jnp.where(low, mine, shifted)
        first[part] = lines[0:8]
        ready[part, 0:32, :] = lines
        ready[part, 32:64, :] = jnp.where(jnp.logical_and(top, ~low), shifted, mirror)
    copy = pltpu.make_async_copy(
        ready.at[:, pl.ds(8, ROWS - 8)], out.at[0, :, pl.ds(8, ROWS - 8)], sem
    )
    copy.start()
    copy.wait()


HBM = pl.BlockSpec(memory_space=pltpu.HBM)
VMEM = pl.BlockSpec(memory_space=pltpu.VMEM)
SMEM = pl.BlockSpec(memory_space=pltpu.SMEM)


def kept(value):
    return pltpu.with_memory_space_constraint(value, pltpu.HBM)


def sizes(flops, count=2**20):
    return pl.CostEstimate(flops=flops, bytes_accessed=count, transcendentals=0)


def params(mib):
    return pltpu.CompilerParams(vmem_limit_bytes=mib * 2**20)


def local(input_proj, value_proj, output_proj, grad_out, filter_spectrum):
    cos64, sin64 = dft_tables()
    half_tables = np.concatenate([cos64[: N // 2], sin64[: N // 2]]).reshape(4, WIDE, N)
    half_tables = jnp.asarray(half_tables.astype(ml_dtypes.bfloat16))
    half_sections = jnp.asarray(section_table()[:, : N // 2])
    turn_out = jnp.asarray(forward_turn())
    turn_back = jnp.asarray(inverse_turn())
    half_rows = jnp.asarray(np.stack(half_turn()).astype(np.float32))
    ctx_rank = lax.axis_index("ctx")
    rank = ctx_rank.astype(jnp.int32).reshape(1)
    half_ranks = RANKS // 2
    mirror_of = [(r, RANKS - 1 - r) for r in range(RANKS)]
    special_of = [(r, RANKS - r) for r in range(1, RANKS) if r != half_ranks]
    special_of += [(0, half_ranks), (half_ranks, 0)]

    filter_rows, filter_row, signals, sections, turns = pl.pallas_call(
        gather_kernel,
        out_shape=[
            pltpu.VMEM((2 * SLOTS, N), BF),
            pltpu.VMEM((2, N), BF),
            pltpu.VMEM((512, N // 2), BF),
            pltpu.VMEM((N, N // 2), BF),
            pltpu.VMEM((N // 2, 128), F32),
        ],
        in_specs=[SMEM] + [HBM] * 7,
        out_specs=[VMEM] * 5,
        scratch_shapes=[
            pltpu.VMEM((4, 2, ROWS, N), BF),
            pltpu.VMEM((2, SLOTS, N), F32),
            pltpu.VMEM((2, 8, N), F32),
            pltpu.SemaphoreType.DMA((8,)),
        ],
        compiler_params=params(16),
        cost_estimate=sizes(2**24),
        name="gather",
    )(
        rank,
        kept(input_proj),
        kept(value_proj),
        kept(output_proj),
        kept(grad_out),
        kept(half_sections),
        kept(turn_out),
        kept(filter_spectrum),
    )
    other_rows = lax.ppermute(filter_rows, "ctx", mirror_of)
    turned, filter_row = pl.pallas_call(
        section_kernel,
        out_shape=[pltpu.HBM((2, RANKS, ROWS, 128), BF), pltpu.VMEM((2, N), BF)],
        in_specs=[VMEM] * 4,
        out_specs=[HBM, VMEM],
        scratch_shapes=[
            pltpu.VMEM((2, RANKS, ROWS, 128), BF),
            pltpu.SemaphoreType.DMA((2 * BLOCKS,)),
        ],
        compiler_params=params(16),
        cost_estimate=sizes(A_COST),
        name="sections",
    )(signals, sections, turns, filter_row)
    other_row = lax.ppermute(filter_row, "ctx", special_of)
    arrived = lax.all_to_all(
        turned.reshape(2 * RANKS, ROWS, 128), ("core", "ctx"), 0, 0, tiled=True
    )

    tables = pl.pallas_call(
        table_kernel,
        out_shape=[pltpu.VMEM((WIDE, N), BF)] * 4,
        in_specs=[HBM] * 2,
        out_specs=[VMEM] * 4,
        scratch_shapes=[pltpu.SemaphoreType.DMA((4,))],
        compiler_params=params(16),
        cost_estimate=sizes(W_COST),
        name="bring_tables",
    )(other_rows, kept(half_tables))
    folded_filter = pl.pallas_call(
        filter_kernel,
        out_shape=pltpu.HBM((2, SLOTS, N), F32),
        in_specs=[SMEM, HBM, VMEM],
        out_specs=VMEM,
        scratch_shapes=[pltpu.VMEM((2, ROWS, N), F32), pltpu.SemaphoreType.DMA(())],
        compiler_params=params(16),
        cost_estimate=sizes(2**24),
        name="fold_filter",
    )(rank, kept(filter_spectrum), other_rows)

    spectra, grad_own, grad_low, grad_row, filter_near, turn_near = pl.pallas_call(
        spectrum_kernel,
        out_shape=[
            pltpu.VMEM((272, N), BF),
            pltpu.VMEM((2, SLOTS, N), F32),
            pltpu.VMEM((2 * SLOTS, N), BF),
            pltpu.VMEM((2, N), BF),
            pltpu.VMEM((2, SLOTS, N), F32),
            pltpu.VMEM((N, 128), F32),
        ],
        in_specs=[SMEM] + [VMEM] * 5 + [HBM, HBM, VMEM],
        out_specs=[VMEM] * 6,
        scratch_shapes=[
            pltpu.VMEM((544, N), BF),
            pltpu.SemaphoreType.DMA((2,)),
        ],
        compiler_params=params(20),
        cost_estimate=sizes(2**24),
        name="spectra",
    )(
        rank,
        arrived,
        *tables,
        kept(folded_filter),
        kept(turn_back),
        half_rows,
    )

    mirror_grad = lax.ppermute(grad_low, "ctx", mirror_of)
    mirror_row = lax.ppermute(grad_row, "ctx", special_of)

    unturned, grad_far = pl.pallas_call(
        inverse_kernel,
        out_shape=[
            jax.ShapeDtypeStruct((2, N, 128), BF),
            pltpu.HBM((2, SLOTS, N), F32),
        ],
        in_specs=[SMEM] + [VMEM] * 9,
        out_specs=[VMEM, HBM],
        scratch_shapes=[pltpu.VMEM((N, 256), F32), pltpu.SemaphoreType.DMA(())],
        compiler_params=params(24),
        cost_estimate=sizes(B_COST),
        name="inverse",
    )(rank, spectra, filter_near, other_row, *tables, turn_near, grad_own)
    returned = lax.all_to_all(
        unturned.reshape(2 * RANKS, ROWS, 128), ("core", "ctx"), 0, 0, tiled=True
    )

    sections_near, gates_near = pl.pallas_call(
        near_kernel,
        out_shape=[pltpu.VMEM((N, N // 2), BF), pltpu.VMEM((3, 2, ROWS, N), BF)],
        in_specs=[HBM] * 5,
        out_specs=[VMEM] * 2,
        scratch_shapes=[pltpu.SemaphoreType.DMA((4,))],
        compiler_params=params(16),
        cost_estimate=sizes(W_COST),
        name="bring_near",
    )(mirror_grad, kept(half_sections), kept(input_proj), kept(value_proj), kept(grad_out))
    most_rows, first_rows = pl.pallas_call(
        assemble_kernel,
        out_shape=[
            pltpu.HBM((1, 2, ROWS, N), F32),
            pltpu.VMEM((2, 8, N), F32),
        ],
        in_specs=[SMEM] + [VMEM] * 2,
        out_specs=[HBM, VMEM],
        scratch_shapes=[pltpu.VMEM((2, ROWS, N), F32), pltpu.SemaphoreType.DMA(())],
        compiler_params=params(16),
        cost_estimate=sizes(2**24),
        name="assemble",
    )(rank, grad_far, mirror_grad)

    grad_input, grad_value, grad_output_proj, grad_filter = pl.pallas_call(
        result_kernel,
        out_shape=[pltpu.HBM((2, ROWS, N), BF)] * 3 + [pltpu.HBM((1, 2, ROWS, N), F32)],
        in_specs=[SMEM] + [VMEM] * 3 + [HBM, VMEM, VMEM],
        out_specs=[HBM] * 4,
        input_output_aliases={4: 3},
        scratch_shapes=[
            pltpu.VMEM((512, N), BF),
            pltpu.VMEM((3, 2, ROWS, N), BF),
            pltpu.VMEM((2, 8, N), F32),
            pltpu.SemaphoreType.DMA((3 * BLOCKS + 1,)),
        ],
        compiler_params=params(20),
        cost_estimate=sizes(2 * 256 * N * N),
        name="results",
    )(rank, returned, sections_near, gates_near, most_rows, first_rows, mirror_row)
    return (grad_input, grad_value, grad_output_proj, grad_filter)


def solution(mesh):
    split = Mesh(mesh.devices.reshape(-1, 2, RANKS), ("group", "core", "ctx"))
    data = P(("group", "core"), "ctx", None)
    filt = P(("group", "core"), None, "ctx", None)
    return jax.shard_map(
        local,
        mesh=split,
        in_specs=(data, data, data, data, filt),
        out_specs=(data, data, data, filt),
        check_vma=False,
    )
```

```python
import functools

import jax
import jax.numpy as jnp
import ml_dtypes
import numpy as np
from jax import lax
from jax.experimental import pallas as pl
from jax.experimental.pallas import tpu as pltpu
from jax.sharding import Mesh
from jax.sharding import PartitionSpec as P

N = 1024
TOTAL = N * N
RANKS = 16
ROWS = 64
SLOTS = 32
SCALE = 1.0 / TOTAL
BF = jnp.bfloat16
F32 = jnp.float32
NT = (((1,), (1,)), ((), ()))
BLOCKS = 4
WIDE = N // BLOCKS
BROAD = N // 2
A_COST = 10**10
B_COST = 10**10
W_COST = 4 * 10**10


def kept_rows():
    rank = np.arange(RANKS)
    return (ROWS * rank + (rank >= RANKS // 2))[:, None] + np.arange(SLOTS)[None, :]


def dft_tables():
    index = np.arange(N, dtype=np.int64)
    phase = (index[:, None] * index[None, :] % N).astype(np.float64) * (2.0 * np.pi / N)
    return np.cos(phase), np.sin(phase)


def section_table():
    cos, sin = dft_tables()
    rows = kept_rows()
    imag = -sin[rows]
    imag[0, 0] = 1.0 - 2.0 * (np.arange(N) % 2)
    both = np.stack([cos[rows], imag])
    both = both.reshape(2, RANKS // 2, 2, SLOTS, N).transpose(1, 0, 2, 3, 4)
    return both.reshape(N, N).astype(ml_dtypes.bfloat16)


def forward_turn():
    rows = kept_rows().reshape(1, -1, 1)
    place = np.arange(N).reshape(RANKS, 1, ROWS)
    phase = (rows * place % TOTAL).astype(np.float64) * (2.0 * np.pi / TOTAL)
    return np.concatenate([np.cos(phase), np.sin(phase)], axis=2).astype(np.float32)


def inverse_turn():
    rows = kept_rows().reshape(RANKS, 1, SLOTS)
    place = np.arange(N).reshape(1, N, 1)
    phase = (rows * place % TOTAL).astype(np.float64) * (2.0 * np.pi / TOTAL)
    cos, sin = np.cos(phase), np.sin(phase)
    sin[0, :, 0] = packed_turn()
    return np.concatenate([cos, cos, sin, sin], axis=2).astype(np.float32)


def half_turn():
    phase = np.arange(N) * (np.pi / N)
    return np.cos(phase), np.sin(phase)


def packed_turn():
    cos, sin = half_turn()
    middle = np.abs(np.arange(N) - N // 2 + 0.5) < N // 4
    return np.where(middle, -1.0 / np.where(middle, sin, 1.0), 1.0 / np.where(middle, 1.0, cos))


def lanes_of(shape):
    return lax.broadcasted_iota(jnp.int32, shape, len(shape) - 1)


def rows_of(shape):
    return lax.broadcasted_iota(jnp.int32, shape, len(shape) - 2)


def swap_halves(value):
    half = value.shape[-1] // 2
    return jnp.concatenate([value[..., half:], value[..., :half]], axis=-1)


def split_turn(packed):
    swapped = swap_halves(packed)
    low = lanes_of(packed.shape) < packed.shape[-1] // 2
    return jnp.where(low, packed, swapped), jnp.where(low, swapped, packed)


def start_all(copies):
    for copy in copies:
        copy.start()


def gather_kernel(
    rank, inp, val, outp, grad, table, turn, filt,
    rows, row, signals, sections, turns, gates, lines, first, sems
):
    line_copy = pltpu.make_async_copy(filt.at[0, :, pl.ds(SLOTS, SLOTS)], lines, sems.at[0])
    row_copy = pltpu.make_async_copy(filt.at[0, :, pl.ds(0, 8)], first, sems.at[1])
    gate_copies = [
        pltpu.make_async_copy(source, gates.at[which], sems.at[2 + which])
        for which, source in enumerate((inp, val, outp, grad))
    ]
    table_copy = pltpu.make_async_copy(table, sections, sems.at[6])
    turn_copy = pltpu.make_async_copy(turn.at[rank[0]], turns, sems.at[7])
    start_all([line_copy] + gate_copies + [table_copy, turn_copy, row_copy])
    middle = N // 2
    line_copy.wait()
    for part in range(2):
        rows[SLOTS * part : SLOTS * part + SLOTS, :] = lines[part].astype(BF)
    for copy in gate_copies:
        copy.wait()
    for chan in range(2):
        gated = gates[0, chan].astype(F32) * gates[1, chan].astype(F32)
        conv = gates[3, chan].astype(F32) * gates[2, chan].astype(F32)
        for part in range(2):
            base = 256 * part + 128 * chan
            lanes = slice(middle * part, middle * part + middle)
            signals[base : base + 64, :] = gated[:, lanes].astype(BF)
            signals[base + 64 : base + 128, :] = conv[:, lanes].astype(BF)
    row_copy.wait()
    row[...] = jnp.concatenate([first[0, 0:1], first[1, 0:1]], axis=0).astype(BF)
    table_copy.wait()
    turn_copy.wait()


def section_kernel(signals, sections, turns, row, out, row_out, ready, sems):
    row_out[...] = row[...]
    out_copies = []
    for block in range(BLOCKS):
        rows = slice(WIDE * block, WIDE * block + WIDE)
        halves = lax.dot_general(
            sections[rows, :], signals[...], NT, preferred_element_type=F32
        )
        odd_rows = (rows_of((WIDE, 1)) + (block >= BLOCKS // 2)) % 2
        section = halves[:, :256] + (1 - 2 * odd_rows).astype(F32) * halves[:, 256:]
        for pair in range(2):
            base = WIDE // 2 * block + 64 * pair
            cos, sin = split_turn(turns[base : base + 64, :])
            for chan in range(2):
                lanes = slice(128 * chan, 128 * chan + 128)
                real = section[128 * pair : 128 * pair + 64, lanes]
                imag = section[128 * pair + 64 : 128 * pair + 128, lanes]
                turned_re = (real * cos + imag * sin).astype(BF)
                turned_im = (imag * cos - real * sin).astype(BF)
                for odd in range(2):
                    some = slice(32 * odd, 32 * odd + 32)
                    peer = 4 * block + 2 * pair + odd
                    ready[chan, peer, 0:32, :] = turned_re[some]
                    ready[chan, peer, 32:64, :] = turned_im[some]
        peers = pl.ds(4 * block, 4)
        for chan in range(2):
            copy = pltpu.make_async_copy(
                ready.at[chan, peers], out.at[chan, peers], sems.at[2 * block + chan]
            )
            copy.start()
            out_copies.append(copy)
    for copy in out_copies:
        copy.wait()


def reverse_lanes(value):
    shape = (128, 128)
    flip = jnp.where(rows_of(shape) + lanes_of(shape) == 127, 1.0, 0.0).astype(BF)
    value = value.astype(BF)
    parts = [
        jnp.dot(value[:, 128 * part : 128 * part + 128], flip, preferred_element_type=F32)
        for part in reversed(range(N // 128))
    ]
    return jnp.concatenate(parts, axis=1)


def table_kernel(after, *refs):
    copies = [
        pltpu.make_async_copy(refs[0].at[which], refs[1 + which], refs[-1].at[which])
        for which in range(4)
    ]
    start_all(copies)
    for copy in copies:
        copy.wait()


def near_kernel(after, table, first, second, third, table_out, stack, sems):
    copies = [pltpu.make_async_copy(table, table_out, sems.at[0])] + [
        pltpu.make_async_copy(source, stack.at[which], sems.at[1 + which])
        for which, source in enumerate((first, second, third))
    ]
    start_all(copies)
    for copy in copies:
        copy.wait()


def filter_kernel(rank, own, other, out, mine, sem):
    me = rank[0]
    copy = pltpu.make_async_copy(own.at[0], mine, sem)
    copy.start()
    low = me < RANKS // 2
    shape = (SLOTS, SLOTS)
    wanted = jnp.where(low, 32, 31)
    pick = jnp.where(rows_of(shape) + lanes_of(shape) == wanted, 1.0, 0.0).astype(BF)
    top = rows_of((SLOTS, N)) == 0
    copy.wait()
    for part in range(2):
        sign = 1.0 if part == 0 else -1.0
        kept = jnp.where(low, mine[part, 0:32, :], mine[part, 1:33, :])
        moved = jnp.dot(pick, other[32 * part : 32 * part + 32], preferred_element_type=F32)
        mirror = reverse_lanes(moved)
        first = mine[part, 0:8, :]
        flipped = reverse_lanes(jnp.concatenate([first, first], axis=0))
        head = jnp.where(me == 0, pltpu.roll(flipped[0:8], 1, 1)[0:1], 0.0)
        mirror = jnp.where(jnp.logical_and(top, low), head, mirror)
        out[part] = 0.5 * (kept + sign * mirror)


def special_rows(special):
    rows = [jnp.broadcast_to(special[part : part + 1, :], (8, N)) for part in range(2)]
    both = jnp.concatenate(rows, axis=0)
    return both.astype(F32), reverse_lanes(both)


def alternating(shape):
    return 1 - 2 * (lanes_of(shape) % 2)


def spectrum_kernel(
    rank, turned, cos_0, cos_1, sin_0, sin_1, filt_far, turn_far, half,
    spec, grad, grad_low, grad_row, filt, turn, left, sems
):
    me = rank[0]
    middle = N // 2
    copies = [
        pltpu.make_async_copy(filt_far, filt, sems.at[0]),
        pltpu.make_async_copy(turn_far.at[me], turn, sems.at[1]),
    ]
    start_all(copies)
    for seq in range(2):
        for pair in range(RANKS // 2):
            even = turned[RANKS * seq + 2 * pair]
            odd = turned[RANKS * seq + 2 * pair + 1]
            here = slice(128 * (pair % 4), 128 * (pair % 4) + 128)
            there = slice(middle + 128 * (pair % 4), middle + 128 * (pair % 4) + 128)
            for sig in range(2):
                lanes = slice(64 * sig, 64 * sig + 64)
                both = jnp.concatenate([even[:, lanes], odd[:, lanes]], axis=1)
                base = 272 * (pair // 4) + 32 * (2 * seq + sig)
                left[base : base + 32, here] = both[0:32]
                left[base : base + 32, there] = both[32:64]
                left[128 + base : 160 + base, here] = both[32:64]
                left[128 + base : 160 + base, there] = -both[0:32]
    packed = jnp.logical_and(rows_of((16, middle)) == 0, me == 0)
    for part in range(2):
        heads = []
        for which in range(4):
            base = 272 * part + 32 * which
            block = left[base : base + 16, middle:].astype(F32)
            heads.append(block[0:1])
            cleared = jnp.where(packed, 0.0, block).astype(BF)
            left[base : base + 16, middle:] = cleared
            left[128 + base : 144 + base, :middle] = cleared
        head = jnp.concatenate(heads + heads, axis=0)
        places = slice(middle * part, middle * part + middle)
        real = head * half[0:1, places]
        imag = -head * half[1:2, places]
        lines = slice(272 * part + 256, 272 * part + 272)
        left[lines, :middle] = jnp.concatenate([real, imag], axis=0).astype(BF)
        left[lines, middle:] = jnp.concatenate([imag, -real], axis=0).astype(BF)

    sign = alternating((1, BROAD)).astype(F32)
    for block in range(N // BROAD):
        wide = slice(BROAD * block, BROAD * block + BROAD)
        pieces = [table[:, wide] for table in (cos_0, cos_1, sin_0, sin_1)]
        halves = jnp.dot(
            left[...], jnp.concatenate(pieces, axis=0), preferred_element_type=F32
        )
        result = halves[:272] + sign * halves[272:]
        spec[:, wide] = result.astype(BF)
        real = 0.0
        imag = 0.0
        row_re = 0.0
        row_im = 0.0
        for seq in range(2):
            base = 64 * seq
            u_re, u_im = result[base : base + 32], result[base + 128 : base + 160]
            d_re, d_im = result[base + 32 : base + 64], result[base + 160 : base + 192]
            real = real + (u_re * d_re + u_im * d_im)
            imag = imag + (u_re * d_im - u_im * d_re)
            base = 256 + 2 * seq
            u_re, u_im = result[base : base + 1], result[base + 8 : base + 9]
            d_re, d_im = result[base + 1 : base + 2], result[base + 9 : base + 10]
            row_re = row_re + (u_re * d_re + u_im * d_im)
            row_im = row_im + (u_re * d_im - u_im * d_re)
        real = real * SCALE
        imag = imag * SCALE
        grad[0, :, wide] = real
        grad[1, :, wide] = imag
        grad_low[0:32, wide] = real.astype(BF)
        grad_low[32:64, wide] = imag.astype(BF)
        row_re = jnp.where(me == 0, row_re * SCALE, real[0:1])
        row_im = jnp.where(me == 0, row_im * SCALE, imag[0:1])
        grad_row[:, wide] = jnp.concatenate([row_re, row_im], axis=0).astype(BF)
    for copy in copies:
        copy.wait()


def products(u_re, u_im, d_re, d_im, h_re, h_im):
    return (
        u_re * h_re - u_im * h_im,
        u_re * h_im + u_im * h_re,
        h_re * d_re + h_im * d_im,
        h_re * d_im - h_im * d_re,
    )


def inverse_kernel(
    rank, spec, filt, special, cos_0, cos_1, sin_0, sin_1, turn, grad,
    out, grad_far, total, ready, sems
):
    me = rank[0]
    copy = pltpu.make_async_copy(grad, grad_far, sems.at[0])
    copy.start()
    out_copies = []
    outer, inner = (0, 3), (1, 2)
    sign = alternating((1, BROAD)).astype(BF)
    top = rows_of((SLOTS, BROAD)) == 0
    packed_row = jnp.logical_and(top, me == 0)
    lone, flipped = special_rows(special)
    lone_re, lone_im = 0.5 * lone[0:1], 0.5 * lone[8:9]
    flip_re, flip_im = 0.5 * flipped[0:1], -0.5 * flipped[8:9]
    patched_row = jnp.logical_and(top, jnp.logical_and(me > 0, me < RANKS // 2))
    for block in range(N // BROAD):
        wide = slice(BROAD * block, BROAD * block + BROAD)
        values = spec[:, wide].astype(F32)
        h_re = filt[0, :, wide] + jnp.where(patched_row, flip_re[:, wide], 0.0)
        h_im = filt[1, :, wide] + jnp.where(patched_row, flip_im[:, wide], 0.0)
        x_re, x_im = (lone_re + flip_re)[:, wide], (lone_im + flip_im)[:, wide]
        reals, imags, extra_re, extra_im = [], [], [], []
        for seq in range(2):
            base = 64 * seq
            p_re, p_im, q_re, q_im = products(
                values[base : base + 32],
                values[base + 128 : base + 160],
                values[base + 32 : base + 64],
                values[base + 160 : base + 192],
                h_re,
                h_im,
            )
            reals += [p_re, q_re]
            imags += [p_im, q_im]
            base = 256 + 2 * seq
            p_re, p_im, q_re, q_im = products(
                values[base : base + 1],
                values[base + 8 : base + 9],
                values[base + 1 : base + 2],
                values[base + 9 : base + 10],
                x_re,
                x_im,
            )
            extra_re += [p_re, q_re]
            extra_im += [p_im, q_im]

        def mixed(plain, extra, sign):
            return [jnp.where(packed_row, sign * e, p) for p, e in zip(plain, extra)]

        def joined(first, second):
            return jnp.concatenate(first + second, axis=0).astype(BF)

        less = [-value for value in imags]
        for parts, extra, crossed in (
            (outer, extra_re, mixed(reals, extra_im, -1.0)),
            (inner, extra_im, mixed(reals, extra_re, 1.0)),
        ):
            straight = joined(reals, mixed(imags, extra, 1.0))
            crossing = joined(less, crossed)
            for quarter in parts:
                rows = slice(WIDE * quarter, WIDE * quarter + WIDE)
                cos = (cos_0, cos_1)[quarter % 2][:, wide]
                sin = (sin_0, sin_1)[quarter % 2][:, wide]
                if quarter >= 2:
                    cos, sin = cos * sign, sin * sign
                part = lax.dot_general(
                    cos, straight, NT, preferred_element_type=F32
                ) + lax.dot_general(sin, crossing, NT, preferred_element_type=F32)
                if block == 0:
                    total[rows, :] = part
                else:
                    total[rows, :] += part

    for piece in range(BLOCKS):
        rows = slice(WIDE * piece, WIDE * piece + WIDE)
        turn_cos, turn_sin = split_turn(turn[rows, :])
        real = total[rows, :128]
        imag = total[rows, 128:]
        un_re = real * turn_cos - imag * turn_sin
        un_im = real * turn_sin + imag * turn_cos
        packed = jnp.logical_and(lanes_of((WIDE, 128)) % SLOTS == 0, me == 0)
        un_im = jnp.where(packed, imag * turn_sin, 2.0 * un_im).astype(BF)
        un_re = jnp.where(packed, real, 2.0 * un_re).astype(BF)
        ready[0, rows, :] = jnp.concatenate([un_re[:, :64], un_im[:, :64]], axis=1)
        ready[1, rows, :] = jnp.concatenate([un_re[:, 64:], un_im[:, 64:]], axis=1)
        place = pl.ds(WIDE * piece, WIDE)
        out_copies.append(
            pltpu.make_async_copy(ready.at[:, place], out.at[:, place], sems.at[1 + piece])
        )
        out_copies[-1].start()
    for out_copy in out_copies:
        out_copy.wait()
    copy.wait()


def result_kernel(
    rank, arrived, table, gates, most, first, special,
    d_inp, d_val, d_outp, d_filt, left, ready, patch, sems
):
    me = rank[0]
    lone, flipped = special_rows(special)
    top = jnp.logical_and(rows_of((8, N)) == 0, me >= RANKS // 2)
    for part in range(2):
        lines = slice(8 * part, 8 * part + 8)
        sign = 1.0 if part == 0 else -1.0
        head = jnp.where(me == RANKS // 2, lone[lines], sign * flipped[lines])
        patch[part] = jnp.where(top, head, first[part])
    patch_copy = pltpu.make_async_copy(
        patch, d_filt.at[0, :, pl.ds(0, 8)], sems.at[3 * BLOCKS]
    )
    patch_copy.start()
    half = N // 2
    for chan in range(2):
        for pair in range(RANKS // 2):
            even = arrived[RANKS * chan + 2 * pair]
            odd = arrived[RANKS * chan + 2 * pair + 1]
            sign = alternating((1, 128)) * (1 if pair < RANKS // 4 else -1)
            for sig in range(2):
                low = slice(32 * sig, 32 * sig + 32)
                high = slice(64 + 32 * sig, 96 + 32 * sig)
                base = 64 * (2 * chan + sig)
                lanes = slice(128 * pair, 128 * pair + 128)
                block = jnp.concatenate(
                    [even[:, low], odd[:, low], even[:, high], odd[:, high]], axis=1
                )
                left[base : base + 64, lanes] = block
                left[256 + base : 320 + base, lanes] = block * sign.astype(BF)
    copies = []
    for block in range(BLOCKS // 2):
        near = slice(WIDE * block, WIDE * block + WIDE)
        halves = jnp.dot(left[...], table[:, near], preferred_element_type=F32) * SCALE
        for part in range(2):
            start = half * part + WIDE * block
            wide = slice(start, start + WIDE)
            result = halves[256 * part : 256 * part + 256]
            for chan in range(2):
                conv = result[128 * chan : 128 * chan + 64]
                gated = result[128 * chan + 64 : 128 * chan + 128]
                out_grad = gates[2, chan, :, wide].astype(F32) * conv
                ready[2, chan, :, wide] = out_grad.astype(BF)
                in_grad = gated * gates[1, chan, :, wide].astype(F32)
                ready[0, chan, :, wide] = in_grad.astype(BF)
                val_grad = gated * gates[0, chan, :, wide].astype(F32)
                ready[1, chan, :, wide] = val_grad.astype(BF)
            for which, target in enumerate((d_inp, d_val, d_outp)):
                copy = pltpu.make_async_copy(
                    ready.at[which, :, :, pl.ds(start, WIDE)],
                    target.at[:, :, pl.ds(start, WIDE)],
                    sems.at[3 * (2 * block + part) + which],
                )
                copy.start()
                copies.append(copy)
    for copy in copies:
        copy.wait()
    patch_copy.wait()


def assemble_kernel(rank, own, other, out, first, ready, sem):
    me = rank[0]
    low = me < RANKS // 2
    shape = (SLOTS, SLOTS)
    wanted = jnp.where(low, 31, 32)
    pick = jnp.where(rows_of(shape) + lanes_of(shape) == wanted, 1.0, 0.0).astype(BF)
    top = rows_of((SLOTS, N)) == 0
    for part in range(2):
        sign = 1.0 if part == 0 else -1.0
        mine = own[part]
        shifted = pltpu.roll(mine, 1, 0)
        moved = jnp.dot(pick, other[32 * part : 32 * part + 32], preferred_element_type=F32)
        mirror = sign * reverse_lanes(moved)
        lines = jnp.where(low, mine, shifted)
        first[part] = lines[0:8]
        ready[part, 0:32, :] = lines
        ready[part, 32:64, :] = jnp.where(jnp.logical_and(top, ~low), shifted, mirror)
    copy = pltpu.make_async_copy(
        ready.at[:, pl.ds(8, ROWS - 8)], out.at[0, :, pl.ds(8, ROWS - 8)], sem
    )
    copy.start()
    copy.wait()


HBM = pl.BlockSpec(memory_space=pltpu.HBM)
VMEM = pl.BlockSpec(memory_space=pltpu.VMEM)
SMEM = pl.BlockSpec(memory_space=pltpu.SMEM)


def kept(value):
    return pltpu.with_memory_space_constraint(value, pltpu.HBM)


def sizes(flops, count=2**20):
    return pl.CostEstimate(flops=flops, bytes_accessed=count, transcendentals=0)


def params(mib):
    return pltpu.CompilerParams(vmem_limit_bytes=mib * 2**20)


def local(input_proj, value_proj, output_proj, grad_out, filter_spectrum):
    cos64, sin64 = dft_tables()
    half_tables = np.concatenate([cos64[: N // 2], sin64[: N // 2]]).reshape(4, WIDE, N)
    half_tables = jnp.asarray(half_tables.astype(ml_dtypes.bfloat16))
    half_sections = jnp.asarray(section_table()[:, : N // 2])
    turn_out = jnp.asarray(forward_turn())
    turn_back = jnp.asarray(inverse_turn())
    half_rows = jnp.asarray(np.stack(half_turn()).astype(np.float32))
    ctx_rank = lax.axis_index("ctx")
    rank = ctx_rank.astype(jnp.int32).reshape(1)
    half_ranks = RANKS // 2
    mirror_of = [(r, RANKS - 1 - r) for r in range(RANKS)]
    special_of = [(r, RANKS - r) for r in range(1, RANKS) if r != half_ranks]
    special_of += [(0, half_ranks), (half_ranks, 0)]

    filter_rows, filter_row, signals, sections, turns = pl.pallas_call(
        gather_kernel,
        out_shape=[
            pltpu.VMEM((2 * SLOTS, N), BF),
            pltpu.VMEM((2, N), BF),
            pltpu.VMEM((512, N // 2), BF),
            pltpu.VMEM((N, N // 2), BF),
            pltpu.VMEM((N // 2, 128), F32),
        ],
        in_specs=[SMEM] + [HBM] * 7,
        out_specs=[VMEM] * 5,
        scratch_shapes=[
            pltpu.VMEM((4, 2, ROWS, N), BF),
            pltpu.VMEM((2, SLOTS, N), F32),
            pltpu.VMEM((2, 8, N), F32),
            pltpu.SemaphoreType.DMA((8,)),
        ],
        compiler_params=params(16),
        cost_estimate=sizes(2**24),
        name="gather",
    )(
        rank,
        kept(input_proj),
        kept(value_proj),
        kept(output_proj),
        kept(grad_out),
        kept(half_sections),
        kept(turn_out),
        kept(filter_spectrum),
    )
    other_rows = lax.ppermute(filter_rows, "ctx", mirror_of)
    turned, filter_row = pl.pallas_call(
        section_kernel,
        out_shape=[pltpu.HBM((2, RANKS, ROWS, 128), BF), pltpu.VMEM((2, N), BF)],
        in_specs=[VMEM] * 4,
        out_specs=[HBM, VMEM],
        scratch_shapes=[
            pltpu.VMEM((2, RANKS, ROWS, 128), BF),
            pltpu.SemaphoreType.DMA((2 * BLOCKS,)),
        ],
        compiler_params=params(16),
        cost_estimate=sizes(A_COST),
        name="sections",
    )(signals, sections, turns, filter_row)
    other_row = lax.ppermute(filter_row, "ctx", special_of)
    arrived = lax.all_to_all(
        turned.reshape(2 * RANKS, ROWS, 128), ("core", "ctx"), 0, 0, tiled=True
    )

    tables = pl.pallas_call(
        table_kernel,
        out_shape=[pltpu.VMEM((WIDE, N), BF)] * 4,
        in_specs=[HBM] * 2,
        out_specs=[VMEM] * 4,
        scratch_shapes=[pltpu.SemaphoreType.DMA((4,))],
        compiler_params=params(16),
        cost_estimate=sizes(W_COST),
        name="bring_tables",
    )(other_rows, kept(half_tables))
    folded_filter = pl.pallas_call(
        filter_kernel,
        out_shape=pltpu.HBM((2, SLOTS, N), F32),
        in_specs=[SMEM, HBM, VMEM],
        out_specs=VMEM,
        scratch_shapes=[pltpu.VMEM((2, ROWS, N), F32), pltpu.SemaphoreType.DMA(())],
        compiler_params=params(16),
        cost_estimate=sizes(2**24),
        name="fold_filter",
    )(rank, kept(filter_spectrum), other_rows)

    spectra, grad_own, grad_low, grad_row, filter_near, turn_near = pl.pallas_call(
        spectrum_kernel,
        out_shape=[
            pltpu.VMEM((272, N), BF),
            pltpu.VMEM((2, SLOTS, N), F32),
            pltpu.VMEM((2 * SLOTS, N), BF),
            pltpu.VMEM((2, N), BF),
            pltpu.VMEM((2, SLOTS, N), F32),
            pltpu.VMEM((N, 128), F32),
        ],
        in_specs=[SMEM] + [VMEM] * 5 + [HBM, HBM, VMEM],
        out_specs=[VMEM] * 6,
        scratch_shapes=[
            pltpu.VMEM((544, N), BF),
            pltpu.SemaphoreType.DMA((2,)),
        ],
        compiler_params=params(20),
        cost_estimate=sizes(2**24),
        name="spectra",
    )(
        rank,
        arrived,
        *tables,
        kept(folded_filter),
        kept(turn_back),
        half_rows,
    )

    mirror_grad = lax.ppermute(grad_low, "ctx", mirror_of)
    mirror_row = lax.ppermute(grad_row, "ctx", special_of)

    unturned, grad_far = pl.pallas_call(
        inverse_kernel,
        out_shape=[
            pltpu.HBM((2, N, 128), BF),
            pltpu.HBM((2, SLOTS, N), F32),
        ],
        in_specs=[SMEM] + [VMEM] * 9,
        out_specs=[HBM, HBM],
        scratch_shapes=[
            pltpu.VMEM((N, 256), F32),
            pltpu.VMEM((2, N, 128), BF),
            pltpu.SemaphoreType.DMA((1 + BLOCKS,)),
        ],
        compiler_params=params(24),
        cost_estimate=sizes(B_COST),
        name="inverse",
    )(rank, spectra, filter_near, other_row, *tables, turn_near, grad_own)
    returned = lax.all_to_all(
        unturned.reshape(2 * RANKS, ROWS, 128), ("core", "ctx"), 0, 0, tiled=True
    )

    sections_near, gates_near = pl.pallas_call(
        near_kernel,
        out_shape=[pltpu.VMEM((N, N // 2), BF), pltpu.VMEM((3, 2, ROWS, N), BF)],
        in_specs=[HBM] * 5,
        out_specs=[VMEM] * 2,
        scratch_shapes=[pltpu.SemaphoreType.DMA((4,))],
        compiler_params=params(16),
        cost_estimate=sizes(W_COST),
        name="bring_near",
    )(mirror_grad, kept(half_sections), kept(input_proj), kept(value_proj), kept(grad_out))
    most_rows, first_rows = pl.pallas_call(
        assemble_kernel,
        out_shape=[
            pltpu.HBM((1, 2, ROWS, N), F32),
            pltpu.VMEM((2, 8, N), F32),
        ],
        in_specs=[SMEM] + [VMEM] * 2,
        out_specs=[HBM, VMEM],
        scratch_shapes=[pltpu.VMEM((2, ROWS, N), F32), pltpu.SemaphoreType.DMA(())],
        compiler_params=params(16),
        cost_estimate=sizes(2**24),
        name="assemble",
    )(rank, grad_far, mirror_grad)

    grad_input, grad_value, grad_output_proj, grad_filter = pl.pallas_call(
        result_kernel,
        out_shape=[pltpu.HBM((2, ROWS, N), BF)] * 3 + [pltpu.HBM((1, 2, ROWS, N), F32)],
        in_specs=[SMEM] + [VMEM] * 3 + [HBM, VMEM, VMEM],
        out_specs=[HBM] * 4,
        input_output_aliases={4: 3},
        scratch_shapes=[
            pltpu.VMEM((512, N), BF),
            pltpu.VMEM((3, 2, ROWS, N), BF),
            pltpu.VMEM((2, 8, N), F32),
            pltpu.SemaphoreType.DMA((3 * BLOCKS + 1,)),
        ],
        compiler_params=params(20),
        cost_estimate=sizes(2 * 256 * N * N),
        name="results",
    )(rank, returned, sections_near, gates_near, most_rows, first_rows, mirror_row)
    return (grad_input, grad_value, grad_output_proj, grad_filter)


def solution(mesh):
    split = Mesh(mesh.devices.reshape(-1, 2, RANKS), ("group", "core", "ctx"))
    data = P(("group", "core"), "ctx", None)
    filt = P(("group", "core"), None, "ctx", None)
    return jax.shard_map(
        local,
        mesh=split,
        in_specs=(data, data, data, data, filt),
        out_specs=(data, data, data, filt),
        check_vma=False,
    )
```

```python
import functools

import jax
import jax.numpy as jnp
import ml_dtypes
import numpy as np
from jax import lax
from jax.experimental import pallas as pl
from jax.experimental.pallas import tpu as pltpu
from jax.sharding import Mesh
from jax.sharding import PartitionSpec as P

N = 1024
TOTAL = N * N
RANKS = 16
ROWS = 64
SLOTS = 32
SCALE = 1.0 / TOTAL
BF = jnp.bfloat16
F32 = jnp.float32
NT = (((1,), (1,)), ((), ()))
BLOCKS = 4
WIDE = N // BLOCKS
BROAD = N
A_COST = 10**10
B_COST = 10**10
W_COST = 4 * 10**10


def kept_rows():
    rank = np.arange(RANKS)
    return (ROWS * rank + (rank >= RANKS // 2))[:, None] + np.arange(SLOTS)[None, :]


def dft_tables():
    index = np.arange(N, dtype=np.int64)
    phase = (index[:, None] * index[None, :] % N).astype(np.float64) * (2.0 * np.pi / N)
    return np.cos(phase), np.sin(phase)


def section_table():
    cos, sin = dft_tables()
    rows = kept_rows()
    imag = -sin[rows]
    imag[0, 0] = 1.0 - 2.0 * (np.arange(N) % 2)
    both = np.stack([cos[rows], imag])
    both = both.reshape(2, RANKS // 2, 2, SLOTS, N).transpose(1, 0, 2, 3, 4)
    return both.reshape(N, N).astype(ml_dtypes.bfloat16)


def forward_turn():
    rows = kept_rows().reshape(1, -1, 1)
    place = np.arange(N).reshape(RANKS, 1, ROWS)
    phase = (rows * place % TOTAL).astype(np.float64) * (2.0 * np.pi / TOTAL)
    return np.concatenate([np.cos(phase), np.sin(phase)], axis=2).astype(np.float32)


def inverse_turn():
    rows = kept_rows().reshape(RANKS, 1, SLOTS)
    place = np.arange(N).reshape(1, N, 1)
    phase = (rows * place % TOTAL).astype(np.float64) * (2.0 * np.pi / TOTAL)
    cos, sin = np.cos(phase), np.sin(phase)
    sin[0, :, 0] = packed_turn()
    return np.concatenate([cos, cos, sin, sin], axis=2).astype(np.float32)


def half_turn():
    phase = np.arange(N) * (np.pi / N)
    return np.cos(phase), np.sin(phase)


def packed_turn():
    cos, sin = half_turn()
    middle = np.abs(np.arange(N) - N // 2 + 0.5) < N // 4
    return np.where(middle, -1.0 / np.where(middle, sin, 1.0), 1.0 / np.where(middle, 1.0, cos))


def lanes_of(shape):
    return lax.broadcasted_iota(jnp.int32, shape, len(shape) - 1)


def rows_of(shape):
    return lax.broadcasted_iota(jnp.int32, shape, len(shape) - 2)


def swap_halves(value):
    half = value.shape[-1] // 2
    return jnp.concatenate([value[..., half:], value[..., :half]], axis=-1)


def split_turn(packed):
    swapped = swap_halves(packed)
    low = lanes_of(packed.shape) < packed.shape[-1] // 2
    return jnp.where(low, packed, swapped), jnp.where(low, swapped, packed)


def start_all(copies):
    for copy in copies:
        copy.start()


def gather_kernel(
    rank, inp, val, outp, grad, table, turn, filt,
    rows, row, signals, sections, turns, gates, lines, first, sems
):
    line_copy = pltpu.make_async_copy(filt.at[0, :, pl.ds(SLOTS, SLOTS)], lines, sems.at[0])
    row_copy = pltpu.make_async_copy(filt.at[0, :, pl.ds(0, 8)], first, sems.at[1])
    gate_copies = [
        pltpu.make_async_copy(source, gates.at[which], sems.at[2 + which])
        for which, source in enumerate((inp, val, outp, grad))
    ]
    table_copy = pltpu.make_async_copy(table, sections, sems.at[6])
    turn_copy = pltpu.make_async_copy(turn.at[rank[0]], turns, sems.at[7])
    start_all([line_copy] + gate_copies + [table_copy, turn_copy, row_copy])
    middle = N // 2
    line_copy.wait()
    for part in range(2):
        rows[SLOTS * part : SLOTS * part + SLOTS, :] = lines[part].astype(BF)
    for copy in gate_copies:
        copy.wait()
    for chan in range(2):
        gated = gates[0, chan].astype(F32) * gates[1, chan].astype(F32)
        conv = gates[3, chan].astype(F32) * gates[2, chan].astype(F32)
        for part in range(2):
            base = 256 * part + 128 * chan
            lanes = slice(middle * part, middle * part + middle)
            signals[base : base + 64, :] = gated[:, lanes].astype(BF)
            signals[base + 64 : base + 128, :] = conv[:, lanes].astype(BF)
    row_copy.wait()
    row[...] = jnp.concatenate([first[0, 0:1], first[1, 0:1]], axis=0).astype(BF)
    table_copy.wait()
    turn_copy.wait()


def section_kernel(signals, sections, turns, row, out, row_out, ready, sems):
    row_out[...] = row[...]
    out_copies = []
    for block in range(BLOCKS):
        rows = slice(WIDE * block, WIDE * block + WIDE)
        halves = lax.dot_general(
            sections[rows, :], signals[...], NT, preferred_element_type=F32
        )
        odd_rows = (rows_of((WIDE, 1)) + (block >= BLOCKS // 2)) % 2
        section = halves[:, :256] + (1 - 2 * odd_rows).astype(F32) * halves[:, 256:]
        for pair in range(2):
            base = WIDE // 2 * block + 64 * pair
            cos, sin = split_turn(turns[base : base + 64, :])
            for chan in range(2):
                lanes = slice(128 * chan, 128 * chan + 128)
                real = section[128 * pair : 128 * pair + 64, lanes]
                imag = section[128 * pair + 64 : 128 * pair + 128, lanes]
                turned_re = (real * cos + imag * sin).astype(BF)
                turned_im = (imag * cos - real * sin).astype(BF)
                for odd in range(2):
                    some = slice(32 * odd, 32 * odd + 32)
                    peer = 4 * block + 2 * pair + odd
                    ready[chan, peer, 0:32, :] = turned_re[some]
                    ready[chan, peer, 32:64, :] = turned_im[some]
        peers = pl.ds(4 * block, 4)
        for chan in range(2):
            copy = pltpu.make_async_copy(
                ready.at[chan, peers], out.at[chan, peers], sems.at[2 * block + chan]
            )
            copy.start()
            out_copies.append(copy)
    for copy in out_copies:
        copy.wait()


def reverse_lanes(value):
    shape = (128, 128)
    flip = jnp.where(rows_of(shape) + lanes_of(shape) == 127, 1.0, 0.0).astype(BF)
    value = value.astype(BF)
    parts = [
        jnp.dot(value[:, 128 * part : 128 * part + 128], flip, preferred_element_type=F32)
        for part in reversed(range(N // 128))
    ]
    return jnp.concatenate(parts, axis=1)


def table_kernel(after, *refs):
    copies = [
        pltpu.make_async_copy(refs[0].at[which], refs[1 + which], refs[-1].at[which])
        for which in range(4)
    ]
    start_all(copies)
    for copy in copies:
        copy.wait()


def near_kernel(after, table, first, second, third, table_out, stack, sems):
    copies = [pltpu.make_async_copy(table, table_out, sems.at[0])] + [
        pltpu.make_async_copy(source, stack.at[which], sems.at[1 + which])
        for which, source in enumerate((first, second, third))
    ]
    start_all(copies)
    for copy in copies:
        copy.wait()


def filter_kernel(rank, own, other, out, mine, sem):
    me = rank[0]
    copy = pltpu.make_async_copy(own.at[0], mine, sem)
    copy.start()
    low = me < RANKS // 2
    shape = (SLOTS, SLOTS)
    wanted = jnp.where(low, 32, 31)
    pick = jnp.where(rows_of(shape) + lanes_of(shape) == wanted, 1.0, 0.0).astype(BF)
    top = rows_of((SLOTS, N)) == 0
    copy.wait()
    for part in range(2):
        sign = 1.0 if part == 0 else -1.0
        kept = jnp.where(low, mine[part, 0:32, :], mine[part, 1:33, :])
        moved = jnp.dot(pick, other[32 * part : 32 * part + 32], preferred_element_type=F32)
        mirror = reverse_lanes(moved)
        first = mine[part, 0:8, :]
        flipped = reverse_lanes(jnp.concatenate([first, first], axis=0))
        head = jnp.where(me == 0, pltpu.roll(flipped[0:8], 1, 1)[0:1], 0.0)
        mirror = jnp.where(jnp.logical_and(top, low), head, mirror)
        out[part] = 0.5 * (kept + sign * mirror)


def special_rows(special):
    rows = [jnp.broadcast_to(special[part : part + 1, :], (8, N)) for part in range(2)]
    both = jnp.concatenate(rows, axis=0)
    return both.astype(F32), reverse_lanes(both)


def alternating(shape):
    return 1 - 2 * (lanes_of(shape) % 2)


def spectrum_kernel(
    rank, turned, cos_0, cos_1, sin_0, sin_1, filt_far, turn_far, half,
    spec, grad, grad_low, grad_row, filt, turn, left, sems
):
    me = rank[0]
    middle = N // 2
    copies = [
        pltpu.make_async_copy(filt_far, filt, sems.at[0]),
        pltpu.make_async_copy(turn_far.at[me], turn, sems.at[1]),
    ]
    start_all(copies)
    for seq in range(2):
        for pair in range(RANKS // 2):
            even = turned[RANKS * seq + 2 * pair]
            odd = turned[RANKS * seq + 2 * pair + 1]
            here = slice(128 * (pair % 4), 128 * (pair % 4) + 128)
            there = slice(middle + 128 * (pair % 4), middle + 128 * (pair % 4) + 128)
            for sig in range(2):
                lanes = slice(64 * sig, 64 * sig + 64)
                both = jnp.concatenate([even[:, lanes], odd[:, lanes]], axis=1)
                base = 272 * (pair // 4) + 32 * (2 * seq + sig)
                left[base : base + 32, here] = both[0:32]
                left[base : base + 32, there] = both[32:64]
                left[128 + base : 160 + base, here] = both[32:64]
                left[128 + base : 160 + base, there] = -both[0:32]
    packed = jnp.logical_and(rows_of((16, middle)) == 0, me == 0)
    for part in range(2):
        heads = []
        for which in range(4):
            base = 272 * part + 32 * which
            block = left[base : base + 16, middle:].astype(F32)
            heads.append(block[0:1])
            cleared = jnp.where(packed, 0.0, block).astype(BF)
            left[base : base + 16, middle:] = cleared
            left[128 + base : 144 + base, :middle] = cleared
        head = jnp.concatenate(heads + heads, axis=0)
        places = slice(middle * part, middle * part + middle)
        real = head * half[0:1, places]
        imag = -head * half[1:2, places]
        lines = slice(272 * part + 256, 272 * part + 272)
        left[lines, :middle] = jnp.concatenate([real, imag], axis=0).astype(BF)
        left[lines, middle:] = jnp.concatenate([imag, -real], axis=0).astype(BF)

    sign = alternating((1, BROAD)).astype(F32)
    for block in range(N // BROAD):
        wide = slice(BROAD * block, BROAD * block + BROAD)
        pieces = [table[:, wide] for table in (cos_0, cos_1, sin_0, sin_1)]
        halves = jnp.dot(
            left[...], jnp.concatenate(pieces, axis=0), preferred_element_type=F32
        )
        result = halves[:272] + sign * halves[272:]
        spec[:, wide] = result.astype(BF)
        real = 0.0
        imag = 0.0
        row_re = 0.0
        row_im = 0.0
        for seq in range(2):
            base = 64 * seq
            u_re, u_im = result[base : base + 32], result[base + 128 : base + 160]
            d_re, d_im = result[base + 32 : base + 64], result[base + 160 : base + 192]
            real = real + (u_re * d_re + u_im * d_im)
            imag = imag + (u_re * d_im - u_im * d_re)
            base = 256 + 2 * seq
            u_re, u_im = result[base : base + 1], result[base + 8 : base + 9]
            d_re, d_im = result[base + 1 : base + 2], result[base + 9 : base + 10]
            row_re = row_re + (u_re * d_re + u_im * d_im)
            row_im = row_im + (u_re * d_im - u_im * d_re)
        real = real * SCALE
        imag = imag * SCALE
        grad[0, :, wide] = real
        grad[1, :, wide] = imag
        grad_low[0:32, wide] = real.astype(BF)
        grad_low[32:64, wide] = imag.astype(BF)
        row_re = jnp.where(me == 0, row_re * SCALE, real[0:1])
        row_im = jnp.where(me == 0, row_im * SCALE, imag[0:1])
        grad_row[:, wide] = jnp.concatenate([row_re, row_im], axis=0).astype(BF)
    for copy in copies:
        copy.wait()


def products(u_re, u_im, d_re, d_im, h_re, h_im):
    return (
        u_re * h_re - u_im * h_im,
        u_re * h_im + u_im * h_re,
        h_re * d_re + h_im * d_im,
        h_re * d_im - h_im * d_re,
    )


def inverse_kernel(
    rank, spec, filt, special, cos_0, cos_1, sin_0, sin_1, turn, grad,
    out, grad_far, total, ready, sems
):
    me = rank[0]
    copy = pltpu.make_async_copy(grad, grad_far, sems.at[0])
    copy.start()
    out_copies = []
    outer, inner = (0, 3), (1, 2)
    sign = alternating((1, BROAD)).astype(BF)
    top = rows_of((SLOTS, BROAD)) == 0
    packed_row = jnp.logical_and(top, me == 0)
    lone, flipped = special_rows(special)
    lone_re, lone_im = 0.5 * lone[0:1], 0.5 * lone[8:9]
    flip_re, flip_im = 0.5 * flipped[0:1], -0.5 * flipped[8:9]
    patched_row = jnp.logical_and(top, jnp.logical_and(me > 0, me < RANKS // 2))
    for block in range(N // BROAD):
        wide = slice(BROAD * block, BROAD * block + BROAD)
        values = spec[:, wide].astype(F32)
        h_re = filt[0, :, wide] + jnp.where(patched_row, flip_re[:, wide], 0.0)
        h_im = filt[1, :, wide] + jnp.where(patched_row, flip_im[:, wide], 0.0)
        x_re, x_im = (lone_re + flip_re)[:, wide], (lone_im + flip_im)[:, wide]
        reals, imags, extra_re, extra_im = [], [], [], []
        for seq in range(2):
            base = 64 * seq
            p_re, p_im, q_re, q_im = products(
                values[base : base + 32],
                values[base + 128 : base + 160],
                values[base + 32 : base + 64],
                values[base + 160 : base + 192],
                h_re,
                h_im,
            )
            reals += [p_re, q_re]
            imags += [p_im, q_im]
            base = 256 + 2 * seq
            p_re, p_im, q_re, q_im = products(
                values[base : base + 1],
                values[base + 8 : base + 9],
                values[base + 1 : base + 2],
                values[base + 9 : base + 10],
                x_re,
                x_im,
            )
            extra_re += [p_re, q_re]
            extra_im += [p_im, q_im]

        def mixed(plain, extra, sign):
            return [jnp.where(packed_row, sign * e, p) for p, e in zip(plain, extra)]

        def joined(first, second):
            return jnp.concatenate(first + second, axis=0).astype(BF)

        less = [-value for value in imags]
        for parts, extra, crossed in (
            (outer, extra_re, mixed(reals, extra_im, -1.0)),
            (inner, extra_im, mixed(reals, extra_re, 1.0)),
        ):
            straight = joined(reals, mixed(imags, extra, 1.0))
            crossing = joined(less, crossed)
            for quarter in parts:
                rows = slice(WIDE * quarter, WIDE * quarter + WIDE)
                cos = (cos_0, cos_1)[quarter % 2][:, wide]
                sin = (sin_0, sin_1)[quarter % 2][:, wide]
                if quarter >= 2:
                    cos, sin = cos * sign, sin * sign
                part = lax.dot_general(
                    cos, straight, NT, preferred_element_type=F32
                ) + lax.dot_general(sin, crossing, NT, preferred_element_type=F32)
                if block == 0:
                    total[rows, :] = part
                else:
                    total[rows, :] += part

    for piece in range(BLOCKS):
        rows = slice(WIDE * piece, WIDE * piece + WIDE)
        turn_cos, turn_sin = split_turn(turn[rows, :])
        real = total[rows, :128]
        imag = total[rows, 128:]
        un_re = real * turn_cos - imag * turn_sin
        un_im = real * turn_sin + imag * turn_cos
        packed = jnp.logical_and(lanes_of((WIDE, 128)) % SLOTS == 0, me == 0)
        un_im = jnp.where(packed, imag * turn_sin, 2.0 * un_im).astype(BF)
        un_re = jnp.where(packed, real, 2.0 * un_re).astype(BF)
        ready[0, rows, :] = jnp.concatenate([un_re[:, :64], un_im[:, :64]], axis=1)
        ready[1, rows, :] = jnp.concatenate([un_re[:, 64:], un_im[:, 64:]], axis=1)
        place = pl.ds(WIDE * piece, WIDE)
        out_copies.append(
            pltpu.make_async_copy(ready.at[:, place], out.at[:, place], sems.at[1 + piece])
        )
        out_copies[-1].start()
    for out_copy in out_copies:
        out_copy.wait()
    copy.wait()


def result_kernel(
    rank, arrived, table, gates, most, first, special,
    d_inp, d_val, d_outp, d_filt, left, ready, patch, sems
):
    me = rank[0]
    lone, flipped = special_rows(special)
    top = jnp.logical_and(rows_of((8, N)) == 0, me >= RANKS // 2)
    for part in range(2):
        lines = slice(8 * part, 8 * part + 8)
        sign = 1.0 if part == 0 else -1.0
        head = jnp.where(me == RANKS // 2, lone[lines], sign * flipped[lines])
        patch[part] = jnp.where(top, head, first[part])
    patch_copy = pltpu.make_async_copy(
        patch, d_filt.at[0, :, pl.ds(0, 8)], sems.at[3 * BLOCKS]
    )
    patch_copy.start()
    half = N // 2
    for chan in range(2):
        for pair in range(RANKS // 2):
            even = arrived[RANKS * chan + 2 * pair]
            odd = arrived[RANKS * chan + 2 * pair + 1]
            sign = alternating((1, 128)) * (1 if pair < RANKS // 4 else -1)
            for sig in range(2):
                low = slice(32 * sig, 32 * sig + 32)
                high = slice(64 + 32 * sig, 96 + 32 * sig)
                base = 64 * (2 * chan + sig)
                lanes = slice(128 * pair, 128 * pair + 128)
                block = jnp.concatenate(
                    [even[:, low], odd[:, low], even[:, high], odd[:, high]], axis=1
                )
                left[base : base + 64, lanes] = block
                left[256 + base : 320 + base, lanes] = block * sign.astype(BF)
    copies = []
    for block in range(BLOCKS // 2):
        near = slice(WIDE * block, WIDE * block + WIDE)
        halves = jnp.dot(left[...], table[:, near], preferred_element_type=F32) * SCALE
        for part in range(2):
            start = half * part + WIDE * block
            wide = slice(start, start + WIDE)
            result = halves[256 * part : 256 * part + 256]
            for chan in range(2):
                conv = result[128 * chan : 128 * chan + 64]
                gated = result[128 * chan + 64 : 128 * chan + 128]
                out_grad = gates[2, chan, :, wide].astype(F32) * conv
                ready[2, chan, :, wide] = out_grad.astype(BF)
                in_grad = gated * gates[1, chan, :, wide].astype(F32)
                ready[0, chan, :, wide] = in_grad.astype(BF)
                val_grad = gated * gates[0, chan, :, wide].astype(F32)
                ready[1, chan, :, wide] = val_grad.astype(BF)
            for which, target in enumerate((d_inp, d_val, d_outp)):
                copy = pltpu.make_async_copy(
                    ready.at[which, :, :, pl.ds(start, WIDE)],
                    target.at[:, :, pl.ds(start, WIDE)],
                    sems.at[3 * (2 * block + part) + which],
                )
                copy.start()
                copies.append(copy)
    for copy in copies:
        copy.wait()
    patch_copy.wait()


def assemble_kernel(rank, own, other, out, first, ready, sem):
    me = rank[0]
    low = me < RANKS // 2
    shape = (SLOTS, SLOTS)
    wanted = jnp.where(low, 31, 32)
    pick = jnp.where(rows_of(shape) + lanes_of(shape) == wanted, 1.0, 0.0).astype(BF)
    top = rows_of((SLOTS, N)) == 0
    for part in range(2):
        sign = 1.0 if part == 0 else -1.0
        mine = own[part]
        shifted = pltpu.roll(mine, 1, 0)
        moved = jnp.dot(pick, other[32 * part : 32 * part + 32], preferred_element_type=F32)
        mirror = sign * reverse_lanes(moved)
        lines = jnp.where(low, mine, shifted)
        first[part] = lines[0:8]
        ready[part, 0:32, :] = lines
        ready[part, 32:64, :] = jnp.where(jnp.logical_and(top, ~low), shifted, mirror)
    copy = pltpu.make_async_copy(
        ready.at[:, pl.ds(8, ROWS - 8)], out.at[0, :, pl.ds(8, ROWS - 8)], sem
    )
    copy.start()
    copy.wait()


HBM = pl.BlockSpec(memory_space=pltpu.HBM)
VMEM = pl.BlockSpec(memory_space=pltpu.VMEM)
SMEM = pl.BlockSpec(memory_space=pltpu.SMEM)


def kept(value):
    return pltpu.with_memory_space_constraint(value, pltpu.HBM)


def sizes(flops, count=2**20):
    return pl.CostEstimate(flops=flops, bytes_accessed=count, transcendentals=0)


def params(mib):
    return pltpu.CompilerParams(vmem_limit_bytes=mib * 2**20)


def local(input_proj, value_proj, output_proj, grad_out, filter_spectrum):
    cos64, sin64 = dft_tables()
    half_tables = np.concatenate([cos64[: N // 2], sin64[: N // 2]]).reshape(4, WIDE, N)
    half_tables = jnp.asarray(half_tables.astype(ml_dtypes.bfloat16))
    half_sections = jnp.asarray(section_table()[:, : N // 2])
    turn_out = jnp.asarray(forward_turn())
    turn_back = jnp.asarray(inverse_turn())
    half_rows = jnp.asarray(np.stack(half_turn()).astype(np.float32))
    ctx_rank = lax.axis_index("ctx")
    rank = ctx_rank.astype(jnp.int32).reshape(1)
    half_ranks = RANKS // 2
    mirror_of = [(r, RANKS - 1 - r) for r in range(RANKS)]
    special_of = [(r, RANKS - r) for r in range(1, RANKS) if r != half_ranks]
    special_of += [(0, half_ranks), (half_ranks, 0)]

    filter_rows, filter_row, signals, sections, turns = pl.pallas_call(
        gather_kernel,
        out_shape=[
            pltpu.VMEM((2 * SLOTS, N), BF),
            pltpu.VMEM((2, N), BF),
            pltpu.VMEM((512, N // 2), BF),
            pltpu.VMEM((N, N // 2), BF),
            pltpu.VMEM((N // 2, 128), F32),
        ],
        in_specs=[SMEM] + [HBM] * 7,
        out_specs=[VMEM] * 5,
        scratch_shapes=[
            pltpu.VMEM((4, 2, ROWS, N), BF),
            pltpu.VMEM((2, SLOTS, N), F32),
            pltpu.VMEM((2, 8, N), F32),
            pltpu.SemaphoreType.DMA((8,)),
        ],
        compiler_params=params(16),
        cost_estimate=sizes(2**24),
        name="gather",
    )(
        rank,
        kept(input_proj),
        kept(value_proj),
        kept(output_proj),
        kept(grad_out),
        kept(half_sections),
        kept(turn_out),
        kept(filter_spectrum),
    )
    other_rows = lax.ppermute(filter_rows, "ctx", mirror_of)
    turned, filter_row = pl.pallas_call(
        section_kernel,
        out_shape=[pltpu.HBM((2, RANKS, ROWS, 128), BF), pltpu.VMEM((2, N), BF)],
        in_specs=[VMEM] * 4,
        out_specs=[HBM, VMEM],
        scratch_shapes=[
            pltpu.VMEM((2, RANKS, ROWS, 128), BF),
            pltpu.SemaphoreType.DMA((2 * BLOCKS,)),
        ],
        compiler_params=params(16),
        cost_estimate=sizes(A_COST),
        name="sections",
    )(signals, sections, turns, filter_row)
    other_row = lax.ppermute(filter_row, "ctx", special_of)
    arrived = lax.all_to_all(
        turned.reshape(2 * RANKS, ROWS, 128), ("core", "ctx"), 0, 0, tiled=True
    )

    tables = pl.pallas_call(
        table_kernel,
        out_shape=[pltpu.VMEM((WIDE, N), BF)] * 4,
        in_specs=[HBM] * 2,
        out_specs=[VMEM] * 4,
        scratch_shapes=[pltpu.SemaphoreType.DMA((4,))],
        compiler_params=params(16),
        cost_estimate=sizes(W_COST),
        name="bring_tables",
    )(other_rows, kept(half_tables))
    folded_filter = pl.pallas_call(
        filter_kernel,
        out_shape=pltpu.HBM((2, SLOTS, N), F32),
        in_specs=[SMEM, HBM, VMEM],
        out_specs=VMEM,
        scratch_shapes=[pltpu.VMEM((2, ROWS, N), F32), pltpu.SemaphoreType.DMA(())],
        compiler_params=params(16),
        cost_estimate=sizes(2**24),
        name="fold_filter",
    )(rank, kept(filter_spectrum), other_rows)

    spectra, grad_own, grad_low, grad_row, filter_near, turn_near = pl.pallas_call(
        spectrum_kernel,
        out_shape=[
            pltpu.VMEM((272, N), BF),
            pltpu.VMEM((2, SLOTS, N), F32),
            pltpu.VMEM((2 * SLOTS, N), BF),
            pltpu.VMEM((2, N), BF),
            pltpu.VMEM((2, SLOTS, N), F32),
            pltpu.VMEM((N, 128), F32),
        ],
        in_specs=[SMEM] + [VMEM] * 5 + [HBM, HBM, VMEM],
        out_specs=[VMEM] * 6,
        scratch_shapes=[
            pltpu.VMEM((544, N), BF),
            pltpu.SemaphoreType.DMA((2,)),
        ],
        compiler_params=params(20),
        cost_estimate=sizes(2**24),
        name="spectra",
    )(
        rank,
        arrived,
        *tables,
        kept(folded_filter),
        kept(turn_back),
        half_rows,
    )

    mirror_grad = lax.ppermute(grad_low, "ctx", mirror_of)
    mirror_row = lax.ppermute(grad_row, "ctx", special_of)

    unturned, grad_far = pl.pallas_call(
        inverse_kernel,
        out_shape=[
            pltpu.HBM((2, N, 128), BF),
            pltpu.HBM((2, SLOTS, N), F32),
        ],
        in_specs=[SMEM] + [VMEM] * 9,
        out_specs=[HBM, HBM],
        scratch_shapes=[
            pltpu.VMEM((N, 256), F32),
            pltpu.VMEM((2, N, 128), BF),
            pltpu.SemaphoreType.DMA((1 + BLOCKS,)),
        ],
        compiler_params=params(24),
        cost_estimate=sizes(B_COST),
        name="inverse",
    )(rank, spectra, filter_near, other_row, *tables, turn_near, grad_own)
    returned = lax.all_to_all(
        unturned.reshape(2 * RANKS, ROWS, 128), ("core", "ctx"), 0, 0, tiled=True
    )

    sections_near, gates_near = pl.pallas_call(
        near_kernel,
        out_shape=[pltpu.VMEM((N, N // 2), BF), pltpu.VMEM((3, 2, ROWS, N), BF)],
        in_specs=[HBM] * 5,
        out_specs=[VMEM] * 2,
        scratch_shapes=[pltpu.SemaphoreType.DMA((4,))],
        compiler_params=params(16),
        cost_estimate=sizes(W_COST),
        name="bring_near",
    )(mirror_grad, kept(half_sections), kept(input_proj), kept(value_proj), kept(grad_out))
    most_rows, first_rows = pl.pallas_call(
        assemble_kernel,
        out_shape=[
            pltpu.HBM((1, 2, ROWS, N), F32),
            pltpu.VMEM((2, 8, N), F32),
        ],
        in_specs=[SMEM] + [VMEM] * 2,
        out_specs=[HBM, VMEM],
        scratch_shapes=[pltpu.VMEM((2, ROWS, N), F32), pltpu.SemaphoreType.DMA(())],
        compiler_params=params(16),
        cost_estimate=sizes(2**24),
        name="assemble",
    )(rank, grad_far, mirror_grad)

    grad_input, grad_value, grad_output_proj, grad_filter = pl.pallas_call(
        result_kernel,
        out_shape=[pltpu.HBM((2, ROWS, N), BF)] * 3 + [pltpu.HBM((1, 2, ROWS, N), F32)],
        in_specs=[SMEM] + [VMEM] * 3 + [HBM, VMEM, VMEM],
        out_specs=[HBM] * 4,
        input_output_aliases={4: 3},
        scratch_shapes=[
            pltpu.VMEM((512, N), BF),
            pltpu.VMEM((3, 2, ROWS, N), BF),
            pltpu.VMEM((2, 8, N), F32),
            pltpu.SemaphoreType.DMA((3 * BLOCKS + 1,)),
        ],
        compiler_params=params(20),
        cost_estimate=sizes(2 * 256 * N * N),
        name="results",
    )(rank, returned, sections_near, gates_near, most_rows, first_rows, mirror_row)
    return (grad_input, grad_value, grad_output_proj, grad_filter)


def solution(mesh):
    split = Mesh(mesh.devices.reshape(-1, 2, RANKS), ("group", "core", "ctx"))
    data = P(("group", "core"), "ctx", None)
    filt = P(("group", "core"), None, "ctx", None)
    return jax.shard_map(
        local,
        mesh=split,
        in_specs=(data, data, data, data, filt),
        out_specs=(data, data, data, filt),
        check_vma=False,
    )
```
